32 devices in a mesh: dp: 8 (over z, x), seq: 4 (over y, core).
Axes of the slice: x: 2, y: 2, z: 4, core: 2. Of those that a mesh axis runs over, the one named last changes fastest.
Arguments:
- inputs: bfloat16 [32, 512, 768], P('dp', 'seq'), may hold values from -6 to 6
- cotangent: bfloat16 [32, 512, 768], P('dp', 'seq'), may hold values from -6 to 6
- masked: int32 [32, 512], P('dp', 'seq'), may hold values from 0 to 1, as said below
- w_query: bfloat16 [768, 768], replicated, may hold values from -0.21875 to 0.21875
- b_query: bfloat16 [768], replicated, may hold values from -3 to 3
- w_key: bfloat16 [768, 768], replicated, may hold values from -0.21875 to 0.21875
- w_value: bfloat16 [768, 768], replicated, may hold values from -0.21875 to 0.21875
- b_value: bfloat16 [768], replicated, may hold values from -3 to 3
- w_output: bfloat16 [768, 768], replicated, may hold values from -0.625 to 0.625
- b_output: bfloat16 [768], replicated, may hold values from -3 to 3
- attn_gain: bfloat16 [768], replicated, may hold values from 0.5 to 1.5
- attn_shift: bfloat16 [768], replicated, may hold values from -3 to 3
- w_inner: bfloat16 [768, 3072], replicated, may hold values from -0.21875 to 0.21875
- b_inner: bfloat16 [3072], replicated, may hold values from -3 to 3
- w_outer: bfloat16 [3072, 768], replicated, may hold values from -0.109375 to 0.109375
- b_outer: bfloat16 [768], replicated, may hold values from -3 to 3
- ffn_gain: bfloat16 [768], replicated, may hold values from 0.5 to 1.5
- ffn_shift: bfloat16 [768], replicated, may hold values from -3 to 3
Outputs:
- outputs: bfloat16 [32, 512, 768], P('dp', 'seq')
- grad_inputs: bfloat16 [32, 512, 768], P('dp', 'seq')
- grad_w_query: float32 [768, 768], P('dp')
- grad_b_query: float32 [768], P('dp')
- grad_w_key: float32 [768, 768], P('dp')
- grad_w_value: float32 [768, 768], P('dp')
- grad_b_value: float32 [768], P('dp')
- grad_w_output: float32 [768, 768], P('dp')
- grad_b_output: float32 [768], P('dp')
- grad_attn_gain: float32 [768], P('dp')
- grad_attn_shift: float32 [768], P('dp')
- grad_w_inner: float32 [768, 3072], P('dp')
- grad_b_inner: float32 [3072], P('dp')
- grad_w_outer: float32 [3072, 768], P('dp')
- grad_b_outer: float32 [768], P('dp')
- grad_ffn_gain: float32 [768], P('dp')
- grad_ffn_shift: float32 [768], P('dp')
The draws below stay inside these ranges and needn't reach their ends.
Inputs may be any that keep to these rules, and one draw needn't show every extreme that they name: The share of masked positions may differ from one block of 128 positions of a sentence to the next.
All inputs are finite; a program needn't handle non-finite values.
Results may differ from the reference program's by a relative error of at most 0.019.
Values may be sent and summed in bfloat16 or wider, within the bound.
No kernel may reach another device: no remote copies, remote signals or barrier semaphores. Data moves between devices by JAX's collectives and lax.ppermute only.
A program may use at most 128 MiB of HBM per device.

```python
import math
import jax
import jax.numpy as jnp
from jax import lax

D = 768
HD = 64
FF = 3072
BLK = 128
SENTS = 32
LEN = 512


def draw_masked(key, part):
    key = jax.random.fold_in(key, 7)
    rate_key, roll_key = jax.random.split(key)
    rates = jax.random.randint(rate_key, (SENTS, LEN // BLK, 1), 2, 13)
    rolls = jax.random.randint(roll_key, (SENTS, LEN // BLK, BLK), 0, 40)
    return (rolls < rates).astype(jnp.int32).reshape(SENTS, LEN)


def shard_levels(stream_key, shape, pieces, low, largest):
    def one(position, shards_of):
        draws = jax.random.uniform(jax.random.fold_in(jax.random.fold_in(stream_key, 6), position), (shards_of,), jnp.float32, low / len(pieces), largest / len(pieces))
        return jnp.repeat(jnp.exp(draws), shape[position] // shards_of).reshape((-1,) + (1,) * (len(shape) - position - 1))

    loudness = one(*pieces[0])
    for cut in pieces[1:]:
        loudness = loudness * one(*cut)
    return loudness


def normal_values(own_key, extent, spread, most, cuts=(), kind=jnp.bfloat16):
    level = shard_levels(own_key, extent, cuts, -0.22, 0.18) if cuts else 1.0
    values = jax.random.normal(own_key, extent, jnp.float32) * spread * level
    return jnp.minimum(jnp.maximum(values, -most), most).astype(kind)


def setup_inputs(seed: int = 0) -> dict:
    splits = jax.random.split(jax.random.key(seed), 19)
    inputs = normal_values(splits[0], (SENTS, LEN, D), 1.0, 6.0, ((0, 8), (1, 4)))
    cotangent = normal_values(splits[1], (SENTS, LEN, D), 1.0, 6.0, ((0, 8), (1, 4)))
    masked = draw_masked(jax.random.fold_in(splits[18], 71), 0)
    w_query = normal_values(splits[3], (D, D), D ** -0.5, 0.21875)
    b_query = normal_values(splits[4], (D,), 0.5, 3.0)
    w_key = normal_values(splits[5], (D, D), D ** -0.5, 0.21875)
    w_value = normal_values(splits[6], (D, D), D ** -0.5, 0.21875)
    b_value = normal_values(splits[7], (D,), 0.5, 3.0)
    w_output = normal_values(splits[8], (D, D), (D // 8) ** -0.5, 0.625)
    b_output = normal_values(splits[9], (D,), 0.5, 3.0)
    attn_gain = jnp.clip(1.0 + 0.1 * jax.random.normal(splits[10], (D,), jnp.float32), 0.5, 1.5).astype(jnp.bfloat16)
    attn_shift = normal_values(splits[11], (D,), 0.5, 3.0)
    w_inner = normal_values(splits[12], (D, FF), D ** -0.5, 0.21875)
    b_inner = normal_values(splits[13], (FF,), 0.5, 3.0)
    w_outer = normal_values(splits[14], (FF, D), FF ** -0.5, 0.109375)
    b_outer = normal_values(splits[15], (D,), 0.5, 3.0)
    ffn_gain = jnp.clip(1.0 + 0.1 * jax.random.normal(splits[16], (D,), jnp.float32), 0.5, 1.5).astype(jnp.bfloat16)
    ffn_shift = normal_values(splits[17], (D,), 0.5, 3.0)
    return dict(inputs=inputs, cotangent=cotangent, masked=masked, w_query=w_query, b_query=b_query, w_key=w_key, w_value=w_value, b_value=b_value, w_output=w_output, b_output=b_output, attn_gain=attn_gain, attn_shift=attn_shift, w_inner=w_inner, b_inner=b_inner, w_outer=w_outer, b_outer=b_outer, ffn_gain=ffn_gain, ffn_shift=ffn_shift)


@jax.custom_vjp
def low(v):
    return lax.optimization_barrier(v.astype(jnp.bfloat16)).astype(jnp.float32)

@jax.custom_vjp
def low_back(v):
    return v

def low_keep(v):
    return (low(v), None)

def low_pass(kept, grad):
    return (grad,)

def back_keep(v):
    return (v, None)

def back_low(kept, grad):
    return (low(grad),)
low.defvjp(low_keep, low_pass)
low_back.defvjp(back_keep, back_low)
HIGHEST = lax.Precision.HIGHEST
EPSILON = 1e-05

def project(left, right):
    return jnp.dot(left, right, precision=HIGHEST, preferred_element_type=jnp.float32)

def normalize(values, scale_row, offset_row):
    average = lax.optimization_barrier(jnp.mean(values, axis=-1, keepdims=True))
    centered = values - average
    variance = lax.optimization_barrier(jnp.mean(centered * centered, axis=-1, keepdims=True))
    return centered * lax.rsqrt(variance + EPSILON) * scale_row + offset_row

def block_forward(inputs, w_query, b_query, w_key, w_value, b_value, w_output, b_output, attn_gain, attn_shift, w_inner, b_inner, w_outer, b_outer, ffn_gain, ffn_shift):
    group_size, positions, features = inputs.shape
    head_count = features // HD
    rows_in = inputs.reshape(group_size * positions, features)
    queries = low_back(low(project(rows_in, w_query) + b_query))
    key_rows = low_back(low(project(rows_in, w_key)))
    value_rows = low_back(low(project(rows_in, w_value) + b_value))
    split_shape = (group_size, positions, head_count, HD)
    scores = jnp.einsum('gqhe,gkhe->ghqk', queries.reshape(split_shape), key_rows.reshape(split_shape), precision=HIGHEST) * HD ** (-0.5)
    scores = low_back(scores)
    log_total = jax.nn.logsumexp(scores, axis=-1, keepdims=True)
    weights = low(jnp.exp(scores - log_total))
    context = jnp.einsum('ghqk,gkhe->gqhe', weights, value_rows.reshape(split_shape), precision=HIGHEST)
    context = low_back(low(context.reshape(group_size * positions, features)))
    attended = low_back(project(context, w_output) + b_output)
    normed = normalize(rows_in + attended, attn_gain, attn_shift)
    hidden = low_back(project(low(normed), w_inner) + b_inner)
    active = low(jax.nn.gelu(hidden, approximate=False))
    branch = low_back(project(active, w_outer) + b_outer)
    result = normalize(normed + branch, ffn_gain, ffn_shift)
    return result.reshape(group_size, positions, features)

def reference(inputs, cotangent, masked, w_query, b_query, w_key, w_value, b_value, w_output, b_output, attn_gain, attn_shift, w_inner, b_inner, w_outer, b_outer, ffn_gain, ffn_shift):
    parameters = tuple((item.astype(jnp.float32) for item in (w_query, b_query, w_key, w_value, b_value, w_output, b_output, attn_gain, attn_shift, w_inner, b_inner, w_outer, b_outer, ffn_gain, ffn_shift)))
    group_size = math.gcd(SENTS, 8)
    group_count = SENTS // group_size
    input_groups = inputs.astype(jnp.float32).reshape(group_count, group_size, LEN, D)
    grad_groups = (cotangent.astype(jnp.float32) * masked.astype(jnp.float32)[:, :, None]).reshape(group_count, group_size, LEN, D)

    def accumulate(summed, slices):
        input_part, grad_part = slices
        result, pullback = jax.vjp(block_forward, input_part, *parameters)
        pulled = pullback(grad_part)
        summed = tuple((left + right for left, right in zip(summed, pulled[1:])))
        return (summed, (result.astype(jnp.bfloat16), pulled[0].astype(jnp.bfloat16)))
    zeros_start = tuple((jnp.zeros_like(item) for item in parameters))
    summed, (result_all, grad_all) = lax.scan(accumulate, zeros_start, (input_groups, grad_groups))
    outputs = result_all.reshape(SENTS, LEN, D)
    grad_inputs = grad_all.reshape(SENTS, LEN, D)
    return (outputs, grad_inputs, summed[0], summed[1], summed[2], summed[3], summed[4], summed[5], summed[6], summed[7], summed[8], summed[9], summed[10], summed[11], summed[12], summed[13], summed[14])
```

```python
import jax
import jax.numpy as jnp
from jax import lax
from jax.sharding import PartitionSpec as P

HD = 64
EPSILON = 1e-05


def project(left, right):
    return jnp.dot(left, right, preferred_element_type=jnp.float32)


def transposed(left, right):
    return lax.dot_general(
        left, right, (((0,), (0,)), ((), ())), preferred_element_type=jnp.float32
    )


def backprod(left, right):
    return lax.dot_general(
        left, right, (((1,), (1,)), ((), ())), preferred_element_type=jnp.float32
    )


def normalize(values, scale_row, offset_row):
    average = jnp.mean(values, axis=-1, keepdims=True)
    centered = values - average
    variance = jnp.mean(centered * centered, axis=-1, keepdims=True)
    return centered * lax.rsqrt(variance + EPSILON) * scale_row + offset_row


def smooth(values):
    return jax.nn.gelu(values, approximate=False)


def heads_of(values, count):
    rows, features = values.shape
    return values.reshape(count, rows // count, features // HD, HD)


def attend(queries, key_rows, value_rows, count):
    scaling = HD ** (-0.5)
    query_heads, key_heads, value_heads = (
        heads_of(v, count) for v in (queries, key_rows, value_rows)
    )
    scores = (
        jnp.einsum("sqhe,skhe->shqk", query_heads, key_heads, preferred_element_type=jnp.float32)
        * scaling
    )
    log_total = jax.nn.logsumexp(scores, axis=-1, keepdims=True)
    weights = jnp.exp(scores - log_total).astype(jnp.bfloat16)
    context = jnp.einsum(
        "shqk,skhe->sqhe", weights, value_heads, preferred_element_type=jnp.float32
    )
    return context.reshape(queries.shape).astype(jnp.bfloat16), log_total


def attend_back(queries, key_rows, value_rows, log_total, grad_context, count):
    scaling = HD ** (-0.5)
    query_heads, key_heads, value_heads, grad_heads = (
        heads_of(v, count) for v in (queries, key_rows, value_rows, grad_context)
    )
    scores = (
        jnp.einsum("sqhe,skhe->shqk", query_heads, key_heads, preferred_element_type=jnp.float32)
        * scaling
    )
    probability = jnp.exp(scores - log_total)
    weights = probability.astype(jnp.bfloat16)
    grad_weights = jnp.einsum(
        "sqhe,skhe->shqk", grad_heads, value_heads, preferred_element_type=jnp.float32
    )
    row_dots = jnp.sum(probability * grad_weights, axis=-1, keepdims=True)
    grad_scores = (probability * (grad_weights - row_dots)).astype(jnp.bfloat16)
    grad_queries = (
        jnp.einsum("shqk,skhe->sqhe", grad_scores, key_heads, preferred_element_type=jnp.float32)
        * scaling
    )
    grad_keys = (
        jnp.einsum("shqk,sqhe->skhe", grad_scores, query_heads, preferred_element_type=jnp.float32)
        * scaling
    )
    grad_values = jnp.einsum(
        "shqk,sqhe->skhe", weights, grad_heads, preferred_element_type=jnp.float32
    )
    return tuple(
        v.reshape(queries.shape).astype(jnp.bfloat16) for v in (grad_queries, grad_keys, grad_values)
    )


def swap(value, axis, size, bit):
    return lax.ppermute(value, axis, [(i, i ^ bit) for i in range(size)])


def to_sentences(value, size):
    me = lax.axis_index("seq")
    count, block, features = value.shape
    part = count // size
    blocks = value.reshape(size, part, block, features)
    got = [
        swap(lax.dynamic_index_in_dim(blocks, me ^ k, 0, keepdims=False), "seq", size, k)
        if k
        else lax.dynamic_index_in_dim(blocks, me, 0, keepdims=False)
        for k in range(size)
    ]
    return jnp.stack(got, axis=1).reshape(part * size * block, features)


def to_positions(rows, size, shape):
    me = lax.axis_index("seq")
    count, block, features = shape
    part = count // size
    blocks = rows.reshape(part, size, block, features)
    got = jnp.stack([blocks[:, 0]] + [swap(blocks[:, k], "seq", size, k) for k in range(1, size)])
    back = [lax.dynamic_index_in_dim(got, me ^ j, 0, keepdims=False) for j in range(size)]
    return jnp.concatenate(back, axis=0).reshape(shape)


class Halving:
    def __init__(self, sizes):
        self.sizes = sizes

    def bits(self, axis):
        n = self.sizes[axis]
        return [1 << i for i in range(n.bit_length() - 1)]

    def reduce(self, value, order):
        names = [("seq", 1), *[("dp", b) for b in reversed(self.bits("dp"))], ("seq", 2)]
        kept = [value]
        left = list(names)
        for name in order:
            axis, bit = name
            at = left.index(name)
            mine = (lax.axis_index(axis) & bit) // bit
            send = sum(
                lax.dynamic_index_in_dim(v, 1 - mine, at, keepdims=False).astype(jnp.float32)
                for v in kept
            ).astype(jnp.bfloat16)
            got = swap(send, axis, self.sizes[axis], bit)
            kept = [lax.dynamic_index_in_dim(v, mine, at, keepdims=False) for v in kept] + [got]
            left.pop(at)
        return sum(v.astype(jnp.float32) for v in kept)

    def spread(self, value):
        for bit in (2, 1):
            mine = lax.axis_index("seq") & bit
            other = swap(value, "seq", self.sizes["seq"], bit)
            value = jnp.where(mine != 0, jnp.stack([other, value]), jnp.stack([value, other]))
        return jnp.swapaxes(value, 0, 1)


def cut(grad, dp):
    rows, columns = grad.shape
    bits = dp.bit_length() - 1
    piece = grad.reshape(dp, 2, rows // dp // 2, 2, columns // 2)
    piece = piece.transpose(3, 0, 1, 2, 4)
    return piece.reshape(2, *[2] * bits, 2, rows // dp // 2, columns // 2)


def uncut(pieces, rows, columns):
    return pieces.transpose(0, 2, 1, 3).reshape(rows, columns)


def make_body(sizes):
    size, dp = sizes["seq"], sizes["dp"]
    halving = Halving(sizes)

    def reduce_group(grads, order):
        width = grads[0].shape[1]
        parts = []
        for g in grads:
            c = cut(g.astype(jnp.bfloat16), dp)
            parts.append(c)
        joined = jnp.concatenate(parts, axis=-2)
        piece = halving.reduce(joined, order).astype(jnp.bfloat16)
        spread = halving.spread(piece).astype(jnp.float32)
        out, at = [], 0
        for g in grads:
            rows = g.shape[0] // dp
            out.append(uncut(spread[:, :, at : at + rows // 2], rows, width))
            at += rows // 2
        return out

    def body(
        inputs,
        cotangent,
        masked,
        w_query,
        b_query,
        w_key,
        w_value,
        b_value,
        w_output,
        b_output,
        attn_gain,
        attn_shift,
        w_inner,
        b_inner,
        w_outer,
        b_outer,
        ffn_gain,
        ffn_shift,
    ):
        shape = inputs.shape
        count = shape[0] // size
        masked_grad = cotangent * masked[:, :, None].astype(jnp.bfloat16)
        rows_in = to_sentences(inputs, size)
        grad_local = to_sentences(masked_grad, size)
        queries = (project(rows_in, w_query) + b_query).astype(jnp.bfloat16)
        key_rows = project(rows_in, w_key).astype(jnp.bfloat16)
        value_rows = (project(rows_in, w_value) + b_value).astype(jnp.bfloat16)
        context_rows, log_total = attend(queries, key_rows, value_rows, count)
        attended = project(context_rows, w_output) + b_output
        residual = rows_in.astype(jnp.float32) + attended
        normed, first_back = jax.vjp(
            normalize, residual, attn_gain.astype(jnp.float32), attn_shift.astype(jnp.float32)
        )
        normed_low = normed.astype(jnp.bfloat16)
        hidden = project(normed_low, w_inner) + b_inner
        activated, gelu_back = jax.vjp(smooth, hidden)
        active = activated.astype(jnp.bfloat16)
        branch = project(active, w_outer) + b_outer
        result, second_back = jax.vjp(
            normalize, normed + branch, ffn_gain.astype(jnp.float32), ffn_shift.astype(jnp.float32)
        )
        grad_mid, grad_ffn_gain, grad_ffn_shift = second_back(grad_local.astype(jnp.float32))
        grad_branch = grad_mid.astype(jnp.bfloat16)
        grad_w_outer = transposed(active, grad_branch)
        grad_b_outer = jnp.sum(grad_branch, axis=0, dtype=jnp.float32)
        (grad_hidden_f,) = gelu_back(backprod(grad_branch, w_outer))
        grad_hidden = grad_hidden_f.astype(jnp.bfloat16)
        grad_w_inner = transposed(normed_low, grad_hidden)
        grad_b_inner = jnp.sum(grad_hidden, axis=0, dtype=jnp.float32)
        grad_normed = backprod(grad_hidden, w_inner) + grad_mid
        grad_sum, grad_attn_gain, grad_attn_shift = first_back(grad_normed)
        grad_attended = grad_sum.astype(jnp.bfloat16)
        grad_w_output = transposed(context_rows, grad_attended)
        grad_b_output = jnp.sum(grad_attended, axis=0, dtype=jnp.float32)
        grad_context = backprod(grad_attended, w_output).astype(jnp.bfloat16)
        grad_queries, grad_keys, grad_values = attend_back(
            queries, key_rows, value_rows, log_total, grad_context, count
        )
        grad_w_query = transposed(rows_in, grad_queries)
        grad_b_query = jnp.sum(grad_queries, axis=0, dtype=jnp.float32)
        grad_w_key = transposed(rows_in, grad_keys)
        grad_w_value = transposed(rows_in, grad_values)
        grad_b_value = jnp.sum(grad_values, axis=0, dtype=jnp.float32)
        grad_rows_in = (
            backprod(grad_queries, w_query)
            + backprod(grad_keys, w_key)
            + backprod(grad_values, w_value)
            + grad_sum
        )
        outputs = to_positions(result.astype(jnp.bfloat16), size, shape)
        grad_inputs = to_positions(grad_rows_in.astype(jnp.bfloat16), size, shape)

        core, y = ("seq", 1), ("seq", 2)
        dp_bits = [("dp", b) for b in halving.bits("dp")]
        (g_outer,) = reduce_group([grad_w_outer], [core, y, *dp_bits])
        (g_inner,) = reduce_group([grad_w_inner], [core, *dp_bits, y])
        vectors = [
            grad_b_query,
            grad_b_value,
            grad_b_output,
            grad_attn_gain,
            grad_attn_shift,
            grad_b_inner,
            grad_b_outer,
            grad_ffn_gain,
            grad_ffn_shift,
        ]
        table = jnp.concatenate([v.reshape(dp, -1) for v in vectors], axis=1)
        used = table.shape[1]
        width = w_query.shape[1]
        extra = -(-used // (2 * width)) * 2
        table = jnp.pad(table, ((0, 0), (0, extra * width - used))).reshape(dp * extra, width)
        g_output, g_query, g_key, g_value, g_table = reduce_group(
            [grad_w_output, grad_w_query, grad_w_key, grad_w_value, table],
            [core, *dp_bits[1:], dp_bits[0], y],
        )
        flat = g_table.reshape(-1)
        out_vectors, at = [], 0
        for v in vectors:
            n = v.shape[0] // dp
            out_vectors.append(flat[at : at + n])
            at += n
        bq, bv, bo, ag, ash, bi, bou, fg, fs = out_vectors
        return (
            outputs,
            grad_inputs,
            g_query,
            bq,
            g_key,
            g_value,
            bv,
            g_output,
            bo,
            ag,
            ash,
            g_inner,
            bi,
            g_outer,
            bou,
            fg,
            fs,
        )

    return body


def solution(mesh):
    rows = P("dp", "seq", None)
    matrix, vector = P("dp", None), P("dp")
    in_specs = (rows, rows, P("dp", "seq"), *[P()] * 15)
    out_specs = (
        rows,
        rows,
        matrix,
        vector,
        matrix,
        matrix,
        vector,
        matrix,
        vector,
        vector,
        vector,
        matrix,
        vector,
        matrix,
        vector,
        vector,
        vector,
    )
    body = make_body(dict(mesh.shape))
    return jax.shard_map(
        body, mesh=mesh, in_specs=in_specs, out_specs=out_specs, check_vma=False
    )
```

```python
import jax
import jax.numpy as jnp
from jax import lax
from jax.experimental import pallas as pl
from jax.experimental.pallas import tpu as pltpu
from jax.sharding import PartitionSpec as P

HD = 64
EPSILON = 1e-05
F32, BF16 = jnp.float32, jnp.bfloat16
PAIR = 2 * HD


def nn(a, b):
    return lax.dot_general(a, b, (((1,), (0,)), ((), ())), preferred_element_type=F32)


def nt(a, b):
    return lax.dot_general(a, b, (((1,), (1,)), ((), ())), preferred_element_type=F32)


def tn(a, b):
    return lax.dot_general(a, b, (((0,), (0,)), ((), ())), preferred_element_type=F32)


def halves(value):
    lane = lax.broadcasted_iota(jnp.int32, value.shape, 1)
    zero = jnp.zeros_like(value)
    return jnp.where(lane < HD, value, zero), jnp.where(lane < HD, zero, value)


def standardize(v):
    mean = jnp.mean(v, axis=-1, keepdims=True)
    c = v - mean
    r = lax.rsqrt(jnp.mean(c * c, axis=-1, keepdims=True) + EPSILON)
    return c * r, r


def attention_kernel(
    x_ref, wq_ref, wk_ref, wv_ref, wo_ref, bq_ref, bv_ref, bo_ref, gain_ref, shift_ref,
    q_ref, k_ref, v_ref, p_ref, ctx_ref, n_ref, r_ref, low_ref,
):
    rows, width = x_ref.shape
    tile = 256
    for j in range(width // tile):
        at = pl.ds(j * tile, tile)
        x = x_ref[...]
        q = (nn(x, wq_ref[:, at]) + bq_ref[:, at].astype(F32)).astype(BF16)
        q_ref[:, at] = q * jnp.asarray(HD ** -0.5, BF16)
        k_ref[:, at] = nn(x, wk_ref[:, at]).astype(BF16)
        v_ref[:, at] = (nn(x, wv_ref[:, at]) + bv_ref[:, at].astype(F32)).astype(BF16)

    def pair(p, carry):
        at = pl.ds(pl.multiple_of(p * PAIR, PAIR), PAIR)
        q, k, v = q_ref[:, at], k_ref[:, at], v_ref[:, at]
        vt = v.astype(F32).T.astype(BF16)
        out = []
        for i, kh in enumerate(halves(k)):
            s = nt(kh, q)
            e = jnp.exp(s - jnp.max(s, axis=0, keepdims=True))
            w = (e * (1.0 / jnp.sum(e, axis=0, keepdims=True))).astype(BF16)
            p_ref[2 * p + i] = w
            out.append(nn(vt[i * HD : (i + 1) * HD], w))
        ctx_ref[:, at] = jnp.concatenate(out, axis=0).T.astype(BF16)
        return carry

    lax.fori_loop(0, width // PAIR, pair, 0)
    v1 = jnp.concatenate(
        [nn(ctx_ref[...], wo_ref[:, j * tile : (j + 1) * tile]) for j in range(width // tile)], axis=1
    )
    v1 = x_ref[...].astype(F32) + (v1 + bo_ref[...].astype(F32))
    n, r = standardize(v1)
    n_ref[...] = n
    r_ref[...] = r
    low_ref[...] = (n * gain_ref[...].astype(F32) + shift_ref[...].astype(F32)).astype(BF16)


def params(mb):
    return pltpu.CompilerParams(vmem_limit_bytes=mb * 1024 * 1024)


def attention(x, wq, wk, wv, wo, bq, bv, bo, gain, shift):
    rows, width = x.shape
    heads = width // HD
    wide = jax.ShapeDtypeStruct((rows, width), BF16)
    return pl.pallas_call(
        attention_kernel,
        out_shape=(
            wide, wide, wide,
            jax.ShapeDtypeStruct((heads, rows, rows), BF16),
            wide,
            jax.ShapeDtypeStruct((rows, width), F32),
            jax.ShapeDtypeStruct((rows, 1), F32),
            wide,
        ),
        compiler_params=params(48),
        name="attention",
    )(x, wq, wk, wv, wo, bq, bv, bo, gain, shift)


def hidden_kernel(low_ref, w_ref, b_ref, act_ref, slope_ref):
    tile = 256

    def step(j, carry):
        at = pl.ds(pl.multiple_of(j * tile, tile), tile)
        h = nn(low_ref[...], w_ref[:, at]) + b_ref[:, at].astype(F32)
        a = jnp.abs(h)
        bell = jnp.exp(h * h * -0.5)
        t = 1.0 / (1.0 + (0.3275911 * 0.7071067811865476) * a)
        poly = t * (0.127414796 + t * (-0.142248368 + t * (0.7107068705 + t * (-0.7265760135 + t * 0.5307027145))))
        tail = poly * bell
        phi = jnp.where(h < 0.0, tail, 1.0 - tail)
        act_ref[:, at] = (h * phi).astype(BF16)
        slope_ref[:, at] = (phi + h * (bell * 0.3989422804014327)).astype(BF16)
        return carry

    lax.fori_loop(0, w_ref.shape[1] // tile, step, 0)


def hidden_layer(low, w, b):
    shape = jax.ShapeDtypeStruct((low.shape[0], w.shape[1]), BF16)
    return pl.pallas_call(hidden_kernel, out_shape=(shape, shape), compiler_params=params(32), name="hidden")(low, w, b)


def norm_back(e, n, r):
    return r * (e - jnp.mean(e, axis=-1, keepdims=True) - n * jnp.mean(e * n, axis=-1, keepdims=True))


def branch_kernel(
    core_ref, act_ref, w_ref, b_ref, n_ref, gain1_ref, shift1_ref, gain_ref, shift_ref, cot_ref,
    out_ref, mid_ref, low_ref, half_ref, other_ref, sums_ref,
):
    rows, width = out_ref.shape
    tile = 256
    normed = n_ref[...] * gain1_ref[...].astype(F32) + shift1_ref[...].astype(F32)
    branch = jnp.concatenate(
        [nn(act_ref[...], w_ref[:, j * tile : (j + 1) * tile]) for j in range(width // tile)], axis=1
    )
    n, r = standardize(normed + (branch + b_ref[...].astype(F32)))
    gain = gain_ref[...].astype(F32)
    out_ref[...] = (n * gain + shift_ref[...].astype(F32)).astype(BF16)
    go = cot_ref[...].astype(F32)
    mid = norm_back(go * gain, n, r)
    mid_ref[...] = mid
    low = mid.astype(BF16)
    low_ref[...] = low
    half = width // 2
    core = core_ref[0]
    half_ref[...] = jnp.where(core == 0, low[:, :half], low[:, half:])
    other_ref[...] = jnp.where(core == 0, low[:, half:], low[:, :half])
    sums_ref[0:1] = jnp.sum(go * n, axis=0, keepdims=True)
    sums_ref[1:2] = jnp.sum(go, axis=0, keepdims=True)
    sums_ref[2:3] = jnp.sum(low.astype(F32), axis=0, keepdims=True)


SCALAR = pl.BlockSpec(memory_space=pltpu.SMEM)
VMEM = pl.BlockSpec(memory_space=pltpu.VMEM)


def branch_layer(core, act, w, b, n, gain1, shift1, gain, shift, cot):
    rows, width = n.shape
    half = jax.ShapeDtypeStruct((rows, width // 2), BF16)
    wide = jax.ShapeDtypeStruct((rows, width), BF16)
    return pl.pallas_call(
        branch_kernel,
        in_specs=[SCALAR] + [VMEM] * 9,
        out_shape=(wide, jax.ShapeDtypeStruct((rows, width), F32), wide, half, half, jax.ShapeDtypeStruct((3, width), F32)),
        compiler_params=params(40),
        name="branch",
    )(core, act, w, b, n, gain1, shift1, gain, shift, cot)


def hidden_back_kernel(core_ref, low_ref, w_ref, slope_ref, full_ref, half_ref, other_ref, sums_ref):
    tile = 256
    per = half_ref.shape[1] // tile
    core = core_ref[0]

    def step(j, carry):
        at = pl.ds(pl.multiple_of(j * tile, tile), tile)
        g = (nt(low_ref[...], w_ref[at, :]) * slope_ref[:, at].astype(F32)).astype(BF16)
        full_ref[:, at] = g
        sums_ref[:, at] = jnp.sum(g.astype(F32), axis=0, keepdims=True)
        inner = pl.ds(pl.multiple_of(lax.rem(j, per) * tile, tile), tile)
        mine = j // per == core

        @pl.when(mine)
        def _():
            half_ref[:, inner] = g

        @pl.when(jnp.logical_not(mine))
        def _():
            other_ref[:, inner] = g

        return carry

    lax.fori_loop(0, w_ref.shape[0] // tile, step, 0)


def hidden_back(core, low, w, slope):
    rows, wide = slope.shape
    half = jax.ShapeDtypeStruct((rows, wide // 2), BF16)
    return pl.pallas_call(
        hidden_back_kernel,
        in_specs=[SCALAR] + [VMEM] * 3,
        out_shape=(jax.ShapeDtypeStruct((rows, wide), BF16), half, half, jax.ShapeDtypeStruct((1, wide), F32)),
        compiler_params=params(40),
        name="hidden_back",
    )(core, low, w, slope)


def outer_kernel(left_a, left_b, right_a, right_b, out_ref):
    tile = 256

    def step(j, carry):
        at = pl.ds(pl.multiple_of(j * tile, tile), tile)
        out_ref[at, :] = (tn(left_a[:, at], right_a[...]) + tn(left_b[:, at], right_b[...])).astype(BF16)
        return carry

    lax.fori_loop(0, left_a.shape[1] // tile, step, 0)


def outer(left_a, left_b, right_a, right_b, name):
    return pl.pallas_call(
        outer_kernel,
        out_shape=jax.ShapeDtypeStruct((left_a.shape[1], right_a.shape[1]), BF16),
        compiler_params=params(32),
        name=name,
    )(left_a, left_b, right_a, right_b)


def first_back_kernel(
    core_ref, gh_ref, w_ref, mid_ref, n_ref, r_ref, gain_ref, wo_ref,
    sum_ref, gctx_ref, half_ref, other_ref, sums_ref,
):
    rows, width = mid_ref.shape
    tile = 256
    gn = jnp.concatenate(
        [nt(gh_ref[...], w_ref[j * tile : (j + 1) * tile, :]) for j in range(width // tile)], axis=1
    )
    gn = gn + mid_ref[...]
    n = n_ref[...]
    gs = norm_back(gn * gain_ref[...].astype(F32), n, r_ref[...])
    sum_ref[...] = gs
    low = gs.astype(BF16)
    half = width // 2
    core = core_ref[0]
    half_ref[...] = jnp.where(core == 0, low[:, :half], low[:, half:])
    other_ref[...] = jnp.where(core == 0, low[:, half:], low[:, :half])
    sums_ref[0:1] = jnp.sum(gn * n, axis=0, keepdims=True)
    sums_ref[1:2] = jnp.sum(gn, axis=0, keepdims=True)
    sums_ref[2:3] = jnp.sum(low.astype(F32), axis=0, keepdims=True)
    for j in range(width // tile):
        gctx_ref[:, j * tile : (j + 1) * tile] = nt(low, wo_ref[j * tile : (j + 1) * tile, :]).astype(BF16)


def first_back(core, gh, w, mid, n, r, gain, wo):
    rows, width = mid.shape
    half = jax.ShapeDtypeStruct((rows, width // 2), BF16)
    wide = jax.ShapeDtypeStruct((rows, width), BF16)
    return pl.pallas_call(
        first_back_kernel,
        in_specs=[SCALAR] + [VMEM] * 7,
        out_shape=(jax.ShapeDtypeStruct((rows, width), F32), wide, half, half, jax.ShapeDtypeStruct((3, width), F32)),
        compiler_params=params(40),
        name="first_back",
    )(core, gh, w, mid, n, r, gain, wo)


def attention_back_kernel(core_ref, q_ref, k_ref, v_ref, p_ref, g_ref, full_ref, half_ref, other_ref, sums_ref):
    rows, width = q_ref.shape
    pairs = width // PAIR
    per = pairs // 2
    core = core_ref[0]

    def pair(p, carry):
        at = pl.ds(pl.multiple_of(p * PAIR, PAIR), PAIR)
        q, k, v, g = q_ref[:, at], k_ref[:, at], v_ref[:, at], g_ref[:, at]
        kt = k.astype(F32).T.astype(BF16)
        gk = jnp.zeros((rows, PAIR), F32)
        gv = jnp.zeros((rows, PAIR), F32)
        gq = []
        for i, (qh, vh, gh) in enumerate(zip(halves(q), halves(v), halves(g))):
            w = p_ref[2 * p + i]
            dw = nt(vh, g)
            w32 = w.astype(F32)
            prod = w32 * dw
            gs = (prod - w32 * jnp.sum(prod, axis=0, keepdims=True)).astype(BF16)
            gk = gk + nn(gs, qh)
            gv = gv + nn(w, gh)
            gq.append(nn(kt[i * HD : (i + 1) * HD], gs))
        gq = (jnp.concatenate(gq, axis=0).T * HD ** -0.5).astype(BF16)
        gk, gv = gk.astype(BF16), gv.astype(BF16)
        inner = pl.ds(pl.multiple_of(lax.rem(p, per) * PAIR, PAIR), PAIR)
        mine = p // per == core
        for i, value in enumerate((gq, gk, gv)):
            full_ref[i, :, at] = value
            sums_ref[i : i + 1, at] = jnp.sum(value.astype(F32), axis=0, keepdims=True)

        @pl.when(mine)
        def _():
            for i, value in enumerate((gq, gk, gv)):
                half_ref[i, :, inner] = value

        @pl.when(jnp.logical_not(mine))
        def _():
            for i, value in enumerate((gq, gk, gv)):
                other_ref[i, :, inner] = value

        return carry

    lax.fori_loop(0, pairs, pair, 0)


def attention_back(core, q, k, v, p, g):
    rows, width = q.shape
    half = jax.ShapeDtypeStruct((3, rows, width // 2), BF16)
    return pl.pallas_call(
        attention_back_kernel,
        in_specs=[SCALAR] + [VMEM] * 5,
        out_shape=(jax.ShapeDtypeStruct((3, rows, width), BF16), half, half, jax.ShapeDtypeStruct((3, width), F32)),
        compiler_params=params(40),
        name="attention_back",
    )(core, q, k, v, p, g)


def three_kernel(xa_ref, xb_ref, ga_ref, gb_ref, out_ref):
    tile = 256
    for j in range(xa_ref.shape[1] // tile):
        xa = xa_ref[:, j * tile : (j + 1) * tile]
        xb = xb_ref[:, j * tile : (j + 1) * tile]
        for i in range(3):
            out_ref[i, j * tile : (j + 1) * tile, :] = (tn(xa, ga_ref[i]) + tn(xb, gb_ref[i])).astype(BF16)


def three_outer(xa, xb, ga, gb):
    return pl.pallas_call(
        three_kernel,
        out_shape=jax.ShapeDtypeStruct((3, xa.shape[1], ga.shape[2]), BF16),
        compiler_params=params(32),
        name="three_outer",
    )(xa, xb, ga, gb)


def input_back_kernel(g_ref, wq_ref, wk_ref, wv_ref, sum_ref, out_ref):
    tile = 256
    for j in range(out_ref.shape[1] // tile):
        at = slice(j * tile, (j + 1) * tile)
        total = nt(g_ref[0], wq_ref[at, :]) + nt(g_ref[1], wk_ref[at, :]) + nt(g_ref[2], wv_ref[at, :])
        out_ref[:, at] = (total + sum_ref[:, at]).astype(BF16)


def input_back(g, wq, wk, wv, gsum):
    return pl.pallas_call(
        input_back_kernel,
        out_shape=jax.ShapeDtypeStruct(gsum.shape, BF16),
        compiler_params=params(32),
        name="input_back",
    )(g, wq, wk, wv, gsum)


def swap(value, axis, size, bit):
    return lax.ppermute(value, axis, [(i, i ^ bit) for i in range(size)])


def to_sentences(value, size):
    me = lax.axis_index("seq")
    count, block, features = value.shape
    assert count == size
    got = [lax.dynamic_index_in_dim(value, me ^ k, 0, keepdims=False) for k in range(size)]
    got = [swap(v, "seq", size, k) if k else v for k, v in enumerate(got)]
    return jnp.concatenate(got, axis=0)


def to_positions(rows, size, shape):
    me = lax.axis_index("seq")
    blocks = rows.reshape(size, shape[1], shape[2])
    got = jnp.stack([blocks[0]] + [swap(blocks[k], "seq", size, k) for k in range(1, size)])
    back = [lax.dynamic_index_in_dim(got, me ^ j, 0, keepdims=False) for j in range(size)]
    return jnp.stack(back)


def make_body(sizes):
    size, dp = sizes["seq"], sizes["dp"]
    dp_bits = [1 << i for i in range(dp.bit_length() - 1)]
    y = ("seq", 2)
    names = [*[("dp", b) for b in reversed(dp_bits)], y]

    def my_bit(axis, bit):
        return (lax.axis_index(axis) & bit) // bit

    def pair(value):
        return swap(value, "seq", size, 1)

    def halve(value, order):
        kept, left = [value], list(names)
        for name in order:
            at = left.index(name) + 1
            mine = my_bit(*name)
            send = sum(lax.dynamic_index_in_dim(v, 1 - mine, at, keepdims=False).astype(F32) for v in kept)
            got = swap(send.astype(BF16), name[0], sizes[name[0]], name[1])
            kept = [lax.dynamic_index_in_dim(v, mine, at, keepdims=False) for v in kept] + [got]
            left.pop(at - 1)
        total = sum(v.astype(F32) for v in kept).astype(BF16)
        return total, left

    def spread(value, bit):
        other = swap(value, "seq", size, bit)
        first = my_bit("seq", bit) == 0
        return jnp.where(first, value, other), jnp.where(first, other, value)

    def reduce_group(value, order):
        group, rows, half = value.shape
        part = rows // dp // 2
        total, left = halve(value.reshape(group, *[2] * len(names), part, half), order)
        if left:
            total = (total.astype(F32) + swap(total, "seq", size, 2).astype(F32)).astype(BF16)
        else:
            total = jnp.stack(spread(total, 2), axis=1)
        total = total.reshape(group, 2 * part, half)
        return jnp.concatenate(spread(total, 1), axis=-1).astype(F32)

    def body(
        inputs,
        cotangent,
        masked,
        w_query,
        b_query,
        w_key,
        w_value,
        b_value,
        w_output,
        b_output,
        attn_gain,
        attn_shift,
        w_inner,
        b_inner,
        w_outer,
        b_outer,
        ffn_gain,
        ffn_shift,
    ):
        shape = inputs.shape
        width = shape[2]
        core = my_bit("seq", 1).reshape(1)
        row = lambda v: v.reshape(1, -1)
        x = to_sentences(inputs, size)
        cot = to_sentences(cotangent * masked[:, :, None].astype(BF16), size)
        q, k, v, p, ctx, n1, r1, low1 = attention(
            x, w_query, w_key, w_value, w_output, row(b_query), row(b_value), row(b_output),
            row(attn_gain), row(attn_shift),
        )
        x_other, ctx_other, low_other = pair(x), pair(ctx), pair(low1)
        act, slope = hidden_layer(low1, w_inner, row(b_inner))
        act_other = pair(act)
        out, mid, gb, gb_mine, gb_send, sums2 = branch_layer(
            core, act, w_outer, row(b_outer), n1, row(attn_gain), row(attn_shift),
            row(ffn_gain), row(ffn_shift), cot,
        )
        gb_other = pair(gb_send)
        gh, gh_mine, gh_send, sum_inner = hidden_back(core, gb, w_outer, slope)
        gh_other = pair(gh_send)
        grad_outer = outer(act, act_other, gb_mine, gb_other, "grad_outer")
        (g_outer,) = reduce_group(grad_outer[None], names[-1:] + names[:-1][::-1])
        grad_inner = outer(low1, low_other, gh_mine, gh_other, "grad_inner")
        (g_inner,) = reduce_group(grad_inner[None], names[:-1][::-1] + names[-1:])
        gsum, gctx, ga_mine, ga_send, sums1 = first_back(
            core, gh, w_inner, mid, n1, r1, row(attn_gain), w_output
        )
        ga_other = pair(ga_send)
        g3, g3_mine, g3_send, sums0 = attention_back(core, q, k, v, p, gctx)
        g3_other = pair(g3_send)
        grad_output = outer(ctx, ctx_other, ga_mine, ga_other, "grad_output")
        grad_three = three_outer(x, x_other, g3_mine, g3_other)
        grad_x = input_back(g3, w_query, w_key, w_value, gsum)
        outputs = to_positions(out, size, shape)
        grad_inputs = to_positions(grad_x, size, shape)

        vectors = [
            sums0[0], sums0[2], sums1[2], sums1[0], sums1[1], sum_inner[0], sums2[2], sums2[0], sums2[1],
        ]
        table = jnp.concatenate([v.reshape(dp, -1) for v in vectors], axis=1)
        used = table.shape[1]
        half = width // 2
        lines = -(-used // (4 * half))
        table = jnp.pad(table, ((0, 0), (0, lines * 4 * half - used)))
        table = table + pair(table)
        table = table.reshape(dp, 2, lines, 2, half)
        table = lax.dynamic_index_in_dim(table, core[0], 3, keepdims=False).astype(BF16)
        part = width // dp // 2
        rest = jnp.concatenate([grad_three, grad_output[None]]).reshape(4, dp, 2, part, half)
        rest = rest.transpose(1, 2, 0, 3, 4).reshape(dp, 2, 4 * part, half)
        rest = jnp.concatenate([rest, table], axis=2)
        (rest,) = reduce_group(
            rest.reshape(1, dp * 2 * (4 * part + lines), half), names[:-1][::-1] + names[-1:]
        )
        rest = rest.reshape(2, 4 * part + lines, width)
        g_query, g_key, g_value, g_output = (
            rest[:, i * part : (i + 1) * part].reshape(2 * part, width) for i in range(4)
        )
        flat = rest[:, 4 * part :].reshape(-1)
        small, at = [], 0
        for v in vectors:
            small.append(flat[at : at + v.shape[0] // dp])
            at += v.shape[0] // dp
        bq, bv, bo, ag, ash, bi, bou, fg, fs = small
        return (
            outputs,
            grad_inputs,
            g_query,
            bq,
            g_key,
            g_value,
            bv,
            g_output,
            bo,
            ag,
            ash,
            g_inner,
            bi,
            g_outer,
            bou,
            fg,
            fs,
        )

    return body


def solution(mesh):
    rows = P("dp", "seq", None)
    matrix, vector = P("dp", None), P("dp")
    in_specs = (rows, rows, P("dp", "seq"), *[P()] * 15)
    out_specs = (
        rows,
        rows,
        matrix,
        vector,
        matrix,
        matrix,
        vector,
        matrix,
        vector,
        vector,
        vector,
        matrix,
        vector,
        matrix,
        vector,
        vector,
        vector,
    )
    body = make_body(dict(mesh.shape))
    return jax.shard_map(
        body, mesh=mesh, in_specs=in_specs, out_specs=out_specs, check_vma=False
    )
```

```python
import jax
import jax.numpy as jnp
from jax import lax
from jax.experimental import pallas as pl
from jax.experimental.pallas import tpu as pltpu
from jax.sharding import PartitionSpec as P

HD = 64
PAIR = 2 * HD
TILE = 256
EPSILON = 1e-05
F32, BF16 = jnp.float32, jnp.bfloat16
CORE, YBIT, SLOTS = 0, 1, 2
TABLE = 16


def nn(a, b):
    return lax.dot_general(a, b, (((1,), (0,)), ((), ())), preferred_element_type=F32)


def nt(a, b):
    return lax.dot_general(a, b, (((1,), (1,)), ((), ())), preferred_element_type=F32)


def tn(a, b):
    return lax.dot_general(a, b, (((0,), (0,)), ((), ())), preferred_element_type=F32)


def like(shape, dtype=BF16):
    return jax.ShapeDtypeStruct(shape, dtype)


def call(kernel, name, info, ins, outs, us, mb=16, after=()):
    n, skip = len(ins), len(after)

    def run(info_ref, *refs):
        kernel(info_ref, *refs[:n], *refs[n + skip :])

    return pl.pallas_call(
        run,
        in_specs=[pl.BlockSpec(memory_space=pltpu.SMEM)]
        + [pl.BlockSpec(memory_space=pltpu.VMEM)] * n
        + [pl.BlockSpec(memory_space=pl.ANY)] * skip,
        out_shape=outs,
        compiler_params=pltpu.CompilerParams(vmem_limit_bytes=mb * 1024 * 1024),
        cost_estimate=pl.CostEstimate(
            flops=int(us * 1.1e9), bytes_accessed=int(us * 1e5), transcendentals=0
        ),
        name=name,
    )(info, *ins, *after)


def halves(value):
    lane = lax.broadcasted_iota(jnp.int32, value.shape, 1)
    zero = jnp.zeros_like(value)
    return jnp.where(lane < HD, value, zero), jnp.where(lane < HD, zero, value)


def standardize(v):
    mean = jnp.mean(v, axis=-1, keepdims=True)
    c = v - mean
    r = lax.rsqrt(jnp.mean(c * c, axis=-1, keepdims=True) + EPSILON)
    return c * r, r


def norm_back(e, n, r):
    return r * (e - jnp.mean(e, axis=-1, keepdims=True) - n * jnp.mean(e * n, axis=-1, keepdims=True))


def columns(width):
    return [slice(j, j + TILE) for j in range(0, width, TILE)]


def total(value):
    return jnp.sum(value, axis=0, keepdims=True)


def attention_kernel(
    info_ref, x0, x1, x2, x3, wq_ref, wk_ref, wv_ref, wo_ref, bq_ref, bv_ref, bo_ref, gain_ref, shift_ref,
    x_ref, q_ref, k_ref, v_ref, p_ref, ctx_ref, n_ref, r_ref, low_ref,
):
    rows, width = x_ref.shape
    block = x0.shape[0]
    for i, part in enumerate((x0, x1, x2, x3)):
        x_ref[i * block : (i + 1) * block, :] = part[...]
    for at in columns(width):
        x = x_ref[...]
        q = (nn(x, wq_ref[:, at]) + bq_ref[:, at].astype(F32)).astype(BF16)
        q_ref[:, at] = q * jnp.asarray(HD ** -0.5, BF16)
        k_ref[:, at] = nn(x, wk_ref[:, at]).astype(BF16)
        v_ref[:, at] = (nn(x, wv_ref[:, at]) + bv_ref[:, at].astype(F32)).astype(BF16)

    def pair(p, carry):
        at = pl.ds(pl.multiple_of(p * PAIR, PAIR), PAIR)
        q, k, v = q_ref[:, at], k_ref[:, at], v_ref[:, at]
        vt = v.astype(F32).T.astype(BF16)
        out = []
        for i, kh in enumerate(halves(k)):
            s = nt(kh, q)
            e = jnp.exp(s - jnp.max(s, axis=0, keepdims=True))
            w = (e * (1.0 / total(e))).astype(BF16)
            p_ref[2 * p + i] = w
            out.append(nn(vt[i * HD : (i + 1) * HD], w))
        ctx_ref[:, at] = jnp.concatenate(out, axis=0).T.astype(BF16)
        return carry

    lax.fori_loop(0, width // PAIR, pair, 0)
    v1 = jnp.concatenate([nn(ctx_ref[...], wo_ref[:, at]) for at in columns(width)], axis=1)
    v1 = x_ref[...].astype(F32) + (v1 + bo_ref[...].astype(F32))
    n, r = standardize(v1)
    n_ref[...] = n
    r_ref[...] = r
    low_ref[...] = (n * gain_ref[...].astype(F32) + shift_ref[...].astype(F32)).astype(BF16)


def hidden_kernel(info_ref, low_ref, w_ref, b_ref, act_ref, slope_ref):
    def step(j, carry):
        at = pl.ds(pl.multiple_of(j * TILE, TILE), TILE)
        h = nn(low_ref[...], w_ref[:, at]) + b_ref[:, at].astype(F32)
        bell = jnp.exp(h * h * -0.5)
        t = 1.0 / (1.0 + (0.3275911 * 0.7071067811865476) * jnp.abs(h))
        poly = 0.7107068705 + t * (-0.7265760135 + t * 0.5307027145)
        tail = (t * (0.127414796 + t * (-0.142248368 + t * poly))) * bell
        phi = jnp.where(h < 0.0, tail, 1.0 - tail)
        act_ref[:, at] = (h * phi).astype(BF16)
        slope_ref[:, at] = (phi + h * (bell * 0.3989422804014327)).astype(BF16)
        return carry

    lax.fori_loop(0, w_ref.shape[1] // TILE, step, 0)


def split_store(core, value, mine_ref, other_ref):
    half = value.shape[1] // 2
    mine_ref[...] = jnp.where(core == 0, value[:, :half], value[:, half:])
    other_ref[...] = jnp.where(core == 0, value[:, half:], value[:, :half])


def branch_kernel(
    info_ref, act_ref, w_ref, b_ref, n_ref, gain1_ref, shift1_ref, gain_ref, shift_ref, cot_ref,
    out_ref, mid_ref, low_ref, mine_ref, other_ref, sums_ref,
):
    width = out_ref.shape[1]
    normed = n_ref[...] * gain1_ref[...].astype(F32) + shift1_ref[...].astype(F32)
    branch = jnp.concatenate([nn(act_ref[...], w_ref[:, at]) for at in columns(width)], axis=1)
    n, r = standardize(normed + (branch + b_ref[...].astype(F32)))
    gain = gain_ref[...].astype(F32)
    out_ref[...] = (n * gain + shift_ref[...].astype(F32)).astype(BF16)
    go = cot_ref[...].astype(F32)
    mid = norm_back(go * gain, n, r)
    mid_ref[...] = mid
    low = mid.astype(BF16)
    low_ref[...] = low
    split_store(info_ref[CORE], low, mine_ref, other_ref)
    sums_ref[0:1] = total(go * n)
    sums_ref[1:2] = total(go)
    sums_ref[2:3] = total(low.astype(F32))


def hidden_back_kernel(info_ref, low_ref, w_ref, slope_ref, mine_ref, other_ref, sums_ref):
    per = mine_ref.shape[1] // TILE
    core = info_ref[CORE]
    for ref, which in ((other_ref, 1 - core), (mine_ref, core)):

        def step(j, carry):
            at = pl.ds(pl.multiple_of((which * per + j) * TILE, TILE), TILE)
            g = (nt(low_ref[...], w_ref[at, :]) * slope_ref[:, at].astype(F32)).astype(BF16)
            ref[:, pl.ds(pl.multiple_of(j * TILE, TILE), TILE)] = g
            sums_ref[:, at] = total(g.astype(F32))
            return carry

        lax.fori_loop(0, per, step, 0)


def first_back_kernel(
    info_ref, gm_ref, go_ref, w_ref, mid_ref, n_ref, r_ref, gain_ref, wo_ref,
    sum_ref, gctx_ref, mine_ref, other_ref, sums_ref,
):
    width, half = mid_ref.shape[1], gm_ref.shape[1]
    core = info_ref[CORE]
    mine = pl.ds(pl.multiple_of(core * half, half), half)
    other = pl.ds(pl.multiple_of((1 - core) * half, half), half)
    gn = jnp.concatenate(
        [nt(gm_ref[...], w_ref[at, mine]) + nt(go_ref[...], w_ref[at, other]) for at in columns(width)], axis=1
    )
    gn = gn + mid_ref[...]
    n = n_ref[...]
    gs = norm_back(gn * gain_ref[...].astype(F32), n, r_ref[...])
    sum_ref[...] = gs
    low = gs.astype(BF16)
    split_store(core, low, mine_ref, other_ref)
    sums_ref[0:1] = total(gn * n)
    sums_ref[1:2] = total(gn)
    sums_ref[2:3] = total(low.astype(F32))
    for at in columns(width):
        gctx_ref[:, at] = nt(low, wo_ref[at, :]).astype(BF16)


def attention_back_kernel(flip):
    def kernel(info_ref, q_ref, k_ref, v_ref, p_ref, g_ref, out_ref, sums_ref):
        rows, width = q_ref.shape
        per = width // PAIR // 2
        core = info_ref[CORE]
        first = ((1 - core) if flip else core) * per

        def pair(p, carry):
            at = pl.ds(pl.multiple_of((first + p) * PAIR, PAIR), PAIR)
            to = pl.ds(pl.multiple_of(p * PAIR, PAIR), PAIR)
            q, k, v, g = q_ref[:, at], k_ref[:, at], v_ref[:, at], g_ref[:, at]
            kt = k.astype(F32).T.astype(BF16)
            gk = jnp.zeros((rows, PAIR), F32)
            gv = jnp.zeros((rows, PAIR), F32)
            gq = []
            for i, (qh, vh, gh) in enumerate(zip(halves(q), halves(v), halves(g))):
                w = p_ref[2 * (first + p) + i]
                w32 = w.astype(F32)
                prod = w32 * nt(vh, g)
                gs = (prod - w32 * total(prod)).astype(BF16)
                gk = gk + nn(gs, qh)
                gv = gv + nn(w, gh)
                gq.append(nn(kt[i * HD : (i + 1) * HD], gs))
            gq = jnp.concatenate(gq, axis=0).T * HD ** -0.5
            for i, value in enumerate((gq, gk, gv)):
                value = value.astype(BF16)
                out_ref[i, :, to] = value
                sums_ref[i : i + 1, to] = total(value.astype(F32))
            return carry

        lax.fori_loop(0, per, pair, 0)

    return kernel


def input_back_kernel(info_ref, gm_ref, go_ref, wq_ref, wk_ref, wv_ref, sum_ref, out_ref):
    half = gm_ref.shape[2]
    core = info_ref[CORE]
    mine = pl.ds(pl.multiple_of(core * half, half), half)
    other = pl.ds(pl.multiple_of((1 - core) * half, half), half)
    for at in columns(out_ref.shape[1]):
        value = sum_ref[:, at]
        for i, w in enumerate((wq_ref, wk_ref, wv_ref)):
            value = value + nt(gm_ref[i], w[at, mine]) + nt(go_ref[i], w[at, other])
        out_ref[:, at] = value.astype(BF16)


def place(info_ref, base, chunk, part, inner, size, value, keep_ref, send_ref, cols=slice(None)):
    slot = info_ref[base + chunk]
    half = keep_ref.shape[0] // part
    value = value.astype(BF16)

    @pl.when(slot < half)
    def _():
        keep_ref[pl.ds(pl.multiple_of(slot * part + inner, 16), size), cols] = value

    @pl.when(slot >= half)
    def _():
        send_ref[pl.ds(pl.multiple_of((slot - half) * part + inner, 16), size), cols] = value


def outer_kernel(base, rows):
    def kernel(info_ref, la, lb, ra, rb, keep_ref, send_ref):
        def step(d, carry):
            at = pl.ds(pl.multiple_of(d * 2 * rows, 128), 2 * rows)
            value = tn(la[:, at], ra[...]) + tn(lb[:, at], rb[...])
            for y in range(2):
                place(
                    info_ref, base, 2 * d + y, rows, 0, rows, value[y * rows : (y + 1) * rows], keep_ref, send_ref
                )
            return carry

        lax.fori_loop(0, la.shape[1] // (2 * rows), step, 0)

    return kernel


def inner_kernel(base, rows):
    def kernel(info_ref, la, lb, ra, rb, keep_ref, send_ref):
        def step(j, carry):
            at = pl.ds(pl.multiple_of(j * TILE, TILE), TILE)
            value = tn(la[...], ra[:, at]) + tn(lb[...], rb[:, at])
            for c in range(la.shape[1] // rows):
                place(
                    info_ref, base, c, rows, 0, rows, value[c * rows : (c + 1) * rows], keep_ref, send_ref, at
                )
            return carry

        lax.fori_loop(0, ra.shape[1] // TILE, step, 0)

    return kernel


def fill_table(info_ref, table_ref, s0m, s0o, s1, s2, si):
    width, half = table_ref.shape[1], s0m.shape[1]
    core = info_ref[CORE]
    table_ref[...] = jnp.zeros_like(table_ref)
    table_ref[0:3, pl.ds(pl.multiple_of(core * half, half), half)] = s0m[...]
    table_ref[0:3, pl.ds(pl.multiple_of((1 - core) * half, half), half)] = s0o[...]
    table_ref[3:6] = s1[...]
    table_ref[6:9] = s2[...]
    for i in range(si.shape[1] // width):
        table_ref[9 + i : 10 + i] = si[:, i * width : (i + 1) * width]


def rest_kernel(base, rows):
    def kernel(
        info_ref, xa, xb, ca, cb, ga, gb, oa, ob, s0m, s0o, s1, s2, si, keep_ref, send_ref, table_ref
    ):
        part = 4 * rows
        half = s0m.shape[1]
        for i in range(4):
            la, lb, ra, rb = (xa, xb, ga.at[i], gb.at[i]) if i < 3 else (ca, cb, oa, ob)
            value = tn(la[...], ra[...]) + tn(lb[...], rb[...])
            for c in range(xa.shape[1] // rows):
                place(
                    info_ref, base, c, part, i * rows, rows, value[c * rows : (c + 1) * rows], keep_ref, send_ref
                )
        fill_table(info_ref, table_ref, s0m, s0o, s1, s2, si)
        at = keep_ref.shape[0]
        for i in range(2):
            send_ref[at + i * TABLE : at + (i + 1) * TABLE] = table_ref[:, i * half : (i + 1) * half].astype(BF16)

    return kernel


def stage_kernel(low, high, out_dtype, tables):
    def kernel(info_ref, *refs):
        ins, out_ref = refs[:-1], refs[-1]
        if tables:
            sent_ref, ins = ins[-1], ins[:-1]
        value = ins[0][low:high].astype(F32)
        for ref in ins[1:]:
            value = value + ref[low:high].astype(F32)
        out_ref[0 : high - low] = value.astype(out_dtype)
        if tables:
            rows = sent_ref.shape[0]
            value = sent_ref[rows - 2 * TABLE :].astype(F32) + ins[-1][rows - 2 * TABLE :].astype(F32)
            out_ref[high - low :] = value.astype(out_dtype)

    return kernel


def swap(value, axis, size, bit):
    return lax.ppermute(value, axis, [(i, i ^ bit) for i in range(size)])


def make_body(sizes):
    size, dp = sizes["seq"], sizes["dp"]
    nbits = dp.bit_length()
    chunks = 2 * dp
    rest_bits = list(range(3, nbits))
    orders = {
        "outer": ([0, 1, 2, *rest_bits], [1, 0, 2, *rest_bits]),
        "inner": ([2, 1, 0, *rest_bits], [2, 0, 1, *rest_bits]),
        "rest": ([1, 2, 0, *rest_bits], [2, 1, 0, *rest_bits]),
    }
    bases = {name: SLOTS + i * chunks for i, name in enumerate(orders)}

    def my_bit(axis, bit):
        return (lax.axis_index(axis) & bit) // bit

    def pair(value):
        return swap(value, "seq", size, 1)

    def exchange(value, bits):
        moves = []
        for d in range(dp):
            for s in range(size):
                bit = bits[s % 2]
                to = (d, s ^ 2) if bit == 0 else (d ^ (1 << (bit - 1)), s)
                moves.append((d * size + s, to[0] * size + to[1]))
        return lax.ppermute(value, ("dp", "seq"), moves)

    def slot_table(me, core, order):
        rel = jnp.arange(chunks, dtype=jnp.int32) ^ me
        slots = [
            sum(((rel >> bit) & 1) << (nbits - 1 - s) for s, bit in enumerate(bits)) for bits in order
        ]
        return jnp.where(core == 0, slots[0], slots[1])

    def halving(info, keep, send, order, part, name, tables=False, after={}):
        got, n = [], chunks // 2
        for s in range(nbits):
            bits = (order[0][s], order[1][s])
            got.append(exchange(send, bits))
            ins = [keep, *got] + ([send] if tables else [])
            last = s == nbits - 1
            low, high = (0, part) if last else (n // 2 * part, n * part)
            extra = 2 * TABLE if tables else 0
            shape = like((high - low + extra, keep.shape[1]))
            send = call(
                stage_kernel(low, high, BF16, tables),
                f"{name}{s}", info, ins, shape, 1, after=after.get(s, ()),
            )
            n //= 2
        return send

    def spread(value, bit):
        other = swap(value, "seq", size, bit)
        first = my_bit("seq", bit) == 0
        return jnp.where(first, value, other), jnp.where(first, other, value)

    def plain_halving(value, order, me, core):
        slots = slot_table(me, core, order)
        kept = [jnp.zeros_like(value).at[slots].set(value)]
        n = chunks
        for s in range(nbits):
            n //= 2
            send = sum(v[n : 2 * n].astype(F32) for v in kept).astype(BF16)
            kept.append(exchange(send, (order[0][s], order[1][s])))
        return sum(v[0].astype(F32) for v in kept).astype(BF16)

    def body(
        inputs,
        cotangent,
        masked,
        w_query,
        b_query,
        w_key,
        w_value,
        b_value,
        w_output,
        b_output,
        attn_gain,
        attn_shift,
        w_inner,
        b_inner,
        w_outer,
        b_outer,
        ffn_gain,
        ffn_shift,
    ):
        shape = inputs.shape
        count, block, width = shape
        rows, wide, half = count * block, w_inner.shape[1], width // 2
        assert count == size == 4
        seq = lax.axis_index("seq")
        core, ybit = my_bit("seq", 1), my_bit("seq", 2)
        me = lax.axis_index("dp") * 2 + ybit
        info = jnp.concatenate(
            [jnp.stack([core, ybit])] + [slot_table(me, core, order) for order in orders.values()]
        ).astype(jnp.int32)
        row = lambda v: v.reshape(1, -1)
        full = like((rows, width))

        def gather(value):
            parts = [lax.dynamic_index_in_dim(value, seq ^ k, 0, keepdims=False) for k in range(size)]
            return [swap(v, "seq", size, k) if k else v for k, v in enumerate(parts)]

        def scatter(value):
            parts = value.reshape(size, block, width)
            got = jnp.stack([parts[0]] + [swap(parts[k], "seq", size, k) for k in range(1, size)])
            return jnp.stack([lax.dynamic_index_in_dim(got, seq ^ j, 0, keepdims=False) for j in range(size)])

        x_parts = gather(inputs)
        cot = jnp.concatenate(gather(cotangent * masked[:, :, None].astype(BF16)))
        x, q, k, v, p, ctx, n1, r1, low1 = call(
            attention_kernel, "attention", info,
            [*x_parts, w_query, w_key, w_value, w_output, row(b_query), row(b_value), row(b_output),
             row(attn_gain), row(attn_shift)],
            (full, full, full, full, like((width // HD, rows, rows)), full, like((rows, width), F32),
             like((rows, 1), F32), full),
            15, 32,
        )
        x_other, ctx_other, low_other = pair(x), pair(ctx), pair(low1)
        act, slope = call(
            hidden_kernel, "hidden", info, [low1, w_inner, row(b_inner)],
            (like((rows, wide)), like((rows, wide))), 9,
        )
        act_other = pair(act)
        out, mid, gb, gb_mine, gb_send, sums2 = call(
            branch_kernel, "branch", info,
            [act, w_outer, row(b_outer), n1, row(attn_gain), row(attn_shift), row(ffn_gain), row(ffn_shift), cot],
            (full, like((rows, width), F32), full, like((rows, half)), like((rows, half)), like((3, width), F32)),
            4,
        )
        gb_other = pair(gb_send)
        gh_mine, gh_send, sum_inner = call(
            hidden_back_kernel, "hidden_back", info, [gb, w_outer, slope],
            (like((rows, wide // 2)), like((rows, wide // 2)), like((1, wide), F32)), 8,
        )
        gh_other = pair(gh_send)
        outputs = scatter(out)

        part_o, part_i = wide // dp // 2, width // dp // 2
        fast = part_i % 16 == 0 and (2 * part_o) % 128 == 0

        def buffers(part, columns, extra=0):
            return like((dp * part, columns)), like((dp * part + extra, columns))

        def product(a, b):
            return (tn(a[0], b[0]) + tn(a[1], b[1])).astype(BF16)

        if fast:
            keep_o, send_o = call(
                outer_kernel(bases["outer"], part_o), "grad_outer", info, [act, act_other, gb_mine, gb_other],
                buffers(part_o, half), 7,
            )
            keep_i, send_i = call(
                inner_kernel(bases["inner"], part_i), "grad_inner", info, [low1, low_other, gh_mine, gh_other],
                buffers(part_i, wide // 2), 5, after=[send_o],
            )
            behind = [send_i]
        else:
            behind = []
        gsum, gctx, ga_mine, ga_send, sums1 = call(
            first_back_kernel, "first_back", info,
            [gh_mine, gh_send, w_inner, mid, n1, r1, row(attn_gain), w_output],
            (like((rows, width), F32), full, like((rows, half)), like((rows, half)), like((3, width), F32)),
            6, after=behind,
        )
        ga_other = pair(ga_send)
        three = (like((3, rows, half)), like((3, half), F32))
        g3_send, sums0_other = call(
            attention_back_kernel(True), "attention_back_other", info, [q, k, v, p, gctx], three, 6
        )
        g3_other = pair(g3_send)
        g3_mine, sums0_mine = call(
            attention_back_kernel(False), "attention_back_mine", info, [q, k, v, p, gctx], three, 6,
            after=[sums0_other],
        )
        sums = [sums0_mine, sums0_other, sums1, sums2, sum_inner]
        if fast:
            keep_r, send_r, table = call(
                rest_kernel(bases["rest"], part_i), "grad_rest", info,
                [x, x_other, ctx, ctx_other, g3_mine, g3_other, ga_mine, ga_other, *sums],
                (*buffers(4 * part_i, half, 2 * TABLE), like((TABLE, width), F32)), 6,
            )
        grad_x = call(
            input_back_kernel, "input_back", info, [g3_mine, g3_send, w_query, w_key, w_value, gsum], full, 2,
            after=[table] if fast else [],
        )
        grad_inputs = scatter(grad_x)

        def finish(value, group, part, columns):
            value = jnp.stack(spread(value.reshape(group, part, columns // 2), 2), axis=1)
            value = value.reshape(group, 2 * part, columns // 2)
            return jnp.concatenate(spread(value, 1), axis=-1).astype(F32)

        if fast:
            own_o = halving(info, keep_o, send_o, orders["outer"], part_o, "outer")
            own_i = halving(info, keep_i, send_i, orders["inner"], part_i, "inner")
            own_r = halving(info, keep_r, send_r, orders["rest"], 4 * part_i, "rest", True)
            own_r, table = own_r[: 4 * part_i], own_r[4 * part_i :]
            table = table.astype(F32) + pair(table).astype(F32)
            table = jnp.concatenate([table[:TABLE], table[TABLE:]], axis=1)
        else:
            me_core = (me, core)

            def cut(value, part):
                return value.reshape(chunks, part, value.shape[1])

            own_o = plain_halving(
                cut(product((act, act_other), (gb_mine, gb_other)), part_o), orders["outer"], *me_core
            )
            own_i = plain_halving(
                cut(product((low1, low_other), (gh_mine, gh_other)), part_i), orders["inner"], *me_core
            )
            four = [product((x, x_other), (g3_mine[i], g3_other[i])) for i in range(3)]
            four.append(product((ctx, ctx_other), (ga_mine, ga_other)))
            four = jnp.stack([cut(f, part_i) for f in four], axis=1)
            own_r = plain_halving(four, orders["rest"], *me_core)
            first = jnp.where(core == 0, sums0_mine, sums0_other)
            second = jnp.where(core == 0, sums0_other, sums0_mine)
            table = jnp.concatenate(
                [jnp.concatenate([first, second], axis=1), sums1, sums2, sum_inner.reshape(-1, width)]
            )
            table = lax.psum(table, ("dp", "seq"))
        (g_outer,) = finish(own_o, 1, part_o, width)
        (g_inner,) = finish(own_i, 1, part_i, wide)
        g_query, g_key, g_value, g_output = finish(own_r, 4, part_i, width)
        index = lax.axis_index("dp")

        def own(lines):
            flat = lines.reshape(-1)
            return lax.dynamic_slice_in_dim(flat, index * (flat.shape[0] // dp), flat.shape[0] // dp)

        return (
            outputs,
            grad_inputs,
            g_query,
            own(table[0]),
            g_key,
            g_value,
            own(table[2]),
            g_output,
            own(table[5]),
            own(table[3]),
            own(table[4]),
            g_inner,
            own(table[9 : 9 + wide // width]),
            g_outer,
            own(table[8]),
            own(table[6]),
            own(table[7]),
        )

    return body


def solution(mesh):
    rows = P("dp", "seq", None)
    matrix, vector = P("dp", None), P("dp")
    in_specs = (rows, rows, P("dp", "seq"), *[P()] * 15)
    out_specs = (
        rows,
        rows,
        matrix,
        vector,
        matrix,
        matrix,
        vector,
        matrix,
        vector,
        vector,
        vector,
        matrix,
        vector,
        matrix,
        vector,
        vector,
        vector,
    )
    body = make_body(dict(mesh.shape))
    return jax.shard_map(
        body, mesh=mesh, in_specs=in_specs, out_specs=out_specs, check_vma=False
    )
```

```python
import jax
import jax.numpy as jnp
from jax import lax
from jax.experimental import pallas as pl
from jax.experimental.pallas import tpu as pltpu
from jax.sharding import PartitionSpec as P

HD = 64
PAIR = 2 * HD
TILE = 256
EPSILON = 1e-05
F32, BF16 = jnp.float32, jnp.bfloat16
CORE, SEQ, DP, SLOTS = 0, 1, 2, 3
TABLE = 16
SCALE = 3e9
ORDER = (
    "ho", "hm", "go", "co", "gi", "fb", "ao", "o", "am", "o", "gr", "i", "r", "ib", "i", "o", "r",
    "i", "o", "ci", "r", "fo", "i", "r", "fi", "fr",
)
OUTER, INNER, REST = ((0, 1, 2), (1, 0, 2)), ((2, 0, 1), (1, 2, 0)), ((0, 1, 2), (1, 0, 2))


def nn(a, b):
    return lax.dot_general(a, b, (((1,), (0,)), ((), ())), preferred_element_type=F32)


def nt(a, b):
    return lax.dot_general(a, b, (((1,), (1,)), ((), ())), preferred_element_type=F32)


def tn(a, b):
    return lax.dot_general(a, b, (((0,), (0,)), ((), ())), preferred_element_type=F32)


def like(shape, dtype=BF16):
    return jax.ShapeDtypeStruct(shape, dtype)


def call(kernel, name, info, ins, outs, us, mb=14, after=(), hbm=0, scratch=()):
    n, skip = len(ins), len(after)

    def run(info_ref, *refs):
        kernel(info_ref, *refs[:n], *refs[n + skip :])

    return pl.pallas_call(
        run,
        in_specs=[pl.BlockSpec(memory_space=pltpu.SMEM)]
        + [pl.BlockSpec(memory_space=pltpu.VMEM)] * (n - hbm)
        + [pl.BlockSpec(memory_space=pltpu.HBM)] * hbm
        + [pl.BlockSpec(memory_space=pl.ANY)] * skip,
        out_shape=outs,
        scratch_shapes=list(scratch),
        compiler_params=pltpu.CompilerParams(vmem_limit_bytes=mb * 1024 * 1024),
        cost_estimate=pl.CostEstimate(
            flops=int(us * SCALE), bytes_accessed=1, transcendentals=0
        ),
        name=name,
    )(info, *ins, *after)


def fetch(sources, targets, sems):
    copies = [pltpu.make_async_copy(a, b, sems.at[i]) for i, (a, b) in enumerate(zip(sources, targets))]
    for c in copies:
        c.start()
    return copies


def halves(value):
    lane = lax.broadcasted_iota(jnp.int32, value.shape, 1)
    zero = jnp.zeros_like(value)
    return jnp.where(lane < HD, value, zero), jnp.where(lane < HD, zero, value)


def standardize(v):
    mean = jnp.mean(v, axis=-1, keepdims=True)
    c = v - mean
    r = lax.rsqrt(jnp.mean(c * c, axis=-1, keepdims=True) + EPSILON)
    return c * r, r


def norm_back(e, n, r):
    return r * (e - jnp.mean(e, axis=-1, keepdims=True) - n * jnp.mean(e * n, axis=-1, keepdims=True))


def columns(width):
    return [slice(j, j + TILE) for j in range(0, width, TILE)]


def total(value):
    return jnp.sum(value, axis=0, keepdims=True)


def attention_kernel(
    info_ref, x0, x1, x2, x3, bq_ref, bv_ref, bo_ref, gain_ref, shift_ref, wq_hbm, wk_hbm, wv_hbm, wo_hbm,
    x_ref, q_ref, k_ref, v_ref, p_ref, ctx_ref, n_ref, r_ref, low_ref,
    wq_ref, wk_ref, wv_ref, wo_ref, sems,
):
    rows, width = x_ref.shape
    block = x0.shape[0]
    copies = fetch((wq_hbm, wk_hbm, wv_hbm, wo_hbm), (wq_ref, wk_ref, wv_ref, wo_ref), sems)
    for i, part in enumerate((x0, x1, x2, x3)):
        x_ref[i * block : (i + 1) * block, :] = part[...]
    x = x_ref[...]
    copies[0].wait()
    for at in columns(width):
        q = (nn(x, wq_ref[:, at]) + bq_ref[:, at].astype(F32)).astype(BF16)
        q_ref[:, at] = q * jnp.asarray(HD ** -0.5, BF16)
    copies[1].wait()
    for at in columns(width):
        k_ref[:, at] = nn(x, wk_ref[:, at]).astype(BF16)
    copies[2].wait()
    for at in columns(width):
        v_ref[:, at] = (nn(x, wv_ref[:, at]) + bv_ref[:, at].astype(F32)).astype(BF16)
    for p in range(width // PAIR):
        at = slice(p * PAIR, (p + 1) * PAIR)
        q, k, v = q_ref[:, at], k_ref[:, at], v_ref[:, at]
        vt = v.astype(F32).T.astype(BF16)
        out = []
        for i, kh in enumerate(halves(k)):
            s = nt(kh, q)
            e = jnp.exp(s - jnp.max(s, axis=0, keepdims=True))
            w = (e * (1.0 / total(e))).astype(BF16)
            p_ref[2 * p + i] = w
            out.append(nn(vt[i * HD : (i + 1) * HD], w))
        ctx_ref[:, at] = jnp.concatenate(out, axis=0).T.astype(BF16)
    copies[3].wait()
    v1 = jnp.concatenate([nn(ctx_ref[...], wo_ref[:, at]) for at in columns(width)], axis=1)
    v1 = x_ref[...].astype(F32) + (v1 + bo_ref[...].astype(F32))
    n, r = standardize(v1)
    n_ref[...] = n
    r_ref[...] = r
    low_ref[...] = (n * gain_ref[...].astype(F32) + shift_ref[...].astype(F32)).astype(BF16)


def hidden_kernel(info_ref, low_ref, w_ref, b_ref, act_ref, slope_ref):
    for at in columns(w_ref.shape[1]):
        h = nn(low_ref[...], w_ref[:, at]) + b_ref[:, at].astype(F32)
        z = h * 0.7071067811865476
        phi = 0.5 + 0.5 * lax.erf(z)
        bell = jnp.exp2(z * z * -1.4426950408889634)
        act_ref[:, at] = (h * phi).astype(BF16)
        slope_ref[:, at] = (phi + z * bell * 0.5641895835477563).astype(BF16)


def split_store(core, value, mine_ref, other_ref):
    half = value.shape[1] // 2
    mine_ref[...] = jnp.where(core == 0, value[:, :half], value[:, half:])
    other_ref[...] = jnp.where(core == 0, value[:, half:], value[:, :half])


def branch_kernel(
    info_ref, act_ref, w_ref, b_ref, n_ref, gain1_ref, shift1_ref, gain_ref, shift_ref, c0, c1, c2, c3,
    o0, o1, o2, o3, mid_ref, low_ref, mine_ref, other_ref, sums_ref,
):
    width = mid_ref.shape[1]
    normed = n_ref[...] * gain1_ref[...].astype(F32) + shift1_ref[...].astype(F32)
    branch = jnp.concatenate([nn(act_ref[...], w_ref[:, at]) for at in columns(width)], axis=1)
    n, r = standardize(normed + (branch + b_ref[...].astype(F32)))
    gain = gain_ref[...].astype(F32)
    out = (n * gain + shift_ref[...].astype(F32)).astype(BF16)
    for i, ref in enumerate((o0, o1, o2, o3)):
        ref[...] = out[i * ref.shape[0] : (i + 1) * ref.shape[0]]
    go = jnp.concatenate([c[...] for c in (c0, c1, c2, c3)]).astype(F32)
    mid = norm_back(go * gain, n, r)
    mid_ref[...] = mid
    low = mid.astype(BF16)
    low_ref[...] = low
    split_store(info_ref[CORE], low, mine_ref, other_ref)
    sums_ref[0:1] = total(go * n)
    sums_ref[1:2] = total(go)
    sums_ref[2:3] = total(low.astype(F32))


def hidden_back_kernel(flip):
    def kernel(info_ref, low_ref, w_ref, slope_ref, out_ref, sums_ref):
        half = out_ref.shape[1]
        core = info_ref[CORE]
        first = ((1 - core) if flip else core) * half
        for to in columns(half):
            at = pl.ds(pl.multiple_of(first + to.start, TILE), TILE)
            g = (nt(low_ref[...], w_ref[at, :]) * slope_ref[:, at].astype(F32)).astype(BF16)
            out_ref[:, to] = g
            sums_ref[:, to] = total(g.astype(F32))

    return kernel


def first_back_kernel(
    info_ref, gm_ref, go_ref, w_ref, mid_ref, n_ref, r_ref, gain_ref, wo_ref,
    sum_ref, gctx_ref, mine_ref, other_ref, sums_ref,
):
    width, half = mid_ref.shape[1], gm_ref.shape[1]
    core = info_ref[CORE]
    mine = pl.ds(pl.multiple_of(core * half, half), half)
    other = pl.ds(pl.multiple_of((1 - core) * half, half), half)
    gn = jnp.concatenate(
        [nt(gm_ref[...], w_ref[at, mine]) + nt(go_ref[...], w_ref[at, other]) for at in columns(width)], axis=1
    )
    gn = gn + mid_ref[...]
    n = n_ref[...]
    gs = norm_back(gn * gain_ref[...].astype(F32), n, r_ref[...])
    sum_ref[...] = gs
    low = gs.astype(BF16)
    split_store(core, low, mine_ref, other_ref)
    sums_ref[0:1] = total(gn * n)
    sums_ref[1:2] = total(gn)
    sums_ref[2:3] = total(low.astype(F32))
    for at in columns(width):
        gctx_ref[:, at] = nt(low, wo_ref[at, :]).astype(BF16)


def attention_back_kernel(flip):
    def kernel(info_ref, q_ref, k_ref, v_ref, p_ref, g_ref, out_ref, sums_ref):
        rows, width = q_ref.shape
        per = width // PAIR // 2
        core = info_ref[CORE]
        first = ((1 - core) if flip else core) * per

        for p in range(per):
            at = pl.ds(pl.multiple_of((first + p) * PAIR, PAIR), PAIR)
            to = slice(p * PAIR, (p + 1) * PAIR)
            q, k, v, g = q_ref[:, at], k_ref[:, at], v_ref[:, at], g_ref[:, at]
            kt = k.astype(F32).T.astype(BF16)
            gk = jnp.zeros((rows, PAIR), F32)
            gv = jnp.zeros((rows, PAIR), F32)
            gq = []
            for i, (qh, vh, gh) in enumerate(zip(halves(q), halves(v), halves(g))):
                w = p_ref[2 * (first + p) + i]
                w32 = w.astype(F32)
                prod = w32 * nt(vh, g)
                gs = (prod - w32 * total(prod)).astype(BF16)
                gk = gk + nn(gs, qh)
                gv = gv + nn(w, gh)
                gq.append(nn(kt[i * HD : (i + 1) * HD], gs))
            gq = jnp.concatenate(gq, axis=0).T * HD ** -0.5
            for i, value in enumerate((gq, gk, gv)):
                value = value.astype(BF16)
                out_ref[i, :, to] = value
                sums_ref[i : i + 1, to] = total(value.astype(F32))

    return kernel


def input_back_kernel(info_ref, gm_ref, go_ref, sum_ref, wq_hbm, wk_hbm, wv_hbm, o0, o1, o2, o3, wq_ref, wk_ref, wv_ref, sems):
    half = gm_ref.shape[2]
    copies = fetch((wq_hbm, wk_hbm, wv_hbm), (wq_ref, wk_ref, wv_ref), sems)
    core = info_ref[CORE]
    mine = pl.ds(pl.multiple_of(core * half, half), half)
    other = pl.ds(pl.multiple_of((1 - core) * half, half), half)
    tiles = columns(sum_ref.shape[1])
    values = [sum_ref[:, at] for at in tiles]
    for i, w in enumerate((wq_ref, wk_ref, wv_ref)):
        copies[i].wait()
        for j, at in enumerate(tiles):
            values[j] = values[j] + nt(gm_ref[i], w[at, mine]) + nt(go_ref[i], w[at, other])
    for value, at in zip(values, tiles):
        value = value.astype(BF16)
        for i, ref in enumerate((o0, o1, o2, o3)):
            ref[:, at] = value[i * ref.shape[0] : (i + 1) * ref.shape[0]]


def place(info_ref, base, rows, buf_ref, keep_ref, send_ref):
    slots = buf_ref.shape[0] // rows
    for slot in range(slots):
        chunk = buf_ref[pl.ds(pl.multiple_of(info_ref[base + slot] * rows, 16), rows), :]
        ref, to = (keep_ref, slot) if slot < slots // 2 else (send_ref, slot - slots // 2)
        ref[to * rows : (to + 1) * rows, :] = chunk


def outer_kernel(base, rows):
    def kernel(info_ref, la, lb, ra, rb, keep_ref, send_ref, buf_ref):
        for at in columns(la.shape[1]):
            buf_ref[at, :] = (tn(la[:, at], ra[...]) + tn(lb[:, at], rb[...])).astype(BF16)
        place(info_ref, base, rows, buf_ref, keep_ref, send_ref)

    return kernel


def inner_kernel(base, rows):
    def kernel(info_ref, la, lb, ra, rb, keep_ref, send_ref, buf_ref):
        for at in columns(ra.shape[1]):
            buf_ref[:, at] = (tn(la[...], ra[:, at]) + tn(lb[...], rb[:, at])).astype(BF16)
        place(info_ref, base, rows, buf_ref, keep_ref, send_ref)

    return kernel


def fill_table(info_ref, table_ref, s0m, s0o, s1, s2, sim, sio):
    half = s0m.shape[1]
    core = info_ref[CORE]
    own = pl.ds(pl.multiple_of(core * half, half), half)
    others = pl.ds(pl.multiple_of((1 - core) * half, half), half)
    table_ref[...] = jnp.zeros_like(table_ref)
    table_ref[0:3, own] = s0m[...]
    table_ref[0:3, others] = s0o[...]
    table_ref[3:6] = s1[...]
    table_ref[6:9] = s2[...]
    per = sim.shape[1] // half
    for part, which in ((sim, core), (sio, 1 - core)):
        for i in range(per):
            flat = which * per + i
            at = pl.ds(pl.multiple_of(lax.rem(flat, 2) * half, half), half)
            table_ref[pl.ds(9 + lax.div(flat, 2), 1), at] = part[:, i * half : (i + 1) * half]


def rest_kernel(base, rows):
    def kernel(
        info_ref, xa, xb, ca, cb, ga, gb, oa, ob, s0m, s0o, s1, s2, sim, sio, keep_ref, send_ref, table_ref, buf_ref
    ):
        half = s0m.shape[1]
        slots = xa.shape[1] // rows
        for i in range(4):
            la, lb, ra, rb = (xa, xb, ga.at[i], gb.at[i]) if i < 3 else (ca, cb, oa, ob)
            buf_ref[i] = (tn(la[...], ra[...]) + tn(lb[...], rb[...])).astype(BF16)
            for slot in range(slots):
                chunk = buf_ref[i, pl.ds(pl.multiple_of(info_ref[base + slot] * rows, 16), rows), :]
                ref, to = (keep_ref, slot) if slot < slots // 2 else (send_ref, slot - slots // 2)
                ref[(4 * to + i) * rows : (4 * to + i + 1) * rows, :] = chunk
        fill_table(info_ref, table_ref, s0m, s0o, s1, s2, sim, sio)
        at = keep_ref.shape[0]
        for i in range(2):
            send_ref[at + i * TABLE : at + (i + 1) * TABLE] = table_ref[:, i * half : (i + 1) * half].astype(BF16)

    return kernel


def stage_kernel(low, high, out_dtype, tables):
    def kernel(info_ref, *refs):
        ins, out_ref = refs[:-1], refs[-1]
        if tables:
            sent_ref, ins = ins[-1], ins[:-1]
        value = ins[0][low:high].astype(F32)
        for ref in ins[1:]:
            value = value + ref[low:high].astype(F32)
        out_ref[0 : high - low] = value.astype(out_dtype)
        if tables:
            rows = sent_ref.shape[0]
            value = sent_ref[rows - 2 * TABLE :].astype(F32) + ins[-1][rows - 2 * TABLE :].astype(F32)
            out_ref[high - low :] = value.astype(out_dtype)

    return kernel


def deal_kernel(info_ref, in_hbm, *refs):
    outs, sems = refs[:-1], refs[-1]
    for c in fetch([in_hbm.at[info_ref[SEQ] ^ k] for k in range(len(outs))], outs, sems):
        c.wait()


def collect_kernel(info_ref, *refs):
    for k, part in enumerate(refs[:-1]):
        refs[-1][info_ref[SEQ] ^ k] = part[...]


def finish_kernel(part, tables):
    def kernel(info_ref, *refs):
        quarters, outs = refs[:4], refs[4:]
        core, ybit = info_ref[CORE], info_ref[SEQ] // 2
        half = quarters[0].shape[1]
        if tables:
            outs, small_ref, wide_ref = outs[:-2], outs[-2], outs[-1]
        for i, ref in enumerate(quarters):
            row = pl.multiple_of((ybit ^ (i & 1)) * part, 8)
            column = pl.multiple_of((core ^ (i >> 1)) * half, 128)
            for j, out_ref in enumerate(outs):
                out_ref[pl.ds(row, part), pl.ds(column, half)] = ref[j * part : (j + 1) * part].astype(F32)
        if tables:
            at = len(outs) * part
            table = [
                quarters[0][at + i * TABLE : at + (i + 1) * TABLE].astype(F32)
                + quarters[2][at + i * TABLE : at + (i + 1) * TABLE].astype(F32)
                for i in range(2)
            ]
            d = info_ref[DP]
            lanes = 2 * half
            step = 2 * part
            rolled = pltpu.roll(jnp.concatenate(table, axis=1), lax.rem(lanes - d * step, lanes), 1)
            small_ref[...] = rolled[:, : small_ref.shape[1]]
            per = wide_ref.shape[1]
            count = lanes // per
            for row in range(TABLE - 9):
                for k in range(count):
                    line = jnp.concatenate([t[9 + row : 10 + row] for t in table], axis=1)

                    @pl.when(d == row * count + k)
                    def _():
                        wide_ref[...] = line[:, k * per : (k + 1) * per]

    return kernel


def swap(value, axis, size, bit):
    return lax.ppermute(value, axis, [(i, i ^ bit) for i in range(size)])


def make_body(sizes):
    size, dp = sizes["seq"], sizes["dp"]
    nbits = dp.bit_length()
    chunks = 2 * dp
    rest_bits = list(range(3, nbits))
    orders = {
        name: [[*bits, *rest_bits] for bits in order]
        for name, order in (("outer", OUTER), ("inner", INNER), ("rest", REST))
    }
    bases = {name: SLOTS + i * chunks for i, name in enumerate(orders)}

    def my_bit(axis, bit):
        return (lax.axis_index(axis) & bit) // bit

    def pair(value):
        return swap(value, "seq", size, 1)

    def exchange(value, bits):
        moves = []
        for d in range(dp):
            for s in range(size):
                bit = bits[s % 2]
                to = (d, s ^ 2) if bit == 0 else (d ^ (1 << (bit - 1)), s)
                moves.append((d * size + s, to[0] * size + to[1]))
        return lax.ppermute(value, ("dp", "seq"), moves)

    def chunk_table(me, core, order):
        slot = jnp.arange(chunks, dtype=jnp.int32)
        rel = [sum(((slot >> (nbits - 1 - s)) & 1) << bit for s, bit in enumerate(bits)) for bits in order]
        return jnp.where(core == 0, rel[0], rel[1]) ^ me

    class Halving:
        def __init__(self, info, keep, send, name, part, tables=False):
            self.info, self.keep, self.send, self.name, self.part = info, keep, send, name, part
            self.tables, self.got, self.left, self.stage = tables, [], chunks // 2, 0
            self.move()

        def move(self):
            first, second = orders[self.name]
            self.got.append(exchange(self.send, (first[self.stage], second[self.stage])))

        def step(self, *after):
            part, n = self.part, self.left
            last = self.stage == nbits - 1
            low, high = (0, part) if last else (n // 2 * part, n * part)
            ins = [self.keep, *self.got] + ([self.send] if self.tables else [])
            shape = like((high - low + (2 * TABLE if self.tables else 0), self.keep.shape[1]))
            self.send = call(
                stage_kernel(low, high, BF16, self.tables),
                f"{self.name}{self.stage}", self.info, ins, shape, 1, after=after,
            )
            self.left, self.stage = n // 2, self.stage + 1
            if not last:
                self.move()
            return self.send

    def spread(value, bit):
        other = swap(value, "seq", size, bit)
        first = my_bit("seq", bit) == 0
        return jnp.where(first, value, other), jnp.where(first, other, value)

    def plain_halving(value, order, me, core):
        kept = [jnp.take(value, chunk_table(me, core, order), axis=0)]
        n = chunks
        for s in range(nbits):
            n //= 2
            send = sum(v[n : 2 * n].astype(F32) for v in kept).astype(BF16)
            kept.append(exchange(send, (order[0][s], order[1][s])))
        return sum(v[0].astype(F32) for v in kept).astype(BF16)

    def body(
        inputs,
        cotangent,
        masked,
        w_query,
        b_query,
        w_key,
        w_value,
        b_value,
        w_output,
        b_output,
        attn_gain,
        attn_shift,
        w_inner,
        b_inner,
        w_outer,
        b_outer,
        ffn_gain,
        ffn_shift,
    ):
        shape = inputs.shape
        count, block, width = shape
        rows, wide, half = count * block, w_inner.shape[1], width // 2
        assert count == size == 4
        seq = lax.axis_index("seq")
        core, ybit = my_bit("seq", 1), my_bit("seq", 2)
        me = lax.axis_index("dp") * 2 + ybit
        info = jnp.concatenate(
            [jnp.stack([core, seq, lax.axis_index("dp")])] + [chunk_table(me, core, order) for order in orders.values()]
        ).astype(jnp.int32)
        row = lambda v: v.reshape(1, -1)
        full = like((rows, width))

        part_o, part_i = wide // dp // 2, width // dp // 2
        fast = nbits == 4 and part_i % 16 == 0 and (2 * part_o) % 128 == 0 and width % (2 * part_o) == 0
        blocks = [like((block, width))] * size

        def gather(value, name):
            parts = call(
                deal_kernel, name, info, [value], blocks, 1, hbm=1,
                scratch=[pltpu.SemaphoreType.DMA((size,))],
            )
            return [swap(v, "seq", size, k) if k else v for k, v in enumerate(parts)]

        def scatter(parts):
            return [parts[0]] + [swap(parts[k], "seq", size, k) for k in range(1, size)]

        def collect(parts, name, *after):
            return call(collect_kernel, name, info, parts, like(shape), 1, after=after)

        x_parts = gather(inputs, "deal_inputs")
        cot_parts = gather(cotangent * masked[:, :, None].astype(BF16), "deal_cotangent")
        square = pltpu.VMEM((width, width), BF16)
        x, q, k, v, p, ctx, n1, r1, low1 = call(
            attention_kernel, "attention", info,
            [*x_parts, row(b_query), row(b_value), row(b_output), row(attn_gain), row(attn_shift),
             w_query, w_key, w_value, w_output],
            (full, full, full, full, like((width // HD, rows, rows)), full, like((rows, width), F32),
             like((rows, 1), F32), full),
            13, 20, hbm=4, scratch=[square] * 4 + [pltpu.SemaphoreType.DMA((4,))],
        )
        x_other, ctx_other, low_other = pair(x), pair(ctx), pair(low1)
        act, slope = call(
            hidden_kernel, "hidden", info, [low1, w_inner, row(b_inner)],
            (like((rows, wide)), like((rows, wide))), 9, after=cot_parts,
        )
        act_other = pair(act)
        *out, mid, gb, gb_mine, gb_send, sums2 = call(
            branch_kernel, "branch", info,
            [act, w_outer, row(b_outer), n1, row(attn_gain), row(attn_shift), row(ffn_gain), row(ffn_shift),
             *cot_parts],
            (*blocks, like((rows, width), F32), full, like((rows, half)), like((rows, half)), like((3, width), F32)),
            4, 16,
        )
        gb_other = pair(gb_send)
        out = scatter(out)
        env, groups, token = {}, {}, []

        def buffers(part, columns, extra=0):
            return like((dp * part, columns)), like((dp * part + extra, columns))

        def product(a, b):
            return (tn(a[0], b[0]) + tn(a[1], b[1])).astype(BF16)

        def quarters(own):
            other = swap(own, "seq", size, 2)
            return [own, other, pair(own), pair(other)]

        def hidden_back(name, flip):
            shapes = (like((rows, wide // 2)), like((1, wide // 2), F32))
            env["gh_" + name], env["sumi_" + name] = call(
                hidden_back_kernel(flip), "hidden_back_" + name, info, [gb, w_outer, slope], shapes, 3,
                after=[*token, act_other] if flip else [*token, gb_other],
            )
            if flip:
                env["gh_pair"] = pair(env["gh_other"])
            return env["sumi_" + name]

        def grad_outer():
            keep, send = call(
                outer_kernel(bases["outer"], part_o), "grad_outer", info, [act, act_other, gb_mine, gb_other],
                buffers(part_o, half), 5, after=token, scratch=[pltpu.VMEM((wide, half), BF16)],
            )
            groups["o"] = Halving(info, keep, send, "outer", part_o)
            return send

        def grad_inner():
            keep, send = call(
                inner_kernel(bases["inner"], part_i), "grad_inner", info,
                [low1, low_other, env["gh_mine"], env["gh_pair"]], buffers(part_i, wide // 2), 4, after=token,
                scratch=[pltpu.VMEM((width, wide // 2), BF16)],
            )
            groups["i"] = Halving(info, keep, send, "inner", part_i)
            return send

        def first_back():
            env["gsum"], env["gctx"], env["ga"], ga_send, env["sums1"] = call(
                first_back_kernel, "first_back", info,
                [env["gh_mine"], env["gh_other"], w_inner, mid, n1, r1, row(attn_gain), w_output],
                (like((rows, width), F32), full, like((rows, half)), like((rows, half)), like((3, width), F32)),
                6, after=token,
            )
            env["ga_pair"] = pair(ga_send)
            return env["sums1"]

        def attention_back(name, flip):
            env["g3_" + name], env["sums0_" + name] = call(
                attention_back_kernel(flip), "attention_back_" + name, info, [q, k, v, p, env["gctx"]],
                (like((3, rows, half)), like((3, half), F32)), 1, after=token,
            )
            if flip:
                env["g3_pair"] = pair(env["g3_other"])
            return env["sums0_" + name]

        def grad_rest():
            sums = [env["sums0_mine"], env["sums0_other"], env["sums1"], sums2, env["sumi_mine"], env["sumi_other"]]
            keep, send, table = call(
                rest_kernel(bases["rest"], part_i), "grad_rest", info,
                [x, x_other, ctx, ctx_other, env["g3_mine"], env["g3_pair"], env["ga"], env["ga_pair"], *sums],
                (*buffers(4 * part_i, half, 2 * TABLE), like((TABLE, width), F32)), 1, after=token,
                scratch=[pltpu.VMEM((4, width, half), BF16)],
            )
            groups["r"] = Halving(info, keep, send, "rest", 4 * part_i, True)
            return table

        def input_back():
            parts = call(
                input_back_kernel, "input_back", info,
                [env["g3_mine"], env["g3_other"], env["gsum"], w_query, w_key, w_value], blocks, 2, after=token,
                hbm=3, mb=52, scratch=[square] * 3 + [pltpu.SemaphoreType.DMA((3,))],
            )
            env["back"] = scatter(parts)
            return parts[0]

        def step(name):
            own = groups[name].step(*token)
            if groups[name].stage == nbits:
                env["q" + name] = quarters(own)
            return own

        def finish_group(name, part, columns, title):
            env["g" + name] = call(
                finish_kernel(part, False), title, info, env["q" + name], like((2 * part, columns), F32), 1, after=token
            )
            return env["g" + name]

        def finish_rest():
            matrix, thin = like((2 * part_i, width), F32), like((TABLE, 128), F32)
            env["gr"] = call(
                finish_kernel(part_i, True), "finish_rest", info, env["qr"],
                (matrix, matrix, matrix, matrix, thin, like((1, 2 * part_o), F32)), 1, after=token,
            )
            return env["gr"][4]

        def collect(name, parts):
            env[name] = call(collect_kernel, "collect_" + name, info, parts, like(shape), 1, after=token)
            return env[name]

        tasks = {
            "ho": lambda: hidden_back("other", True),
            "hm": lambda: hidden_back("mine", False),
            "go": grad_outer,
            "gi": grad_inner,
            "fb": first_back,
            "ao": lambda: attention_back("other", True),
            "am": lambda: attention_back("mine", False),
            "gr": grad_rest,
            "ib": input_back,
            "o": lambda: step("o"),
            "i": lambda: step("i"),
            "r": lambda: step("r"),
            "fo": lambda: finish_group("o", part_o, width, "finish_outer"),
            "fi": lambda: finish_group("i", part_i, wide, "finish_inner"),
            "fr": finish_rest,
            "co": lambda: collect("outputs", out),
            "ci": lambda: collect("inputs", env["back"]),
        }
        for name in ORDER:
            if fast or name in ("ho", "hm", "fb", "ao", "am", "ib", "co", "ci"):
                token = [tasks[name]()]

        def finish(value, group, part, columns):
            value = jnp.stack(spread(value.reshape(group, part, columns // 2), 2), axis=1)
            value = value.reshape(group, 2 * part, columns // 2)
            return jnp.concatenate(spread(value, 1), axis=-1).astype(F32)

        if fast:
            g_outer, g_inner = env["go"], env["gi"]
            g_query, g_key, g_value, g_output, small, wide_row = env["gr"]
            small = [small[i, : 2 * part_i] for i in range(9)] + [wide_row[0]]
        else:
            me_core = (me, core)

            def cut(value, part):
                return value.reshape(chunks, part, value.shape[1])

            own_o = plain_halving(
                cut(product((act, act_other), (gb_mine, gb_other)), part_o), orders["outer"], *me_core
            )
            own_i = plain_halving(
                cut(product((low1, low_other), (env["gh_mine"], env["gh_pair"])), part_i), orders["inner"], *me_core
            )
            four = [product((x, x_other), (env["g3_mine"][i], env["g3_pair"][i])) for i in range(3)]
            four.append(product((ctx, ctx_other), (env["ga"], env["ga_pair"])))
            four = jnp.stack([cut(f, part_i) for f in four], axis=1)
            own_r = plain_halving(four, orders["rest"], *me_core)

            def both(mine, other):
                return jnp.where(
                    core == 0,
                    jnp.concatenate([mine, other], axis=1),
                    jnp.concatenate([other, mine], axis=1),
                )

            table = jnp.concatenate(
                [
                    both(env["sums0_mine"], env["sums0_other"]),
                    env["sums1"],
                    sums2,
                    both(env["sumi_mine"], env["sumi_other"]).reshape(-1, width),
                ]
            )
            table = lax.psum(table, ("dp", "seq"))
            (g_outer,) = finish(own_o, 1, part_o, width)
            (g_inner,) = finish(own_i, 1, part_i, wide)
            g_query, g_key, g_value, g_output = finish(own_r, 4, part_i, width)
            lines = [table[i] for i in range(9)] + [table[9:].reshape(-1)]
            small = []
            for line in lines:
                n = line.shape[0] // dp
                small.append(lax.dynamic_slice_in_dim(line, lax.axis_index("dp") * n, n))
        return (
            env["outputs"],
            env["inputs"],
            g_query,
            small[0],
            g_key,
            g_value,
            small[2],
            g_output,
            small[5],
            small[3],
            small[4],
            g_inner,
            small[9],
            g_outer,
            small[8],
            small[6],
            small[7],
        )

    return body


def solution(mesh):
    rows = P("dp", "seq", None)
    matrix, vector = P("dp", None), P("dp")
    in_specs = (rows, rows, P("dp", "seq"), *[P()] * 15)
    out_specs = (
        rows,
        rows,
        matrix,
        vector,
        matrix,
        matrix,
        vector,
        matrix,
        vector,
        vector,
        vector,
        matrix,
        vector,
        matrix,
        vector,
        vector,
        vector,
    )
    body = make_body(dict(mesh.shape))
    return jax.shard_map(
        body, mesh=mesh, in_specs=in_specs, out_specs=out_specs, check_vma=False
    )
```

```python
import jax
import jax.numpy as jnp
from jax import lax
from jax.experimental import pallas as pl
from jax.experimental.pallas import tpu as pltpu
from jax.sharding import PartitionSpec as P

HD = 64
PAIR = 2 * HD
TILE = 256
EPSILON = 1e-05
F32, BF16 = jnp.float32, jnp.bfloat16
CORE, SEQ, DP, SLOTS = 0, 1, 2, 3
TABLE = 16
SCALE = 3e9
ORDER = (
    "ho", "hm", "go", "co", "gi", "fb", "ao", "o", "am", "o", "gr", "i", "r", "ib", "i", "o", "r",
    "i", "o", "ci", "r", "fo", "i", "r", "fi", "fr",
)
OUTER, INNER, REST = ((0, 1, 2), (1, 0, 2)), ((2, 0, 1), (1, 2, 0)), ((0, 1, 2), (1, 0, 2))


def nn(a, b):
    return lax.dot_general(a, b, (((1,), (0,)), ((), ())), preferred_element_type=F32)


def nt(a, b):
    return lax.dot_general(a, b, (((1,), (1,)), ((), ())), preferred_element_type=F32)


def tn(a, b):
    return lax.dot_general(a, b, (((0,), (0,)), ((), ())), preferred_element_type=F32)


def like(shape, dtype=BF16):
    return jax.ShapeDtypeStruct(shape, dtype)


def call(kernel, name, info, ins, outs, us, mb=14, after=(), hbm=0, scratch=()):
    n, skip = len(ins), len(after)

    def run(info_ref, *refs):
        kernel(info_ref, *refs[:n], *refs[n + skip :])

    return pl.pallas_call(
        run,
        in_specs=[pl.BlockSpec(memory_space=pltpu.SMEM)]
        + [pl.BlockSpec(memory_space=pltpu.VMEM)] * (n - hbm)
        + [pl.BlockSpec(memory_space=pltpu.HBM)] * hbm
        + [pl.BlockSpec(memory_space=pl.ANY)] * skip,
        out_shape=outs,
        scratch_shapes=list(scratch),
        compiler_params=pltpu.CompilerParams(vmem_limit_bytes=mb * 1024 * 1024),
        cost_estimate=pl.CostEstimate(
            flops=int(us * SCALE), bytes_accessed=1, transcendentals=0
        ),
        name=name,
    )(info, *ins, *after)


def fetch(sources, targets, sems):
    copies = [pltpu.make_async_copy(a, b, sems.at[i]) for i, (a, b) in enumerate(zip(sources, targets))]
    for c in copies:
        c.start()
    return copies


def halves(value):
    lane = lax.broadcasted_iota(jnp.int32, value.shape, 1)
    zero = jnp.zeros_like(value)
    return jnp.where(lane < HD, value, zero), jnp.where(lane < HD, zero, value)


def standardize(v):
    mean = jnp.mean(v, axis=-1, keepdims=True)
    c = v - mean
    r = lax.rsqrt(jnp.mean(c * c, axis=-1, keepdims=True) + EPSILON)
    return c * r, r


def norm_back(e, n, r):
    return r * (e - jnp.mean(e, axis=-1, keepdims=True) - n * jnp.mean(e * n, axis=-1, keepdims=True))


def columns(width):
    return [slice(j, j + TILE) for j in range(0, width, TILE)]


def tiles_loop(width, each, body):
    def step(i, carry):
        for j in range(each):
            body(pl.ds(pl.multiple_of((i * each + j) * TILE, TILE), TILE))
        return carry

    lax.fori_loop(0, width // (TILE * each), step, 0)


def total(value):
    return jnp.sum(value, axis=0, keepdims=True)


def attention_kernel(
    info_ref, x0, x1, x2, x3, bq_ref, bv_ref, bo_ref, gain_ref, shift_ref, wq_hbm, wk_hbm, wv_hbm, wo_hbm,
    x_ref, q_ref, k_ref, v_ref, p_ref, ctx_ref, n_ref, r_ref, low_ref,
    wq_ref, wk_ref, wv_ref, wo_ref, sems,
):
    rows, width = x_ref.shape
    block = x0.shape[0]
    copies = fetch((wq_hbm, wk_hbm, wv_hbm, wo_hbm), (wq_ref, wk_ref, wv_ref, wo_ref), sems)
    for i, part in enumerate((x0, x1, x2, x3)):
        x_ref[i * block : (i + 1) * block, :] = part[...]
    x = x_ref[...]
    copies[0].wait()
    for at in columns(width):
        q = (nn(x, wq_ref[:, at]) + bq_ref[:, at].astype(F32)).astype(BF16)
        q_ref[:, at] = q * jnp.asarray(HD ** -0.5, BF16)
    copies[1].wait()
    for at in columns(width):
        k_ref[:, at] = nn(x, wk_ref[:, at]).astype(BF16)
    copies[2].wait()
    for at in columns(width):
        v_ref[:, at] = (nn(x, wv_ref[:, at]) + bv_ref[:, at].astype(F32)).astype(BF16)
    def pair(p, carry):
        at = pl.ds(pl.multiple_of(p * PAIR, PAIR), PAIR)
        q, k, v = q_ref[:, at], k_ref[:, at], v_ref[:, at]
        vt = v.astype(F32).T.astype(BF16)
        out = []
        for i, kh in enumerate(halves(k)):
            s = nt(kh, q)
            e = jnp.exp(s - jnp.max(s, axis=0, keepdims=True))
            w = (e * (1.0 / total(e))).astype(BF16)
            p_ref[2 * p + i] = w
            out.append(nn(vt[i * HD : (i + 1) * HD], w))
        ctx_ref[:, at] = jnp.concatenate(out, axis=0).T.astype(BF16)
        return carry

    lax.fori_loop(0, width // PAIR, pair, 0)
    copies[3].wait()
    v1 = jnp.concatenate([nn(ctx_ref[...], wo_ref[:, at]) for at in columns(width)], axis=1)
    v1 = x_ref[...].astype(F32) + (v1 + bo_ref[...].astype(F32))
    n, r = standardize(v1)
    n_ref[...] = n
    r_ref[...] = r
    low_ref[...] = (n * gain_ref[...].astype(F32) + shift_ref[...].astype(F32)).astype(BF16)


def hidden_kernel(info_ref, low_ref, w_ref, b_ref, act_ref, slope_ref):
    def tile(at):
        h = nn(low_ref[...], w_ref[:, at]) + b_ref[:, at].astype(F32)
        z = h * 0.7071067811865476
        phi = 0.5 + 0.5 * lax.erf(z)
        bell = jnp.exp2(z * z * -1.4426950408889634)
        act_ref[:, at] = (h * phi).astype(BF16)
        slope_ref[:, at] = (phi + z * bell * 0.5641895835477563).astype(BF16)

    tiles_loop(w_ref.shape[1], 3, tile)


def split_store(core, value, mine_ref, other_ref):
    half = value.shape[1] // 2
    mine_ref[...] = jnp.where(core == 0, value[:, :half], value[:, half:])
    other_ref[...] = jnp.where(core == 0, value[:, half:], value[:, :half])


def branch_kernel(
    info_ref, act_ref, w_ref, b_ref, n_ref, gain1_ref, shift1_ref, gain_ref, shift_ref, c0, c1, c2, c3,
    o0, o1, o2, o3, mid_ref, low_ref, mine_ref, other_ref, sums_ref,
):
    width = mid_ref.shape[1]
    normed = n_ref[...] * gain1_ref[...].astype(F32) + shift1_ref[...].astype(F32)
    branch = jnp.concatenate([nn(act_ref[...], w_ref[:, at]) for at in columns(width)], axis=1)
    n, r = standardize(normed + (branch + b_ref[...].astype(F32)))
    gain = gain_ref[...].astype(F32)
    out = (n * gain + shift_ref[...].astype(F32)).astype(BF16)
    for i, ref in enumerate((o0, o1, o2, o3)):
        ref[...] = out[i * ref.shape[0] : (i + 1) * ref.shape[0]]
    go = jnp.concatenate([c[...] for c in (c0, c1, c2, c3)]).astype(F32)
    mid = norm_back(go * gain, n, r)
    mid_ref[...] = mid
    low = mid.astype(BF16)
    low_ref[...] = low
    split_store(info_ref[CORE], low, mine_ref, other_ref)
    sums_ref[0:1] = total(go * n)
    sums_ref[1:2] = total(go)
    sums_ref[2:3] = total(low.astype(F32))


def hidden_back_kernel(flip):
    def kernel(info_ref, low_ref, w_ref, slope_ref, out_ref, sums_ref):
        half = out_ref.shape[1]
        core = info_ref[CORE]
        first = ((1 - core) if flip else core) * half
        for to in columns(half):
            at = pl.ds(pl.multiple_of(first + to.start, TILE), TILE)
            g = (nt(low_ref[...], w_ref[at, :]) * slope_ref[:, at].astype(F32)).astype(BF16)
            out_ref[:, to] = g
            sums_ref[:, to] = total(g.astype(F32))

    return kernel


def first_back_kernel(
    info_ref, gm_ref, go_ref, w_ref, mid_ref, n_ref, r_ref, gain_ref, wo_ref,
    sum_ref, gctx_ref, mine_ref, other_ref, sums_ref,
):
    width, half = mid_ref.shape[1], gm_ref.shape[1]
    core = info_ref[CORE]
    mine = pl.ds(pl.multiple_of(core * half, half), half)
    other = pl.ds(pl.multiple_of((1 - core) * half, half), half)
    gn = jnp.concatenate(
        [nt(gm_ref[...], w_ref[at, mine]) + nt(go_ref[...], w_ref[at, other]) for at in columns(width)], axis=1
    )
    gn = gn + mid_ref[...]
    n = n_ref[...]
    gs = norm_back(gn * gain_ref[...].astype(F32), n, r_ref[...])
    sum_ref[...] = gs
    low = gs.astype(BF16)
    split_store(core, low, mine_ref, other_ref)
    sums_ref[0:1] = total(gn * n)
    sums_ref[1:2] = total(gn)
    sums_ref[2:3] = total(low.astype(F32))
    for at in columns(width):
        gctx_ref[:, at] = nt(low, wo_ref[at, :]).astype(BF16)


def attention_back_kernel(flip):
    def kernel(info_ref, q_ref, k_ref, v_ref, p_ref, g_ref, out_ref, sums_ref):
        rows, width = q_ref.shape
        per = width // PAIR // 2
        core = info_ref[CORE]
        first = ((1 - core) if flip else core) * per

        def pair(p, carry):
            at = pl.ds(pl.multiple_of((first + p) * PAIR, PAIR), PAIR)
            to = pl.ds(pl.multiple_of(p * PAIR, PAIR), PAIR)
            q, k, v, g = q_ref[:, at], k_ref[:, at], v_ref[:, at], g_ref[:, at]
            kt = k.astype(F32).T.astype(BF16)
            gk = jnp.zeros((rows, PAIR), F32)
            gv = jnp.zeros((rows, PAIR), F32)
            gq = []
            for i, (qh, vh, gh) in enumerate(zip(halves(q), halves(v), halves(g))):
                w = p_ref[2 * (first + p) + i]
                w32 = w.astype(F32)
                prod = w32 * nt(vh, g)
                gs = (prod - w32 * total(prod)).astype(BF16)
                gk = gk + nn(gs, qh)
                gv = gv + nn(w, gh)
                gq.append(nn(kt[i * HD : (i + 1) * HD], gs))
            gq = jnp.concatenate(gq, axis=0).T * HD ** -0.5
            for i, value in enumerate((gq, gk, gv)):
                value = value.astype(BF16)
                out_ref[i, :, to] = value
                sums_ref[i : i + 1, to] = total(value.astype(F32))
            return carry

        lax.fori_loop(0, per, pair, 0)

    return kernel


def input_back_kernel(info_ref, gm_ref, go_ref, sum_ref, wq_hbm, wk_hbm, wv_hbm, o0, o1, o2, o3, wq_ref, wk_ref, wv_ref, sems):
    half = gm_ref.shape[2]
    copies = fetch((wq_hbm, wk_hbm, wv_hbm), (wq_ref, wk_ref, wv_ref), sems)
    core = info_ref[CORE]
    mine = pl.ds(pl.multiple_of(core * half, half), half)
    other = pl.ds(pl.multiple_of((1 - core) * half, half), half)
    tiles = columns(sum_ref.shape[1])
    values = [sum_ref[:, at] for at in tiles]
    for i, w in enumerate((wq_ref, wk_ref, wv_ref)):
        copies[i].wait()
        for j, at in enumerate(tiles):
            values[j] = values[j] + nt(gm_ref[i], w[at, mine]) + nt(go_ref[i], w[at, other])
    for value, at in zip(values, tiles):
        value = value.astype(BF16)
        for i, ref in enumerate((o0, o1, o2, o3)):
            ref[:, at] = value[i * ref.shape[0] : (i + 1) * ref.shape[0]]


def place(info_ref, base, rows, buf_ref, keep_ref, send_ref):
    slots = buf_ref.shape[0] // rows
    for slot in range(slots):
        chunk = buf_ref[pl.ds(pl.multiple_of(info_ref[base + slot] * rows, 16), rows), :]
        ref, to = (keep_ref, slot) if slot < slots // 2 else (send_ref, slot - slots // 2)
        ref[to * rows : (to + 1) * rows, :] = chunk


def outer_kernel(base, rows):
    def kernel(info_ref, la, lb, ra, rb, keep_ref, send_ref, buf_ref):
        def tile(at):
            buf_ref[at, :] = (tn(la[:, at], ra[...]) + tn(lb[:, at], rb[...])).astype(BF16)

        tiles_loop(la.shape[1], 3, tile)
        place(info_ref, base, rows, buf_ref, keep_ref, send_ref)

    return kernel


def inner_kernel(base, rows):
    def kernel(info_ref, la, lb, ra, rb, keep_ref, send_ref, buf_ref):
        for at in columns(ra.shape[1]):
            buf_ref[:, at] = (tn(la[...], ra[:, at]) + tn(lb[...], rb[:, at])).astype(BF16)
        place(info_ref, base, rows, buf_ref, keep_ref, send_ref)

    return kernel


def fill_table(info_ref, table_ref, s0m, s0o, s1, s2, sim, sio):
    half = s0m.shape[1]
    core = info_ref[CORE]
    own = pl.ds(pl.multiple_of(core * half, half), half)
    others = pl.ds(pl.multiple_of((1 - core) * half, half), half)
    table_ref[...] = jnp.zeros_like(table_ref)
    table_ref[0:3, own] = s0m[...]
    table_ref[0:3, others] = s0o[...]
    table_ref[3:6] = s1[...]
    table_ref[6:9] = s2[...]
    per = sim.shape[1] // half
    for part, which in ((sim, core), (sio, 1 - core)):
        for i in range(per):
            flat = which * per + i
            at = pl.ds(pl.multiple_of(lax.rem(flat, 2) * half, half), half)
            table_ref[pl.ds(9 + lax.div(flat, 2), 1), at] = part[:, i * half : (i + 1) * half]


def rest_kernel(base, rows):
    def kernel(
        info_ref, xa, xb, ca, cb, ga, gb, oa, ob, s0m, s0o, s1, s2, sim, sio, keep_ref, send_ref, table_ref, buf_ref
    ):
        half = s0m.shape[1]
        slots = xa.shape[1] // rows
        for i in range(4):
            la, lb, ra, rb = (xa, xb, ga.at[i], gb.at[i]) if i < 3 else (ca, cb, oa, ob)
            buf_ref[i] = (tn(la[...], ra[...]) + tn(lb[...], rb[...])).astype(BF16)
            for slot in range(slots):
                chunk = buf_ref[i, pl.ds(pl.multiple_of(info_ref[base + slot] * rows, 16), rows), :]
                ref, to = (keep_ref, slot) if slot < slots // 2 else (send_ref, slot - slots // 2)
                ref[(4 * to + i) * rows : (4 * to + i + 1) * rows, :] = chunk
        fill_table(info_ref, table_ref, s0m, s0o, s1, s2, sim, sio)
        at = keep_ref.shape[0]
        for i in range(2):
            send_ref[at + i * TABLE : at + (i + 1) * TABLE] = table_ref[:, i * half : (i + 1) * half].astype(BF16)

    return kernel


def stage_kernel(low, high, out_dtype, tables):
    def kernel(info_ref, *refs):
        ins, out_ref = refs[:-1], refs[-1]
        if tables:
            sent_ref, ins = ins[-1], ins[:-1]
        value = ins[0][low:high].astype(F32)
        for ref in ins[1:]:
            value = value + ref[low:high].astype(F32)
        out_ref[0 : high - low] = value.astype(out_dtype)
        if tables:
            rows = sent_ref.shape[0]
            value = sent_ref[rows - 2 * TABLE :].astype(F32) + ins[-1][rows - 2 * TABLE :].astype(F32)
            out_ref[high - low :] = value.astype(out_dtype)

    return kernel


def deal_kernel(info_ref, in_hbm, *refs):
    outs, sems = refs[:-1], refs[-1]
    for c in fetch([in_hbm.at[info_ref[SEQ] ^ k] for k in range(len(outs))], outs, sems):
        c.wait()


def collect_kernel(info_ref, *refs):
    for k, part in enumerate(refs[:-1]):
        refs[-1][info_ref[SEQ] ^ k] = part[...]


def finish_kernel(part, tables):
    def kernel(info_ref, *refs):
        quarters, outs = refs[:4], refs[4:]
        core, ybit = info_ref[CORE], info_ref[SEQ] // 2
        half = quarters[0].shape[1]
        if tables:
            outs, small_ref, wide_ref = outs[:-2], outs[-2], outs[-1]
        for i, ref in enumerate(quarters):
            row = pl.multiple_of((ybit ^ (i & 1)) * part, 8)
            column = pl.multiple_of((core ^ (i >> 1)) * half, 128)
            for j, out_ref in enumerate(outs):
                out_ref[pl.ds(row, part), pl.ds(column, half)] = ref[j * part : (j + 1) * part].astype(F32)
        if tables:
            at = len(outs) * part
            table = [
                quarters[0][at + i * TABLE : at + (i + 1) * TABLE].astype(F32)
                + quarters[2][at + i * TABLE : at + (i + 1) * TABLE].astype(F32)
                for i in range(2)
            ]
            d = info_ref[DP]
            lanes = 2 * half
            step = 2 * part
            rolled = pltpu.roll(jnp.concatenate(table, axis=1), lax.rem(lanes - d * step, lanes), 1)
            small_ref[...] = rolled[:, : small_ref.shape[1]]
            per = wide_ref.shape[1]
            count = lanes // per
            for row in range(TABLE - 9):
                for k in range(count):
                    line = jnp.concatenate([t[9 + row : 10 + row] for t in table], axis=1)

                    @pl.when(d == row * count + k)
                    def _():
                        wide_ref[...] = line[:, k * per : (k + 1) * per]

    return kernel


def swap(value, axis, size, bit):
    return lax.ppermute(value, axis, [(i, i ^ bit) for i in range(size)])


def make_body(sizes):
    size, dp = sizes["seq"], sizes["dp"]
    nbits = dp.bit_length()
    chunks = 2 * dp
    rest_bits = list(range(3, nbits))
    orders = {
        name: [[*bits, *rest_bits] for bits in order]
        for name, order in (("outer", OUTER), ("inner", INNER), ("rest", REST))
    }
    bases = {name: SLOTS + i * chunks for i, name in enumerate(orders)}

    def my_bit(axis, bit):
        return (lax.axis_index(axis) & bit) // bit

    def pair(value):
        return swap(value, "seq", size, 1)

    def exchange(value, bits):
        moves = []
        for d in range(dp):
            for s in range(size):
                bit = bits[s % 2]
                to = (d, s ^ 2) if bit == 0 else (d ^ (1 << (bit - 1)), s)
                moves.append((d * size + s, to[0] * size + to[1]))
        return lax.ppermute(value, ("dp", "seq"), moves)

    def chunk_table(me, core, order):
        slot = jnp.arange(chunks, dtype=jnp.int32)
        rel = [sum(((slot >> (nbits - 1 - s)) & 1) << bit for s, bit in enumerate(bits)) for bits in order]
        return jnp.where(core == 0, rel[0], rel[1]) ^ me

    class Halving:
        def __init__(self, info, keep, send, name, part, tables=False):
            self.info, self.keep, self.send, self.name, self.part = info, keep, send, name, part
            self.tables, self.got, self.left, self.stage = tables, [], chunks // 2, 0
            self.move()

        def move(self):
            first, second = orders[self.name]
            self.got.append(exchange(self.send, (first[self.stage], second[self.stage])))

        def step(self, *after):
            part, n = self.part, self.left
            last = self.stage == nbits - 1
            low, high = (0, part) if last else (n // 2 * part, n * part)
            ins = [self.keep, *self.got] + ([self.send] if self.tables else [])
            shape = like((high - low + (2 * TABLE if self.tables else 0), self.keep.shape[1]))
            self.send = call(
                stage_kernel(low, high, BF16, self.tables),
                f"{self.name}{self.stage}", self.info, ins, shape, 1, after=after,
            )
            self.left, self.stage = n // 2, self.stage + 1
            if not last:
                self.move()
            return self.send

    def spread(value, bit):
        other = swap(value, "seq", size, bit)
        first = my_bit("seq", bit) == 0
        return jnp.where(first, value, other), jnp.where(first, other, value)

    def plain_halving(value, order, me, core):
        kept = [jnp.take(value, chunk_table(me, core, order), axis=0)]
        n = chunks
        for s in range(nbits):
            n //= 2
            send = sum(v[n : 2 * n].astype(F32) for v in kept).astype(BF16)
            kept.append(exchange(send, (order[0][s], order[1][s])))
        return sum(v[0].astype(F32) for v in kept).astype(BF16)

    def body(
        inputs,
        cotangent,
        masked,
        w_query,
        b_query,
        w_key,
        w_value,
        b_value,
        w_output,
        b_output,
        attn_gain,
        attn_shift,
        w_inner,
        b_inner,
        w_outer,
        b_outer,
        ffn_gain,
        ffn_shift,
    ):
        shape = inputs.shape
        count, block, width = shape
        rows, wide, half = count * block, w_inner.shape[1], width // 2
        assert count == size == 4
        seq = lax.axis_index("seq")
        core, ybit = my_bit("seq", 1), my_bit("seq", 2)
        me = lax.axis_index("dp") * 2 + ybit
        info = jnp.concatenate(
            [jnp.stack([core, seq, lax.axis_index("dp")])] + [chunk_table(me, core, order) for order in orders.values()]
        ).astype(jnp.int32)
        row = lambda v: v.reshape(1, -1)
        full = like((rows, width))

        part_o, part_i = wide // dp // 2, width // dp // 2
        fast = nbits == 4 and part_i % 16 == 0 and (2 * part_o) % 128 == 0 and width % (2 * part_o) == 0
        blocks = [like((block, width))] * size

        def gather(value, name):
            parts = call(
                deal_kernel, name, info, [value], blocks, 1, hbm=1,
                scratch=[pltpu.SemaphoreType.DMA((size,))],
            )
            return [swap(v, "seq", size, k) if k else v for k, v in enumerate(parts)]

        def scatter(parts):
            return [parts[0]] + [swap(parts[k], "seq", size, k) for k in range(1, size)]

        def collect(parts, name, *after):
            return call(collect_kernel, name, info, parts, like(shape), 1, after=after)

        x_parts = gather(inputs, "deal_inputs")
        cot_parts = gather(cotangent * masked[:, :, None].astype(BF16), "deal_cotangent")
        square = pltpu.VMEM((width, width), BF16)
        x, q, k, v, p, ctx, n1, r1, low1 = call(
            attention_kernel, "attention", info,
            [*x_parts, row(b_query), row(b_value), row(b_output), row(attn_gain), row(attn_shift),
             w_query, w_key, w_value, w_output],
            (full, full, full, full, like((width // HD, rows, rows)), full, like((rows, width), F32),
             like((rows, 1), F32), full),
            13, 20, hbm=4, scratch=[square] * 4 + [pltpu.SemaphoreType.DMA((4,))],
        )
        x_other, ctx_other, low_other = pair(x), pair(ctx), pair(low1)
        act, slope = call(
            hidden_kernel, "hidden", info, [low1, w_inner, row(b_inner)],
            (like((rows, wide)), like((rows, wide))), 9, after=cot_parts,
        )
        act_other = pair(act)
        *out, mid, gb, gb_mine, gb_send, sums2 = call(
            branch_kernel, "branch", info,
            [act, w_outer, row(b_outer), n1, row(attn_gain), row(attn_shift), row(ffn_gain), row(ffn_shift),
             *cot_parts],
            (*blocks, like((rows, width), F32), full, like((rows, half)), like((rows, half)), like((3, width), F32)),
            4, 16,
        )
        gb_other = pair(gb_send)
        out = scatter(out)
        env, groups, token = {}, {}, []

        def buffers(part, columns, extra=0):
            return like((dp * part, columns)), like((dp * part + extra, columns))

        def product(a, b):
            return (tn(a[0], b[0]) + tn(a[1], b[1])).astype(BF16)

        def quarters(own):
            other = swap(own, "seq", size, 2)
            return [own, other, pair(own), pair(other)]

        def hidden_back(name, flip):
            shapes = (like((rows, wide // 2)), like((1, wide // 2), F32))
            env["gh_" + name], env["sumi_" + name] = call(
                hidden_back_kernel(flip), "hidden_back_" + name, info, [gb, w_outer, slope], shapes, 3,
                after=[*token, act_other] if flip else [*token, gb_other],
            )
            if flip:
                env["gh_pair"] = pair(env["gh_other"])
            return env["sumi_" + name]

        def grad_outer():
            keep, send = call(
                outer_kernel(bases["outer"], part_o), "grad_outer", info, [act, act_other, gb_mine, gb_other],
                buffers(part_o, half), 5, after=token, scratch=[pltpu.VMEM((wide, half), BF16)],
            )
            groups["o"] = Halving(info, keep, send, "outer", part_o)
            return send

        def grad_inner():
            keep, send = call(
                inner_kernel(bases["inner"], part_i), "grad_inner", info,
                [low1, low_other, env["gh_mine"], env["gh_pair"]], buffers(part_i, wide // 2), 4, after=token,
                scratch=[pltpu.VMEM((width, wide // 2), BF16)],
            )
            groups["i"] = Halving(info, keep, send, "inner", part_i)
            return send

        def first_back():
            env["gsum"], env["gctx"], env["ga"], ga_send, env["sums1"] = call(
                first_back_kernel, "first_back", info,
                [env["gh_mine"], env["gh_other"], w_inner, mid, n1, r1, row(attn_gain), w_output],
                (like((rows, width), F32), full, like((rows, half)), like((rows, half)), like((3, width), F32)),
                6, after=token,
            )
            env["ga_pair"] = pair(ga_send)
            return env["sums1"]

        def attention_back(name, flip):
            env["g3_" + name], env["sums0_" + name] = call(
                attention_back_kernel(flip), "attention_back_" + name, info, [q, k, v, p, env["gctx"]],
                (like((3, rows, half)), like((3, half), F32)), 1, after=token,
            )
            if flip:
                env["g3_pair"] = pair(env["g3_other"])
            return env["sums0_" + name]

        def grad_rest():
            sums = [env["sums0_mine"], env["sums0_other"], env["sums1"], sums2, env["sumi_mine"], env["sumi_other"]]
            keep, send, table = call(
                rest_kernel(bases["rest"], part_i), "grad_rest", info,
                [x, x_other, ctx, ctx_other, env["g3_mine"], env["g3_pair"], env["ga"], env["ga_pair"], *sums],
                (*buffers(4 * part_i, half, 2 * TABLE), like((TABLE, width), F32)), 1, after=token,
                scratch=[pltpu.VMEM((4, width, half), BF16)],
            )
            groups["r"] = Halving(info, keep, send, "rest", 4 * part_i, True)
            return table

        def input_back():
            parts = call(
                input_back_kernel, "input_back", info,
                [env["g3_mine"], env["g3_other"], env["gsum"], w_query, w_key, w_value], blocks, 2, after=token,
                hbm=3, mb=52, scratch=[square] * 3 + [pltpu.SemaphoreType.DMA((3,))],
            )
            env["back"] = scatter(parts)
            return parts[0]

        def step(name):
            own = groups[name].step(*token)
            if groups[name].stage == nbits:
                env["q" + name] = quarters(own)
            return own

        def finish_group(name, part, columns, title):
            env["g" + name] = call(
                finish_kernel(part, False), title, info, env["q" + name], like((2 * part, columns), F32), 1, after=token
            )
            return env["g" + name]

        def finish_rest():
            matrix, thin = like((2 * part_i, width), F32), like((TABLE, 128), F32)
            env["gr"] = call(
                finish_kernel(part_i, True), "finish_rest", info, env["qr"],
                (matrix, matrix, matrix, matrix, thin, like((1, 2 * part_o), F32)), 1, after=token,
            )
            return env["gr"][4]

        def collect(name, parts):
            env[name] = call(collect_kernel, "collect_" + name, info, parts, like(shape), 1, after=token)
            return env[name]

        tasks = {
            "ho": lambda: hidden_back("other", True),
            "hm": lambda: hidden_back("mine", False),
            "go": grad_outer,
            "gi": grad_inner,
            "fb": first_back,
            "ao": lambda: attention_back("other", True),
            "am": lambda: attention_back("mine", False),
            "gr": grad_rest,
            "ib": input_back,
            "o": lambda: step("o"),
            "i": lambda: step("i"),
            "r": lambda: step("r"),
            "fo": lambda: finish_group("o", part_o, width, "finish_outer"),
            "fi": lambda: finish_group("i", part_i, wide, "finish_inner"),
            "fr": finish_rest,
            "co": lambda: collect("outputs", out),
            "ci": lambda: collect("inputs", env["back"]),
        }
        for name in ORDER:
            if fast or name in ("ho", "hm", "fb", "ao", "am", "ib", "co", "ci"):
                token = [tasks[name]()]

        def finish(value, group, part, columns):
            value = jnp.stack(spread(value.reshape(group, part, columns // 2), 2), axis=1)
            value = value.reshape(group, 2 * part, columns // 2)
            return jnp.concatenate(spread(value, 1), axis=-1).astype(F32)

        if fast:
            g_outer, g_inner = env["go"], env["gi"]
            g_query, g_key, g_value, g_output, small, wide_row = env["gr"]
            small = [small[i, : 2 * part_i] for i in range(9)] + [wide_row[0]]
        else:
            me_core = (me, core)

            def cut(value, part):
                return value.reshape(chunks, part, value.shape[1])

            own_o = plain_halving(
                cut(product((act, act_other), (gb_mine, gb_other)), part_o), orders["outer"], *me_core
            )
            own_i = plain_halving(
                cut(product((low1, low_other), (env["gh_mine"], env["gh_pair"])), part_i), orders["inner"], *me_core
            )
            four = [product((x, x_other), (env["g3_mine"][i], env["g3_pair"][i])) for i in range(3)]
            four.append(product((ctx, ctx_other), (env["ga"], env["ga_pair"])))
            four = jnp.stack([cut(f, part_i) for f in four], axis=1)
            own_r = plain_halving(four, orders["rest"], *me_core)

            def both(mine, other):
                return jnp.where(
                    core == 0,
                    jnp.concatenate([mine, other], axis=1),
                    jnp.concatenate([other, mine], axis=1),
                )

            table = jnp.concatenate(
                [
                    both(env["sums0_mine"], env["sums0_other"]),
                    env["sums1"],
                    sums2,
                    both(env["sumi_mine"], env["sumi_other"]).reshape(-1, width),
                ]
            )
            table = lax.psum(table, ("dp", "seq"))
            (g_outer,) = finish(own_o, 1, part_o, width)
            (g_inner,) = finish(own_i, 1, part_i, wide)
            g_query, g_key, g_value, g_output = finish(own_r, 4, part_i, width)
            lines = [table[i] for i in range(9)] + [table[9:].reshape(-1)]
            small = []
            for line in lines:
                n = line.shape[0] // dp
                small.append(lax.dynamic_slice_in_dim(line, lax.axis_index("dp") * n, n))
        return (
            env["outputs"],
            env["inputs"],
            g_query,
            small[0],
            g_key,
            g_value,
            small[2],
            g_output,
            small[5],
            small[3],
            small[4],
            g_inner,
            small[9],
            g_outer,
            small[8],
            small[6],
            small[7],
        )

    return body


def solution(mesh):
    rows = P("dp", "seq", None)
    matrix, vector = P("dp", None), P("dp")
    in_specs = (rows, rows, P("dp", "seq"), *[P()] * 15)
    out_specs = (
        rows,
        rows,
        matrix,
        vector,
        matrix,
        matrix,
        vector,
        matrix,
        vector,
        vector,
        vector,
        matrix,
        vector,
        matrix,
        vector,
        vector,
        vector,
    )
    body = make_body(dict(mesh.shape))
    return jax.shard_map(
        body, mesh=mesh, in_specs=in_specs, out_specs=out_specs, check_vma=False
    )
```

```python
import jax
import jax.numpy as jnp
from jax import lax
from jax.experimental import pallas as pl
from jax.experimental.pallas import tpu as pltpu
from jax.sharding import PartitionSpec as P

HD = 64
PAIR = 2 * HD
TILE = 256
EPSILON = 1e-05
F32, BF16 = jnp.float32, jnp.bfloat16
CORE, SEQ, DP, SLOTS = 0, 1, 2, 3
TABLE = 16
SCALE = 3e9
ORDER = (
    "ho", "hm", "go", "co", "gi", "fb", "ao", "o", "am", "o", "gr", "i", "r", "ib", "i", "o", "r",
    "i", "o", "ci", "r", "fo", "i", "r", "fi", "fr",
)
OUTER, INNER, REST = ((0, 1, 2), (1, 0, 2)), ((2, 0, 1), (1, 2, 0)), ((0, 1, 2), (1, 0, 2))


def nn(a, b):
    return lax.dot_general(a, b, (((1,), (0,)), ((), ())), preferred_element_type=F32)


def nt(a, b):
    return lax.dot_general(a, b, (((1,), (1,)), ((), ())), preferred_element_type=F32)


def tn(a, b):
    return lax.dot_general(a, b, (((0,), (0,)), ((), ())), preferred_element_type=F32)


def like(shape, dtype=BF16):
    return jax.ShapeDtypeStruct(shape, dtype)


def call(kernel, name, info, ins, outs, us, mb=14, after=(), hbm=0, scratch=()):
    n, skip = len(ins), len(after)

    def run(info_ref, *refs):
        kernel(info_ref, *refs[:n], *refs[n + skip :])

    return pl.pallas_call(
        run,
        in_specs=[pl.BlockSpec(memory_space=pltpu.SMEM)]
        + [pl.BlockSpec(memory_space=pltpu.VMEM)] * (n - hbm)
        + [pl.BlockSpec(memory_space=pltpu.HBM)] * hbm
        + [pl.BlockSpec(memory_space=pl.ANY)] * skip,
        out_shape=outs,
        scratch_shapes=list(scratch),
        compiler_params=pltpu.CompilerParams(vmem_limit_bytes=mb * 1024 * 1024),
        cost_estimate=pl.CostEstimate(
            flops=int(us * SCALE), bytes_accessed=1, transcendentals=0
        ),
        name=name,
    )(info, *ins, *after)


def fetch(sources, targets, sems):
    copies = [pltpu.make_async_copy(a, b, sems.at[i]) for i, (a, b) in enumerate(zip(sources, targets))]
    for c in copies:
        c.start()
    return copies


def halves(value):
    lane = lax.broadcasted_iota(jnp.int32, value.shape, 1)
    zero = jnp.zeros_like(value)
    return jnp.where(lane < HD, value, zero), jnp.where(lane < HD, zero, value)


def standardize(v):
    mean = jnp.mean(v, axis=-1, keepdims=True)
    c = v - mean
    r = lax.rsqrt(jnp.mean(c * c, axis=-1, keepdims=True) + EPSILON)
    return c * r, r


def norm_back(e, n, r):
    return r * (e - jnp.mean(e, axis=-1, keepdims=True) - n * jnp.mean(e * n, axis=-1, keepdims=True))


def columns(width):
    return [slice(j, j + TILE) for j in range(0, width, TILE)]


def tiles_loop(width, each, body):
    def step(i, carry):
        for j in range(each):
            body(pl.ds(pl.multiple_of((i * each + j) * TILE, TILE), TILE))
        return carry

    lax.fori_loop(0, width // (TILE * each), step, 0)


def total(value):
    return jnp.sum(value, axis=0, keepdims=True)


def attention_kernel(
    info_ref, x0, x1, x2, x3, bq_ref, bv_ref, bo_ref, gain_ref, shift_ref, wq_hbm, wk_hbm, wv_hbm, wo_hbm,
    x_ref, q_ref, k_ref, v_ref, p_ref, ctx_ref, n_ref, r_ref, low_ref,
    wq_ref, wk_ref, wv_ref, wo_ref, sems,
):
    rows, width = x_ref.shape
    block = x0.shape[0]
    copies = fetch((wq_hbm, wk_hbm, wv_hbm, wo_hbm), (wq_ref, wk_ref, wv_ref, wo_ref), sems)
    for i, part in enumerate((x0, x1, x2, x3)):
        x_ref[i * block : (i + 1) * block, :] = part[...]
    x = x_ref[...]
    copies[0].wait()
    for at in columns(width):
        q = (nn(x, wq_ref[:, at]) + bq_ref[:, at].astype(F32)).astype(BF16)
        q_ref[:, at] = q * jnp.asarray(HD ** -0.5, BF16)
    copies[1].wait()
    for at in columns(width):
        k_ref[:, at] = nn(x, wk_ref[:, at]).astype(BF16)
    copies[2].wait()
    for at in columns(width):
        v_ref[:, at] = (nn(x, wv_ref[:, at]) + bv_ref[:, at].astype(F32)).astype(BF16)
    for p in range(width // PAIR):
        at = slice(p * PAIR, (p + 1) * PAIR)
        q, k, v = q_ref[:, at], k_ref[:, at], v_ref[:, at]
        vt = v.astype(F32).T.astype(BF16)
        out = []
        for i, kh in enumerate(halves(k)):
            s = nt(kh, q)
            e = jnp.exp(s - jnp.max(s, axis=0, keepdims=True))
            w = (e * (1.0 / total(e))).astype(BF16)
            p_ref[2 * p + i] = w
            out.append(nn(vt[i * HD : (i + 1) * HD], w))
        ctx_ref[:, at] = jnp.concatenate(out, axis=0).T.astype(BF16)
    copies[3].wait()
    v1 = jnp.concatenate([nn(ctx_ref[...], wo_ref[:, at]) for at in columns(width)], axis=1)
    v1 = x_ref[...].astype(F32) + (v1 + bo_ref[...].astype(F32))
    n, r = standardize(v1)
    n_ref[...] = n
    r_ref[...] = r
    low_ref[...] = (n * gain_ref[...].astype(F32) + shift_ref[...].astype(F32)).astype(BF16)


def hidden_kernel(info_ref, low_ref, w_ref, b_ref, act_ref, slope_ref):
    def tile(at):
        h = nn(low_ref[...], w_ref[:, at]) + b_ref[:, at].astype(F32)
        z = h * 0.7071067811865476
        phi = 0.5 + 0.5 * lax.erf(z)
        bell = jnp.exp2(z * z * -1.4426950408889634)
        act_ref[:, at] = (h * phi).astype(BF16)
        slope_ref[:, at] = (phi + z * bell * 0.5641895835477563).astype(BF16)

    tiles_loop(w_ref.shape[1], 3, tile)


def split_store(core, value, mine_ref, other_ref):
    half = value.shape[1] // 2
    mine_ref[...] = jnp.where(core == 0, value[:, :half], value[:, half:])
    other_ref[...] = jnp.where(core == 0, value[:, half:], value[:, :half])


def branch_kernel(
    info_ref, act_ref, w_ref, b_ref, n_ref, gain1_ref, shift1_ref, gain_ref, shift_ref, c0, c1, c2, c3,
    o0, o1, o2, o3, mid_ref, low_ref, mine_ref, other_ref, sums_ref,
):
    width = mid_ref.shape[1]
    normed = n_ref[...] * gain1_ref[...].astype(F32) + shift1_ref[...].astype(F32)
    branch = jnp.concatenate([nn(act_ref[...], w_ref[:, at]) for at in columns(width)], axis=1)
    n, r = standardize(normed + (branch + b_ref[...].astype(F32)))
    gain = gain_ref[...].astype(F32)
    out = (n * gain + shift_ref[...].astype(F32)).astype(BF16)
    for i, ref in enumerate((o0, o1, o2, o3)):
        ref[...] = out[i * ref.shape[0] : (i + 1) * ref.shape[0]]
    go = jnp.concatenate([c[...] for c in (c0, c1, c2, c3)]).astype(F32)
    mid = norm_back(go * gain, n, r)
    mid_ref[...] = mid
    low = mid.astype(BF16)
    low_ref[...] = low
    split_store(info_ref[CORE], low, mine_ref, other_ref)
    sums_ref[0:1] = total(go * n)
    sums_ref[1:2] = total(go)
    sums_ref[2:3] = total(low.astype(F32))


def hidden_back_kernel(flip):
    def kernel(info_ref, low_ref, w_ref, slope_ref, out_ref, sums_ref):
        half = out_ref.shape[1]
        core = info_ref[CORE]
        first = ((1 - core) if flip else core) * half
        for to in columns(half):
            at = pl.ds(pl.multiple_of(first + to.start, TILE), TILE)
            g = (nt(low_ref[...], w_ref[at, :]) * slope_ref[:, at].astype(F32)).astype(BF16)
            out_ref[:, to] = g
            sums_ref[:, to] = total(g.astype(F32))

    return kernel


def first_back_kernel(
    info_ref, gm_ref, go_ref, w_ref, mid_ref, n_ref, r_ref, gain_ref, wo_ref,
    sum_ref, gctx_ref, mine_ref, other_ref, sums_ref,
):
    width, half = mid_ref.shape[1], gm_ref.shape[1]
    core = info_ref[CORE]
    mine = pl.ds(pl.multiple_of(core * half, half), half)
    other = pl.ds(pl.multiple_of((1 - core) * half, half), half)
    gn = jnp.concatenate(
        [nt(gm_ref[...], w_ref[at, mine]) + nt(go_ref[...], w_ref[at, other]) for at in columns(width)], axis=1
    )
    gn = gn + mid_ref[...]
    n = n_ref[...]
    gs = norm_back(gn * gain_ref[...].astype(F32), n, r_ref[...])
    sum_ref[...] = gs
    low = gs.astype(BF16)
    split_store(core, low, mine_ref, other_ref)
    sums_ref[0:1] = total(gn * n)
    sums_ref[1:2] = total(gn)
    sums_ref[2:3] = total(low.astype(F32))
    for at in columns(width):
        gctx_ref[:, at] = nt(low, wo_ref[at, :]).astype(BF16)


def attention_back_kernel(flip):
    def kernel(info_ref, q_ref, k_ref, v_ref, p_ref, g_ref, out_ref, sums_ref):
        rows, width = q_ref.shape
        per = width // PAIR // 2
        core = info_ref[CORE]
        first = ((1 - core) if flip else core) * per

        def pair(p, carry):
            at = pl.ds(pl.multiple_of((first + p) * PAIR, PAIR), PAIR)
            to = pl.ds(pl.multiple_of(p * PAIR, PAIR), PAIR)
            q, k, v, g = q_ref[:, at], k_ref[:, at], v_ref[:, at], g_ref[:, at]
            kt = k.astype(F32).T.astype(BF16)
            gk = jnp.zeros((rows, PAIR), F32)
            gv = jnp.zeros((rows, PAIR), F32)
            gq = []
            for i, (qh, vh, gh) in enumerate(zip(halves(q), halves(v), halves(g))):
                w = p_ref[2 * (first + p) + i]
                w32 = w.astype(F32)
                prod = w32 * nt(vh, g)
                gs = (prod - w32 * total(prod)).astype(BF16)
                gk = gk + nn(gs, qh)
                gv = gv + nn(w, gh)
                gq.append(nn(kt[i * HD : (i + 1) * HD], gs))
            gq = jnp.concatenate(gq, axis=0).T * HD ** -0.5
            for i, value in enumerate((gq, gk, gv)):
                value = value.astype(BF16)
                out_ref[i, :, to] = value
                sums_ref[i : i + 1, to] = total(value.astype(F32))
            return carry

        lax.fori_loop(0, per, pair, 0)

    return kernel


def input_back_kernel(info_ref, gm_ref, go_ref, sum_ref, wq_hbm, wk_hbm, wv_hbm, o0, o1, o2, o3, wq_ref, wk_ref, wv_ref, sems):
    half = gm_ref.shape[2]
    copies = fetch((wq_hbm, wk_hbm, wv_hbm), (wq_ref, wk_ref, wv_ref), sems)
    core = info_ref[CORE]
    mine = pl.ds(pl.multiple_of(core * half, half), half)
    other = pl.ds(pl.multiple_of((1 - core) * half, half), half)
    tiles = columns(sum_ref.shape[1])
    values = [sum_ref[:, at] for at in tiles]
    for i, w in enumerate((wq_ref, wk_ref, wv_ref)):
        copies[i].wait()
        for j, at in enumerate(tiles):
            values[j] = values[j] + nt(gm_ref[i], w[at, mine]) + nt(go_ref[i], w[at, other])
    for value, at in zip(values, tiles):
        value = value.astype(BF16)
        for i, ref in enumerate((o0, o1, o2, o3)):
            ref[:, at] = value[i * ref.shape[0] : (i + 1) * ref.shape[0]]


def place(info_ref, base, rows, buf_ref, keep_ref, send_ref):
    slots = buf_ref.shape[0] // rows
    for slot in range(slots):
        chunk = buf_ref[pl.ds(pl.multiple_of(info_ref[base + slot] * rows, 16), rows), :]
        ref, to = (keep_ref, slot) if slot < slots // 2 else (send_ref, slot - slots // 2)
        ref[to * rows : (to + 1) * rows, :] = chunk


def outer_kernel(base, rows):
    def kernel(info_ref, la, lb, ra, rb, keep_ref, send_ref, buf_ref):
        def tile(at):
            buf_ref[at, :] = (tn(la[:, at], ra[...]) + tn(lb[:, at], rb[...])).astype(BF16)

        tiles_loop(la.shape[1], 3, tile)
        place(info_ref, base, rows, buf_ref, keep_ref, send_ref)

    return kernel


def inner_kernel(base, rows):
    def kernel(info_ref, la, lb, ra, rb, keep_ref, send_ref, buf_ref):
        for at in columns(ra.shape[1]):
            buf_ref[:, at] = (tn(la[...], ra[:, at]) + tn(lb[...], rb[:, at])).astype(BF16)
        place(info_ref, base, rows, buf_ref, keep_ref, send_ref)

    return kernel


def fill_table(info_ref, table_ref, s0m, s0o, s1, s2, sim, sio):
    half = s0m.shape[1]
    core = info_ref[CORE]
    own = pl.ds(pl.multiple_of(core * half, half), half)
    others = pl.ds(pl.multiple_of((1 - core) * half, half), half)
    table_ref[...] = jnp.zeros_like(table_ref)
    table_ref[0:3, own] = s0m[...]
    table_ref[0:3, others] = s0o[...]
    table_ref[3:6] = s1[...]
    table_ref[6:9] = s2[...]
    per = sim.shape[1] // half
    for part, which in ((sim, core), (sio, 1 - core)):
        for i in range(per):
            flat = which * per + i
            at = pl.ds(pl.multiple_of(lax.rem(flat, 2) * half, half), half)
            table_ref[pl.ds(9 + lax.div(flat, 2), 1), at] = part[:, i * half : (i + 1) * half]


def rest_kernel(base, rows):
    def kernel(
        info_ref, xa, xb, ca, cb, ga, gb, oa, ob, s0m, s0o, s1, s2, sim, sio, keep_ref, send_ref, table_ref, buf_ref
    ):
        half = s0m.shape[1]
        slots = xa.shape[1] // rows
        for i in range(4):
            la, lb, ra, rb = (xa, xb, ga.at[i], gb.at[i]) if i < 3 else (ca, cb, oa, ob)
            buf_ref[i] = (tn(la[...], ra[...]) + tn(lb[...], rb[...])).astype(BF16)
            for slot in range(slots):
                chunk = buf_ref[i, pl.ds(pl.multiple_of(info_ref[base + slot] * rows, 16), rows), :]
                ref, to = (keep_ref, slot) if slot < slots // 2 else (send_ref, slot - slots // 2)
                ref[(4 * to + i) * rows : (4 * to + i + 1) * rows, :] = chunk
        fill_table(info_ref, table_ref, s0m, s0o, s1, s2, sim, sio)
        at = keep_ref.shape[0]
        for i in range(2):
            send_ref[at + i * TABLE : at + (i + 1) * TABLE] = table_ref[:, i * half : (i + 1) * half].astype(BF16)

    return kernel


def stage_kernel(low, high, out_dtype, tables):
    def kernel(info_ref, *refs):
        ins, out_ref = refs[:-1], refs[-1]
        if tables:
            sent_ref, ins = ins[-1], ins[:-1]
        value = ins[0][low:high].astype(F32)
        for ref in ins[1:]:
            value = value + ref[low:high].astype(F32)
        out_ref[0 : high - low] = value.astype(out_dtype)
        if tables:
            rows = sent_ref.shape[0]
            value = sent_ref[rows - 2 * TABLE :].astype(F32) + ins[-1][rows - 2 * TABLE :].astype(F32)
            out_ref[high - low :] = value.astype(out_dtype)

    return kernel


def deal_kernel(info_ref, in_hbm, *refs):
    outs, sems = refs[:-1], refs[-1]
    for c in fetch([in_hbm.at[info_ref[SEQ] ^ k] for k in range(len(outs))], outs, sems):
        c.wait()


def collect_kernel(info_ref, *refs):
    for k, part in enumerate(refs[:-1]):
        refs[-1][info_ref[SEQ] ^ k] = part[...]


def finish_kernel(part, tables):
    def kernel(info_ref, *refs):
        quarters, outs = refs[:4], refs[4:]
        core, ybit = info_ref[CORE], info_ref[SEQ] // 2
        half = quarters[0].shape[1]
        if tables:
            outs, small_ref, wide_ref = outs[:-2], outs[-2], outs[-1]
        for i, ref in enumerate(quarters):
            row = pl.multiple_of((ybit ^ (i & 1)) * part, 8)
            column = pl.multiple_of((core ^ (i >> 1)) * half, 128)
            for j, out_ref in enumerate(outs):
                out_ref[pl.ds(row, part), pl.ds(column, half)] = ref[j * part : (j + 1) * part].astype(F32)
        if tables:
            at = len(outs) * part
            table = [
                quarters[0][at + i * TABLE : at + (i + 1) * TABLE].astype(F32)
                + quarters[2][at + i * TABLE : at + (i + 1) * TABLE].astype(F32)
                for i in range(2)
            ]
            d = info_ref[DP]
            lanes = 2 * half
            step = 2 * part
            rolled = pltpu.roll(jnp.concatenate(table, axis=1), lax.rem(lanes - d * step, lanes), 1)
            small_ref[...] = rolled[:, : small_ref.shape[1]]
            per = wide_ref.shape[1]
            count = lanes // per
            for row in range(TABLE - 9):
                for k in range(count):
                    line = jnp.concatenate([t[9 + row : 10 + row] for t in table], axis=1)

                    @pl.when(d == row * count + k)
                    def _():
                        wide_ref[...] = line[:, k * per : (k + 1) * per]

    return kernel


def swap(value, axis, size, bit):
    return lax.ppermute(value, axis, [(i, i ^ bit) for i in range(size)])


def make_body(sizes):
    size, dp = sizes["seq"], sizes["dp"]
    nbits = dp.bit_length()
    chunks = 2 * dp
    rest_bits = list(range(3, nbits))
    orders = {
        name: [[*bits, *rest_bits] for bits in order]
        for name, order in (("outer", OUTER), ("inner", INNER), ("rest", REST))
    }
    bases = {name: SLOTS + i * chunks for i, name in enumerate(orders)}

    def my_bit(axis, bit):
        return (lax.axis_index(axis) & bit) // bit

    def pair(value):
        return swap(value, "seq", size, 1)

    def exchange(value, bits):
        moves = []
        for d in range(dp):
            for s in range(size):
                bit = bits[s % 2]
                to = (d, s ^ 2) if bit == 0 else (d ^ (1 << (bit - 1)), s)
                moves.append((d * size + s, to[0] * size + to[1]))
        return lax.ppermute(value, ("dp", "seq"), moves)

    def chunk_table(me, core, order):
        slot = jnp.arange(chunks, dtype=jnp.int32)
        rel = [sum(((slot >> (nbits - 1 - s)) & 1) << bit for s, bit in enumerate(bits)) for bits in order]
        return jnp.where(core == 0, rel[0], rel[1]) ^ me

    class Halving:
        def __init__(self, info, keep, send, name, part, tables=False):
            self.info, self.keep, self.send, self.name, self.part = info, keep, send, name, part
            self.tables, self.got, self.left, self.stage = tables, [], chunks // 2, 0
            self.move()

        def move(self):
            first, second = orders[self.name]
            self.got.append(exchange(self.send, (first[self.stage], second[self.stage])))

        def step(self, *after):
            part, n = self.part, self.left
            last = self.stage == nbits - 1
            low, high = (0, part) if last else (n // 2 * part, n * part)
            ins = [self.keep, *self.got] + ([self.send] if self.tables else [])
            shape = like((high - low + (2 * TABLE if self.tables else 0), self.keep.shape[1]))
            self.send = call(
                stage_kernel(low, high, BF16, self.tables),
                f"{self.name}{self.stage}", self.info, ins, shape, 1, after=after,
            )
            self.left, self.stage = n // 2, self.stage + 1
            if not last:
                self.move()
            return self.send

    def spread(value, bit):
        other = swap(value, "seq", size, bit)
        first = my_bit("seq", bit) == 0
        return jnp.where(first, value, other), jnp.where(first, other, value)

    def plain_halving(value, order, me, core):
        kept = [jnp.take(value, chunk_table(me, core, order), axis=0)]
        n = chunks
        for s in range(nbits):
            n //= 2
            send = sum(v[n : 2 * n].astype(F32) for v in kept).astype(BF16)
            kept.append(exchange(send, (order[0][s], order[1][s])))
        return sum(v[0].astype(F32) for v in kept).astype(BF16)

    def body(
        inputs,
        cotangent,
        masked,
        w_query,
        b_query,
        w_key,
        w_value,
        b_value,
        w_output,
        b_output,
        attn_gain,
        attn_shift,
        w_inner,
        b_inner,
        w_outer,
        b_outer,
        ffn_gain,
        ffn_shift,
    ):
        shape = inputs.shape
        count, block, width = shape
        rows, wide, half = count * block, w_inner.shape[1], width // 2
        assert count == size == 4
        seq = lax.axis_index("seq")
        core, ybit = my_bit("seq", 1), my_bit("seq", 2)
        me = lax.axis_index("dp") * 2 + ybit
        info = jnp.concatenate(
            [jnp.stack([core, seq, lax.axis_index("dp")])] + [chunk_table(me, core, order) for order in orders.values()]
        ).astype(jnp.int32)
        row = lambda v: v.reshape(1, -1)
        full = like((rows, width))

        part_o, part_i = wide // dp // 2, width // dp // 2
        fast = nbits == 4 and part_i % 16 == 0 and (2 * part_o) % 128 == 0 and width % (2 * part_o) == 0
        blocks = [like((block, width))] * size

        def gather(value, name):
            parts = call(
                deal_kernel, name, info, [value], blocks, 1, hbm=1,
                scratch=[pltpu.SemaphoreType.DMA((size,))],
            )
            return [swap(v, "seq", size, k) if k else v for k, v in enumerate(parts)]

        def scatter(parts):
            return [parts[0]] + [swap(parts[k], "seq", size, k) for k in range(1, size)]

        def collect(parts, name, *after):
            return call(collect_kernel, name, info, parts, like(shape), 1, after=after)

        x_parts = gather(inputs, "deal_inputs")
        cot_parts = gather(cotangent * masked[:, :, None].astype(BF16), "deal_cotangent")
        square = pltpu.VMEM((width, width), BF16)
        x, q, k, v, p, ctx, n1, r1, low1 = call(
            attention_kernel, "attention", info,
            [*x_parts, row(b_query), row(b_value), row(b_output), row(attn_gain), row(attn_shift),
             w_query, w_key, w_value, w_output],
            (full, full, full, full, like((width // HD, rows, rows)), full, like((rows, width), F32),
             like((rows, 1), F32), full),
            13, 20, hbm=4, scratch=[square] * 4 + [pltpu.SemaphoreType.DMA((4,))],
        )
        x_other, ctx_other, low_other = pair(x), pair(ctx), pair(low1)
        act, slope = call(
            hidden_kernel, "hidden", info, [low1, w_inner, row(b_inner)],
            (like((rows, wide)), like((rows, wide))), 9, after=cot_parts,
        )
        act_other = pair(act)
        *out, mid, gb, gb_mine, gb_send, sums2 = call(
            branch_kernel, "branch", info,
            [act, w_outer, row(b_outer), n1, row(attn_gain), row(attn_shift), row(ffn_gain), row(ffn_shift),
             *cot_parts],
            (*blocks, like((rows, width), F32), full, like((rows, half)), like((rows, half)), like((3, width), F32)),
            4, 16,
        )
        gb_other = pair(gb_send)
        out = scatter(out)
        env, groups, token = {}, {}, []

        def buffers(part, columns, extra=0):
            return like((dp * part, columns)), like((dp * part + extra, columns))

        def product(a, b):
            return (tn(a[0], b[0]) + tn(a[1], b[1])).astype(BF16)

        def quarters(own):
            other = swap(own, "seq", size, 2)
            return [own, other, pair(own), pair(other)]

        def hidden_back(name, flip):
            shapes = (like((rows, wide // 2)), like((1, wide // 2), F32))
            env["gh_" + name], env["sumi_" + name] = call(
                hidden_back_kernel(flip), "hidden_back_" + name, info, [gb, w_outer, slope], shapes, 3,
                after=[*token, act_other] if flip else [*token, gb_other],
            )
            if flip:
                env["gh_pair"] = pair(env["gh_other"])
            return env["sumi_" + name]

        def grad_outer():
            keep, send = call(
                outer_kernel(bases["outer"], part_o), "grad_outer", info, [act, act_other, gb_mine, gb_other],
                buffers(part_o, half), 5, after=token, scratch=[pltpu.VMEM((wide, half), BF16)],
            )
            groups["o"] = Halving(info, keep, send, "outer", part_o)
            return send

        def grad_inner():
            keep, send = call(
                inner_kernel(bases["inner"], part_i), "grad_inner", info,
                [low1, low_other, env["gh_mine"], env["gh_pair"]], buffers(part_i, wide // 2), 4, after=token,
                scratch=[pltpu.VMEM((width, wide // 2), BF16)],
            )
            groups["i"] = Halving(info, keep, send, "inner", part_i)
            return send

        def first_back():
            env["gsum"], env["gctx"], env["ga"], ga_send, env["sums1"] = call(
                first_back_kernel, "first_back", info,
                [env["gh_mine"], env["gh_other"], w_inner, mid, n1, r1, row(attn_gain), w_output],
                (like((rows, width), F32), full, like((rows, half)), like((rows, half)), like((3, width), F32)),
                6, after=token,
            )
            env["ga_pair"] = pair(ga_send)
            return env["sums1"]

        def attention_back(name, flip):
            env["g3_" + name], env["sums0_" + name] = call(
                attention_back_kernel(flip), "attention_back_" + name, info, [q, k, v, p, env["gctx"]],
                (like((3, rows, half)), like((3, half), F32)), 1, after=token,
            )
            if flip:
                env["g3_pair"] = pair(env["g3_other"])
            return env["sums0_" + name]

        def grad_rest():
            sums = [env["sums0_mine"], env["sums0_other"], env["sums1"], sums2, env["sumi_mine"], env["sumi_other"]]
            keep, send, table = call(
                rest_kernel(bases["rest"], part_i), "grad_rest", info,
                [x, x_other, ctx, ctx_other, env["g3_mine"], env["g3_pair"], env["ga"], env["ga_pair"], *sums],
                (*buffers(4 * part_i, half, 2 * TABLE), like((TABLE, width), F32)), 1, after=token,
                scratch=[pltpu.VMEM((4, width, half), BF16)],
            )
            groups["r"] = Halving(info, keep, send, "rest", 4 * part_i, True)
            return table

        def input_back():
            parts = call(
                input_back_kernel, "input_back", info,
                [env["g3_mine"], env["g3_other"], env["gsum"], w_query, w_key, w_value], blocks, 2, after=token,
                hbm=3, mb=52, scratch=[square] * 3 + [pltpu.SemaphoreType.DMA((3,))],
            )
            env["back"] = scatter(parts)
            return parts[0]

        def step(name):
            own = groups[name].step(*token)
            if groups[name].stage == nbits:
                env["q" + name] = quarters(own)
            return own

        def finish_group(name, part, columns, title):
            env["g" + name] = call(
                finish_kernel(part, False), title, info, env["q" + name], like((2 * part, columns), F32), 1, after=token
            )
            return env["g" + name]

        def finish_rest():
            matrix, thin = like((2 * part_i, width), F32), like((TABLE, 128), F32)
            env["gr"] = call(
                finish_kernel(part_i, True), "finish_rest", info, env["qr"],
                (matrix, matrix, matrix, matrix, thin, like((1, 2 * part_o), F32)), 1, after=token,
            )
            return env["gr"][4]

        def collect(name, parts):
            env[name] = call(collect_kernel, "collect_" + name, info, parts, like(shape), 1, after=token)
            return env[name]

        tasks = {
            "ho": lambda: hidden_back("other", True),
            "hm": lambda: hidden_back("mine", False),
            "go": grad_outer,
            "gi": grad_inner,
            "fb": first_back,
            "ao": lambda: attention_back("other", True),
            "am": lambda: attention_back("mine", False),
            "gr": grad_rest,
            "ib": input_back,
            "o": lambda: step("o"),
            "i": lambda: step("i"),
            "r": lambda: step("r"),
            "fo": lambda: finish_group("o", part_o, width, "finish_outer"),
            "fi": lambda: finish_group("i", part_i, wide, "finish_inner"),
            "fr": finish_rest,
            "co": lambda: collect("outputs", out),
            "ci": lambda: collect("inputs", env["back"]),
        }
        for name in ORDER:
            if fast or name in ("ho", "hm", "fb", "ao", "am", "ib", "co", "ci"):
                token = [tasks[name]()]

        def finish(value, group, part, columns):
            value = jnp.stack(spread(value.reshape(group, part, columns // 2), 2), axis=1)
            value = value.reshape(group, 2 * part, columns // 2)
            return jnp.concatenate(spread(value, 1), axis=-1).astype(F32)

        if fast:
            g_outer, g_inner = env["go"], env["gi"]
            g_query, g_key, g_value, g_output, small, wide_row = env["gr"]
            small = [small[i, : 2 * part_i] for i in range(9)] + [wide_row[0]]
        else:
            me_core = (me, core)

            def cut(value, part):
                return value.reshape(chunks, part, value.shape[1])

            own_o = plain_halving(
                cut(product((act, act_other), (gb_mine, gb_other)), part_o), orders["outer"], *me_core
            )
            own_i = plain_halving(
                cut(product((low1, low_other), (env["gh_mine"], env["gh_pair"])), part_i), orders["inner"], *me_core
            )
            four = [product((x, x_other), (env["g3_mine"][i], env["g3_pair"][i])) for i in range(3)]
            four.append(product((ctx, ctx_other), (env["ga"], env["ga_pair"])))
            four = jnp.stack([cut(f, part_i) for f in four], axis=1)
            own_r = plain_halving(four, orders["rest"], *me_core)

            def both(mine, other):
                return jnp.where(
                    core == 0,
                    jnp.concatenate([mine, other], axis=1),
                    jnp.concatenate([other, mine], axis=1),
                )

            table = jnp.concatenate(
                [
                    both(env["sums0_mine"], env["sums0_other"]),
                    env["sums1"],
                    sums2,
                    both(env["sumi_mine"], env["sumi_other"]).reshape(-1, width),
                ]
            )
            table = lax.psum(table, ("dp", "seq"))
            (g_outer,) = finish(own_o, 1, part_o, width)
            (g_inner,) = finish(own_i, 1, part_i, wide)
            g_query, g_key, g_value, g_output = finish(own_r, 4, part_i, width)
            lines = [table[i] for i in range(9)] + [table[9:].reshape(-1)]
            small = []
            for line in lines:
                n = line.shape[0] // dp
                small.append(lax.dynamic_slice_in_dim(line, lax.axis_index("dp") * n, n))
        return (
            env["outputs"],
            env["inputs"],
            g_query,
            small[0],
            g_key,
            g_value,
            small[2],
            g_output,
            small[5],
            small[3],
            small[4],
            g_inner,
            small[9],
            g_outer,
            small[8],
            small[6],
            small[7],
        )

    return body


def solution(mesh):
    rows = P("dp", "seq", None)
    matrix, vector = P("dp", None), P("dp")
    in_specs = (rows, rows, P("dp", "seq"), *[P()] * 15)
    out_specs = (
        rows,
        rows,
        matrix,
        vector,
        matrix,
        matrix,
        vector,
        matrix,
        vector,
        vector,
        vector,
        matrix,
        vector,
        matrix,
        vector,
        vector,
        vector,
    )
    body = make_body(dict(mesh.shape))
    return jax.shard_map(
        body, mesh=mesh, in_specs=in_specs, out_specs=out_specs, check_vma=False
    )
```

```python
import jax
import jax.numpy as jnp
from jax import lax
from jax.experimental import pallas as pl
from jax.experimental.pallas import tpu as pltpu
from jax.sharding import PartitionSpec as P

HD = 64
PAIR = 2 * HD
TILE = 256
EPSILON = 1e-05
F32, BF16 = jnp.float32, jnp.bfloat16
CORE, SEQ, DP, SLOTS = 0, 1, 2, 3
TABLE = 16
SCALE = 3e9
ORDER = (
    "ho", "hm", "go", "co", "gi", "fb", "ao", "o", "am", "o", "gr", "i", "r", "ib", "i", "o", "r",
    "i", "o", "ci", "r", "fo", "i", "r", "fi", "fr",
)
OUTER, INNER, REST = ((0, 1, 2), (1, 0, 2)), ((2, 0, 1), (1, 2, 0)), ((0, 1, 2), (1, 0, 2))


def nn(a, b):
    return lax.dot_general(a, b, (((1,), (0,)), ((), ())), preferred_element_type=F32)


def nt(a, b):
    return lax.dot_general(a, b, (((1,), (1,)), ((), ())), preferred_element_type=F32)


def tn(a, b):
    return lax.dot_general(a, b, (((0,), (0,)), ((), ())), preferred_element_type=F32)


def like(shape, dtype=BF16):
    return jax.ShapeDtypeStruct(shape, dtype)


def call(kernel, name, info, ins, outs, us, mb=14, after=(), hbm=0, scratch=()):
    n, skip = len(ins), len(after)

    def run(info_ref, *refs):
        kernel(info_ref, *refs[:n], *refs[n + skip :])

    return pl.pallas_call(
        run,
        in_specs=[pl.BlockSpec(memory_space=pltpu.SMEM)]
        + [pl.BlockSpec(memory_space=pltpu.VMEM)] * (n - hbm)
        + [pl.BlockSpec(memory_space=pltpu.HBM)] * hbm
        + [pl.BlockSpec(memory_space=pl.ANY)] * skip,
        out_shape=outs,
        scratch_shapes=list(scratch),
        compiler_params=pltpu.CompilerParams(vmem_limit_bytes=mb * 1024 * 1024),
        cost_estimate=pl.CostEstimate(
            flops=int(us * SCALE), bytes_accessed=1, transcendentals=0
        ),
        name=name,
    )(info, *ins, *after)


def fetch(sources, targets, sems):
    copies = [pltpu.make_async_copy(a, b, sems.at[i]) for i, (a, b) in enumerate(zip(sources, targets))]
    for c in copies:
        c.start()
    return copies


def halves(value):
    lane = lax.broadcasted_iota(jnp.int32, value.shape, 1)
    zero = jnp.zeros_like(value)
    return jnp.where(lane < HD, value, zero), jnp.where(lane < HD, zero, value)


def standardize(v):
    mean = jnp.mean(v, axis=-1, keepdims=True)
    c = v - mean
    r = lax.rsqrt(jnp.mean(c * c, axis=-1, keepdims=True) + EPSILON)
    return c * r, r


def norm_back(e, n, r):
    return r * (e - jnp.mean(e, axis=-1, keepdims=True) - n * jnp.mean(e * n, axis=-1, keepdims=True))


def columns(width):
    return [slice(j, j + TILE) for j in range(0, width, TILE)]


def tiles_loop(width, each, body):
    def step(i, carry):
        for j in range(each):
            body(pl.ds(pl.multiple_of((i * each + j) * TILE, TILE), TILE))
        return carry

    lax.fori_loop(0, width // (TILE * each), step, 0)


def total(value):
    return jnp.sum(value, axis=0, keepdims=True)


def attention_kernel(
    info_ref, x0, x1, x2, x3, bq_ref, bv_ref, bo_ref, gain_ref, shift_ref, wq_hbm, wk_hbm, wv_hbm, wo_hbm,
    x_ref, q_ref, k_ref, v_ref, p_ref, ctx_ref, n_ref, r_ref, low_ref,
    wq_ref, wk_ref, wv_ref, wo_ref, sems,
):
    rows, width = x_ref.shape
    block = x0.shape[0]
    copies = fetch((wq_hbm, wk_hbm, wv_hbm, wo_hbm), (wq_ref, wk_ref, wv_ref, wo_ref), sems)
    for i, part in enumerate((x0, x1, x2, x3)):
        x_ref[i * block : (i + 1) * block, :] = part[...]
    x = x_ref[...]
    copies[0].wait()
    for at in columns(width):
        q = (nn(x, wq_ref[:, at]) + bq_ref[:, at].astype(F32)).astype(BF16)
        q_ref[:, at] = q * jnp.asarray(HD ** -0.5, BF16)
    copies[1].wait()
    for at in columns(width):
        k_ref[:, at] = nn(x, wk_ref[:, at]).astype(BF16)
    copies[2].wait()
    for at in columns(width):
        v_ref[:, at] = (nn(x, wv_ref[:, at]) + bv_ref[:, at].astype(F32)).astype(BF16)
    def pair(p):
        at = pl.ds(pl.multiple_of(p * PAIR, PAIR), PAIR)
        q, k, v = q_ref[:, at], k_ref[:, at], v_ref[:, at]
        vt = v.astype(F32).T.astype(BF16)
        out = []
        for i, kh in enumerate(halves(k)):
            s = nt(kh, q)
            e = jnp.exp(s - jnp.max(s, axis=0, keepdims=True))
            w = (e * (1.0 / total(e))).astype(BF16)
            p_ref[2 * p + i] = w
            out.append(nn(vt[i * HD : (i + 1) * HD], w))
        ctx_ref[:, at] = jnp.concatenate(out, axis=0).T.astype(BF16)

    def step(i, carry):
        for j in range(3):
            pair(3 * i + j)
        return carry

    lax.fori_loop(0, width // PAIR // 3, step, 0)
    copies[3].wait()
    v1 = jnp.concatenate([nn(ctx_ref[...], wo_ref[:, at]) for at in columns(width)], axis=1)
    v1 = x_ref[...].astype(F32) + (v1 + bo_ref[...].astype(F32))
    n, r = standardize(v1)
    n_ref[...] = n
    r_ref[...] = r
    low_ref[...] = (n * gain_ref[...].astype(F32) + shift_ref[...].astype(F32)).astype(BF16)


def hidden_kernel(info_ref, low_ref, w_ref, b_ref, act_ref, slope_ref):
    def tile(at):
        h = nn(low_ref[...], w_ref[:, at]) + b_ref[:, at].astype(F32)
        z = h * 0.7071067811865476
        phi = 0.5 + 0.5 * lax.erf(z)
        bell = jnp.exp2(z * z * -1.4426950408889634)
        act_ref[:, at] = (h * phi).astype(BF16)
        slope_ref[:, at] = (phi + z * bell * 0.5641895835477563).astype(BF16)

    tiles_loop(w_ref.shape[1], 3, tile)


def split_store(core, value, mine_ref, other_ref):
    half = value.shape[1] // 2
    mine_ref[...] = jnp.where(core == 0, value[:, :half], value[:, half:])
    other_ref[...] = jnp.where(core == 0, value[:, half:], value[:, :half])


def branch_kernel(
    info_ref, act_ref, w_ref, b_ref, n_ref, gain1_ref, shift1_ref, gain_ref, shift_ref, c0, c1, c2, c3,
    o0, o1, o2, o3, mid_ref, low_ref, mine_ref, other_ref, sums_ref,
):
    width = mid_ref.shape[1]
    normed = n_ref[...] * gain1_ref[...].astype(F32) + shift1_ref[...].astype(F32)
    branch = jnp.concatenate([nn(act_ref[...], w_ref[:, at]) for at in columns(width)], axis=1)
    n, r = standardize(normed + (branch + b_ref[...].astype(F32)))
    gain = gain_ref[...].astype(F32)
    out = (n * gain + shift_ref[...].astype(F32)).astype(BF16)
    for i, ref in enumerate((o0, o1, o2, o3)):
        ref[...] = out[i * ref.shape[0] : (i + 1) * ref.shape[0]]
    go = jnp.concatenate([c[...] for c in (c0, c1, c2, c3)]).astype(F32)
    mid = norm_back(go * gain, n, r)
    mid_ref[...] = mid
    low = mid.astype(BF16)
    low_ref[...] = low
    split_store(info_ref[CORE], low, mine_ref, other_ref)
    sums_ref[0:1] = total(go * n)
    sums_ref[1:2] = total(go)
    sums_ref[2:3] = total(low.astype(F32))


def hidden_back_kernel(flip):
    def kernel(info_ref, low_ref, w_ref, slope_ref, out_ref, sums_ref):
        half = out_ref.shape[1]
        core = info_ref[CORE]
        first = ((1 - core) if flip else core) * half
        for to in columns(half):
            at = pl.ds(pl.multiple_of(first + to.start, TILE), TILE)
            g = (nt(low_ref[...], w_ref[at, :]) * slope_ref[:, at].astype(F32)).astype(BF16)
            out_ref[:, to] = g
            sums_ref[:, to] = total(g.astype(F32))

    return kernel


def first_back_kernel(
    info_ref, gm_ref, go_ref, w_ref, mid_ref, n_ref, r_ref, gain_ref, wo_ref,
    sum_ref, gctx_ref, mine_ref, other_ref, sums_ref,
):
    width, half = mid_ref.shape[1], gm_ref.shape[1]
    core = info_ref[CORE]
    mine = pl.ds(pl.multiple_of(core * half, half), half)
    other = pl.ds(pl.multiple_of((1 - core) * half, half), half)
    gn = jnp.concatenate(
        [nt(gm_ref[...], w_ref[at, mine]) + nt(go_ref[...], w_ref[at, other]) for at in columns(width)], axis=1
    )
    gn = gn + mid_ref[...]
    n = n_ref[...]
    gs = norm_back(gn * gain_ref[...].astype(F32), n, r_ref[...])
    sum_ref[...] = gs
    low = gs.astype(BF16)
    split_store(core, low, mine_ref, other_ref)
    sums_ref[0:1] = total(gn * n)
    sums_ref[1:2] = total(gn)
    sums_ref[2:3] = total(low.astype(F32))
    for at in columns(width):
        gctx_ref[:, at] = nt(low, wo_ref[at, :]).astype(BF16)


def attention_back_kernel(flip):
    def kernel(info_ref, q_ref, k_ref, v_ref, p_ref, g_ref, out_ref, sums_ref):
        rows, width = q_ref.shape
        per = width // PAIR // 2
        core = info_ref[CORE]
        first = ((1 - core) if flip else core) * per

        def pair(p, carry):
            at = pl.ds(pl.multiple_of((first + p) * PAIR, PAIR), PAIR)
            to = pl.ds(pl.multiple_of(p * PAIR, PAIR), PAIR)
            q, k, v, g = q_ref[:, at], k_ref[:, at], v_ref[:, at], g_ref[:, at]
            kt = k.astype(F32).T.astype(BF16)
            gk = jnp.zeros((rows, PAIR), F32)
            gv = jnp.zeros((rows, PAIR), F32)
            gq = []
            for i, (qh, vh, gh) in enumerate(zip(halves(q), halves(v), halves(g))):
                w = p_ref[2 * (first + p) + i]
                w32 = w.astype(F32)
                prod = w32 * nt(vh, g)
                gs = (prod - w32 * total(prod)).astype(BF16)
                gk = gk + nn(gs, qh)
                gv = gv + nn(w, gh)
                gq.append(nn(kt[i * HD : (i + 1) * HD], gs))
            gq = jnp.concatenate(gq, axis=0).T * HD ** -0.5
            for i, value in enumerate((gq, gk, gv)):
                value = value.astype(BF16)
                out_ref[i, :, to] = value
                sums_ref[i : i + 1, to] = total(value.astype(F32))
            return carry

        lax.fori_loop(0, per, pair, 0)

    return kernel


def input_back_kernel(info_ref, gm_ref, go_ref, sum_ref, wq_hbm, wk_hbm, wv_hbm, o0, o1, o2, o3, wq_ref, wk_ref, wv_ref, sems):
    half = gm_ref.shape[2]
    copies = fetch((wq_hbm, wk_hbm, wv_hbm), (wq_ref, wk_ref, wv_ref), sems)
    core = info_ref[CORE]
    mine = pl.ds(pl.multiple_of(core * half, half), half)
    other = pl.ds(pl.multiple_of((1 - core) * half, half), half)
    tiles = columns(sum_ref.shape[1])
    values = [sum_ref[:, at] for at in tiles]
    for i, w in enumerate((wq_ref, wk_ref, wv_ref)):
        copies[i].wait()
        for j, at in enumerate(tiles):
            values[j] = values[j] + nt(gm_ref[i], w[at, mine]) + nt(go_ref[i], w[at, other])
    for value, at in zip(values, tiles):
        value = value.astype(BF16)
        for i, ref in enumerate((o0, o1, o2, o3)):
            ref[:, at] = value[i * ref.shape[0] : (i + 1) * ref.shape[0]]


def place(info_ref, base, rows, buf_ref, keep_ref, send_ref):
    slots = buf_ref.shape[0] // rows
    for ref, first in ((keep_ref, base), (send_ref, base + slots // 2)):

        def copy(slot, carry):
            at = pl.ds(pl.multiple_of(info_ref[first + slot] * rows, 16), rows)
            ref[pl.ds(pl.multiple_of(slot * rows, 16), rows), :] = buf_ref[at, :]
            return carry

        lax.fori_loop(0, slots // 2, copy, 0)


def outer_kernel(base, rows):
    def kernel(info_ref, la, lb, ra, rb, keep_ref, send_ref, buf_ref):
        def tile(at):
            buf_ref[at, :] = (tn(la[:, at], ra[...]) + tn(lb[:, at], rb[...])).astype(BF16)

        tiles_loop(la.shape[1], 3, tile)
        place(info_ref, base, rows, buf_ref, keep_ref, send_ref)

    return kernel


def inner_kernel(base, rows):
    def kernel(info_ref, la, lb, ra, rb, keep_ref, send_ref, buf_ref):
        for at in columns(ra.shape[1]):
            buf_ref[:, at] = (tn(la[...], ra[:, at]) + tn(lb[...], rb[:, at])).astype(BF16)
        place(info_ref, base, rows, buf_ref, keep_ref, send_ref)

    return kernel


def fill_table(info_ref, table_ref, s0m, s0o, s1, s2, sim, sio):
    half = s0m.shape[1]
    core = info_ref[CORE]
    own = pl.ds(pl.multiple_of(core * half, half), half)
    others = pl.ds(pl.multiple_of((1 - core) * half, half), half)
    table_ref[...] = jnp.zeros_like(table_ref)
    table_ref[0:3, own] = s0m[...]
    table_ref[0:3, others] = s0o[...]
    table_ref[3:6] = s1[...]
    table_ref[6:9] = s2[...]
    per = sim.shape[1] // half
    for part, which in ((sim, core), (sio, 1 - core)):
        for i in range(per):
            flat = which * per + i
            at = pl.ds(pl.multiple_of(lax.rem(flat, 2) * half, half), half)
            table_ref[pl.ds(9 + lax.div(flat, 2), 1), at] = part[:, i * half : (i + 1) * half]


def rest_kernel(base, rows):
    def kernel(
        info_ref, xa, xb, ca, cb, ga, gb, oa, ob, s0m, s0o, s1, s2, sim, sio, keep_ref, send_ref, table_ref, buf_ref
    ):
        half = s0m.shape[1]
        slots = xa.shape[1] // rows
        for i in range(4):
            la, lb, ra, rb = (xa, xb, ga.at[i], gb.at[i]) if i < 3 else (ca, cb, oa, ob)
            buf_ref[i] = (tn(la[...], ra[...]) + tn(lb[...], rb[...])).astype(BF16)
            for slot in range(slots):
                chunk = buf_ref[i, pl.ds(pl.multiple_of(info_ref[base + slot] * rows, 16), rows), :]
                ref, to = (keep_ref, slot) if slot < slots // 2 else (send_ref, slot - slots // 2)
                ref[(4 * to + i) * rows : (4 * to + i + 1) * rows, :] = chunk
        fill_table(info_ref, table_ref, s0m, s0o, s1, s2, sim, sio)
        at = keep_ref.shape[0]
        for i in range(2):
            send_ref[at + i * TABLE : at + (i + 1) * TABLE] = table_ref[:, i * half : (i + 1) * half].astype(BF16)

    return kernel


def stage_kernel(low, high, out_dtype, tables):
    def kernel(info_ref, *refs):
        ins, out_ref = refs[:-1], refs[-1]
        if tables:
            sent_ref, ins = ins[-1], ins[:-1]
        value = ins[0][low:high].astype(F32)
        for ref in ins[1:]:
            value = value + ref[low:high].astype(F32)
        out_ref[0 : high - low] = value.astype(out_dtype)
        if tables:
            rows = sent_ref.shape[0]
            value = sent_ref[rows - 2 * TABLE :].astype(F32) + ins[-1][rows - 2 * TABLE :].astype(F32)
            out_ref[high - low :] = value.astype(out_dtype)

    return kernel


def deal_kernel(info_ref, in_hbm, *refs):
    outs, sems = refs[:-1], refs[-1]
    for c in fetch([in_hbm.at[info_ref[SEQ] ^ k] for k in range(len(outs))], outs, sems):
        c.wait()


def collect_kernel(info_ref, *refs):
    for k, part in enumerate(refs[:-1]):
        refs[-1][info_ref[SEQ] ^ k] = part[...]


def finish_kernel(part, tables):
    def kernel(info_ref, *refs):
        quarters, outs = refs[:4], refs[4:]
        core, ybit = info_ref[CORE], info_ref[SEQ] // 2
        half = quarters[0].shape[1]
        if tables:
            outs, small_ref, wide_ref = outs[:-2], outs[-2], outs[-1]
        for i, ref in enumerate(quarters):
            row = pl.multiple_of((ybit ^ (i & 1)) * part, 8)
            column = pl.multiple_of((core ^ (i >> 1)) * half, 128)
            for j, out_ref in enumerate(outs):
                out_ref[pl.ds(row, part), pl.ds(column, half)] = ref[j * part : (j + 1) * part].astype(F32)
        if tables:
            at = len(outs) * part
            table = [
                quarters[0][at + i * TABLE : at + (i + 1) * TABLE].astype(F32)
                + quarters[2][at + i * TABLE : at + (i + 1) * TABLE].astype(F32)
                for i in range(2)
            ]
            d = info_ref[DP]
            lanes = 2 * half
            step = 2 * part
            rolled = pltpu.roll(jnp.concatenate(table, axis=1), lax.rem(lanes - d * step, lanes), 1)
            small_ref[...] = rolled[:, : small_ref.shape[1]]
            per = wide_ref.shape[1]
            count = lanes // per
            for row in range(TABLE - 9):
                for k in range(count):
                    line = jnp.concatenate([t[9 + row : 10 + row] for t in table], axis=1)

                    @pl.when(d == row * count + k)
                    def _():
                        wide_ref[...] = line[:, k * per : (k + 1) * per]

    return kernel


def swap(value, axis, size, bit):
    return lax.ppermute(value, axis, [(i, i ^ bit) for i in range(size)])


def make_body(sizes):
    size, dp = sizes["seq"], sizes["dp"]
    nbits = dp.bit_length()
    chunks = 2 * dp
    rest_bits = list(range(3, nbits))
    orders = {
        name: [[*bits, *rest_bits] for bits in order]
        for name, order in (("outer", OUTER), ("inner", INNER), ("rest", REST))
    }
    bases = {name: SLOTS + i * chunks for i, name in enumerate(orders)}

    def my_bit(axis, bit):
        return (lax.axis_index(axis) & bit) // bit

    def pair(value):
        return swap(value, "seq", size, 1)

    def exchange(value, bits):
        moves = []
        for d in range(dp):
            for s in range(size):
                bit = bits[s % 2]
                to = (d, s ^ 2) if bit == 0 else (d ^ (1 << (bit - 1)), s)
                moves.append((d * size + s, to[0] * size + to[1]))
        return lax.ppermute(value, ("dp", "seq"), moves)

    def chunk_table(me, core, order):
        slot = jnp.arange(chunks, dtype=jnp.int32)
        rel = [sum(((slot >> (nbits - 1 - s)) & 1) << bit for s, bit in enumerate(bits)) for bits in order]
        return jnp.where(core == 0, rel[0], rel[1]) ^ me

    class Halving:
        def __init__(self, info, keep, send, name, part, tables=False):
            self.info, self.keep, self.send, self.name, self.part = info, keep, send, name, part
            self.tables, self.got, self.left, self.stage = tables, [], chunks // 2, 0
            self.move()

        def move(self):
            first, second = orders[self.name]
            self.got.append(exchange(self.send, (first[self.stage], second[self.stage])))

        def step(self, *after):
            part, n = self.part, self.left
            last = self.stage == nbits - 1
            low, high = (0, part) if last else (n // 2 * part, n * part)
            ins = [self.keep, *self.got] + ([self.send] if self.tables else [])
            shape = like((high - low + (2 * TABLE if self.tables else 0), self.keep.shape[1]))
            self.send = call(
                stage_kernel(low, high, BF16, self.tables),
                f"{self.name}{self.stage}", self.info, ins, shape, 1, after=after,
            )
            self.left, self.stage = n // 2, self.stage + 1
            if not last:
                self.move()
            return self.send

    def spread(value, bit):
        other = swap(value, "seq", size, bit)
        first = my_bit("seq", bit) == 0
        return jnp.where(first, value, other), jnp.where(first, other, value)

    def plain_halving(value, order, me, core):
        kept = [jnp.take(value, chunk_table(me, core, order), axis=0)]
        n = chunks
        for s in range(nbits):
            n //= 2
            send = sum(v[n : 2 * n].astype(F32) for v in kept).astype(BF16)
            kept.append(exchange(send, (order[0][s], order[1][s])))
        return sum(v[0].astype(F32) for v in kept).astype(BF16)

    def body(
        inputs,
        cotangent,
        masked,
        w_query,
        b_query,
        w_key,
        w_value,
        b_value,
        w_output,
        b_output,
        attn_gain,
        attn_shift,
        w_inner,
        b_inner,
        w_outer,
        b_outer,
        ffn_gain,
        ffn_shift,
    ):
        shape = inputs.shape
        count, block, width = shape
        rows, wide, half = count * block, w_inner.shape[1], width // 2
        assert count == size == 4
        seq = lax.axis_index("seq")
        core, ybit = my_bit("seq", 1), my_bit("seq", 2)
        me = lax.axis_index("dp") * 2 + ybit
        info = jnp.concatenate(
            [jnp.stack([core, seq, lax.axis_index("dp")])] + [chunk_table(me, core, order) for order in orders.values()]
        ).astype(jnp.int32)
        row = lambda v: v.reshape(1, -1)
        full = like((rows, width))

        part_o, part_i = wide // dp // 2, width // dp // 2
        fast = nbits == 4 and part_i % 16 == 0 and (2 * part_o) % 128 == 0 and width % (2 * part_o) == 0
        blocks = [like((block, width))] * size

        def gather(value, name):
            parts = call(
                deal_kernel, name, info, [value], blocks, 1, hbm=1,
                scratch=[pltpu.SemaphoreType.DMA((size,))],
            )
            return [swap(v, "seq", size, k) if k else v for k, v in enumerate(parts)]

        def scatter(parts):
            return [parts[0]] + [swap(parts[k], "seq", size, k) for k in range(1, size)]

        def collect(parts, name, *after):
            return call(collect_kernel, name, info, parts, like(shape), 1, after=after)

        x_parts = gather(inputs, "deal_inputs")
        cot_parts = gather(cotangent * masked[:, :, None].astype(BF16), "deal_cotangent")
        square = pltpu.VMEM((width, width), BF16)
        x, q, k, v, p, ctx, n1, r1, low1 = call(
            attention_kernel, "attention", info,
            [*x_parts, row(b_query), row(b_value), row(b_output), row(attn_gain), row(attn_shift),
             w_query, w_key, w_value, w_output],
            (full, full, full, full, like((width // HD, rows, rows)), full, like((rows, width), F32),
             like((rows, 1), F32), full),
            13, 20, hbm=4, scratch=[square] * 4 + [pltpu.SemaphoreType.DMA((4,))],
        )
        x_other, ctx_other, low_other = pair(x), pair(ctx), pair(low1)
        act, slope = call(
            hidden_kernel, "hidden", info, [low1, w_inner, row(b_inner)],
            (like((rows, wide)), like((rows, wide))), 9, after=cot_parts,
        )
        act_other = pair(act)
        *out, mid, gb, gb_mine, gb_send, sums2 = call(
            branch_kernel, "branch", info,
            [act, w_outer, row(b_outer), n1, row(attn_gain), row(attn_shift), row(ffn_gain), row(ffn_shift),
             *cot_parts],
            (*blocks, like((rows, width), F32), full, like((rows, half)), like((rows, half)), like((3, width), F32)),
            4, 16,
        )
        gb_other = pair(gb_send)
        out = scatter(out)
        env, groups, token = {}, {}, []

        def buffers(part, columns, extra=0):
            return like((dp * part, columns)), like((dp * part + extra, columns))

        def product(a, b):
            return (tn(a[0], b[0]) + tn(a[1], b[1])).astype(BF16)

        def quarters(own):
            other = swap(own, "seq", size, 2)
            return [own, other, pair(own), pair(other)]

        def hidden_back(name, flip):
            shapes = (like((rows, wide // 2)), like((1, wide // 2), F32))
            env["gh_" + name], env["sumi_" + name] = call(
                hidden_back_kernel(flip), "hidden_back_" + name, info, [gb, w_outer, slope], shapes, 3,
                after=[*token, act_other] if flip else [*token, gb_other],
            )
            if flip:
                env["gh_pair"] = pair(env["gh_other"])
            return env["sumi_" + name]

        def grad_outer():
            keep, send = call(
                outer_kernel(bases["outer"], part_o), "grad_outer", info, [act, act_other, gb_mine, gb_other],
                buffers(part_o, half), 5, after=token, scratch=[pltpu.VMEM((wide, half), BF16)],
            )
            groups["o"] = Halving(info, keep, send, "outer", part_o)
            return send

        def grad_inner():
            keep, send = call(
                inner_kernel(bases["inner"], part_i), "grad_inner", info,
                [low1, low_other, env["gh_mine"], env["gh_pair"]], buffers(part_i, wide // 2), 4, after=token,
                scratch=[pltpu.VMEM((width, wide // 2), BF16)],
            )
            groups["i"] = Halving(info, keep, send, "inner", part_i)
            return send

        def first_back():
            env["gsum"], env["gctx"], env["ga"], ga_send, env["sums1"] = call(
                first_back_kernel, "first_back", info,
                [env["gh_mine"], env["gh_other"], w_inner, mid, n1, r1, row(attn_gain), w_output],
                (like((rows, width), F32), full, like((rows, half)), like((rows, half)), like((3, width), F32)),
                6, after=token,
            )
            env["ga_pair"] = pair(ga_send)
            return env["sums1"]

        def attention_back(name, flip):
            env["g3_" + name], env["sums0_" + name] = call(
                attention_back_kernel(flip), "attention_back_" + name, info, [q, k, v, p, env["gctx"]],
                (like((3, rows, half)), like((3, half), F32)), 1, after=token,
            )
            if flip:
                env["g3_pair"] = pair(env["g3_other"])
            return env["sums0_" + name]

        def grad_rest():
            sums = [env["sums0_mine"], env["sums0_other"], env["sums1"], sums2, env["sumi_mine"], env["sumi_other"]]
            keep, send, table = call(
                rest_kernel(bases["rest"], part_i), "grad_rest", info,
                [x, x_other, ctx, ctx_other, env["g3_mine"], env["g3_pair"], env["ga"], env["ga_pair"], *sums],
                (*buffers(4 * part_i, half, 2 * TABLE), like((TABLE, width), F32)), 1, after=token,
                scratch=[pltpu.VMEM((4, width, half), BF16)],
            )
            groups["r"] = Halving(info, keep, send, "rest", 4 * part_i, True)
            return table

        def input_back():
            parts = call(
                input_back_kernel, "input_back", info,
                [env["g3_mine"], env["g3_other"], env["gsum"], w_query, w_key, w_value], blocks, 2, after=token,
                hbm=3, mb=52, scratch=[square] * 3 + [pltpu.SemaphoreType.DMA((3,))],
            )
            env["back"] = scatter(parts)
            return parts[0]

        def step(name):
            own = groups[name].step(*token)
            if groups[name].stage == nbits:
                env["q" + name] = quarters(own)
            return own

        def finish_group(name, part, columns, title):
            env["g" + name] = call(
                finish_kernel(part, False), title, info, env["q" + name], like((2 * part, columns), F32), 1, after=token
            )
            return env["g" + name]

        def finish_rest():
            matrix, thin = like((2 * part_i, width), F32), like((TABLE, 128), F32)
            env["gr"] = call(
                finish_kernel(part_i, True), "finish_rest", info, env["qr"],
                (matrix, matrix, matrix, matrix, thin, like((1, 2 * part_o), F32)), 1, after=token,
            )
            return env["gr"][4]

        def collect(name, parts):
            env[name] = call(collect_kernel, "collect_" + name, info, parts, like(shape), 1, after=token)
            return env[name]

        tasks = {
            "ho": lambda: hidden_back("other", True),
            "hm": lambda: hidden_back("mine", False),
            "go": grad_outer,
            "gi": grad_inner,
            "fb": first_back,
            "ao": lambda: attention_back("other", True),
            "am": lambda: attention_back("mine", False),
            "gr": grad_rest,
            "ib": input_back,
            "o": lambda: step("o"),
            "i": lambda: step("i"),
            "r": lambda: step("r"),
            "fo": lambda: finish_group("o", part_o, width, "finish_outer"),
            "fi": lambda: finish_group("i", part_i, wide, "finish_inner"),
            "fr": finish_rest,
            "co": lambda: collect("outputs", out),
            "ci": lambda: collect("inputs", env["back"]),
        }
        for name in ORDER:
            if fast or name in ("ho", "hm", "fb", "ao", "am", "ib", "co", "ci"):
                token = [tasks[name]()]

        def finish(value, group, part, columns):
            value = jnp.stack(spread(value.reshape(group, part, columns // 2), 2), axis=1)
            value = value.reshape(group, 2 * part, columns // 2)
            return jnp.concatenate(spread(value, 1), axis=-1).astype(F32)

        if fast:
            g_outer, g_inner = env["go"], env["gi"]
            g_query, g_key, g_value, g_output, small, wide_row = env["gr"]
            small = [small[i, : 2 * part_i] for i in range(9)] + [wide_row[0]]
        else:
            me_core = (me, core)

            def cut(value, part):
                return value.reshape(chunks, part, value.shape[1])

            own_o = plain_halving(
                cut(product((act, act_other), (gb_mine, gb_other)), part_o), orders["outer"], *me_core
            )
            own_i = plain_halving(
                cut(product((low1, low_other), (env["gh_mine"], env["gh_pair"])), part_i), orders["inner"], *me_core
            )
            four = [product((x, x_other), (env["g3_mine"][i], env["g3_pair"][i])) for i in range(3)]
            four.append(product((ctx, ctx_other), (env["ga"], env["ga_pair"])))
            four = jnp.stack([cut(f, part_i) for f in four], axis=1)
            own_r = plain_halving(four, orders["rest"], *me_core)

            def both(mine, other):
                return jnp.where(
                    core == 0,
                    jnp.concatenate([mine, other], axis=1),
                    jnp.concatenate([other, mine], axis=1),
                )

            table = jnp.concatenate(
                [
                    both(env["sums0_mine"], env["sums0_other"]),
                    env["sums1"],
                    sums2,
                    both(env["sumi_mine"], env["sumi_other"]).reshape(-1, width),
                ]
            )
            table = lax.psum(table, ("dp", "seq"))
            (g_outer,) = finish(own_o, 1, part_o, width)
            (g_inner,) = finish(own_i, 1, part_i, wide)
            g_query, g_key, g_value, g_output = finish(own_r, 4, part_i, width)
            lines = [table[i] for i in range(9)] + [table[9:].reshape(-1)]
            small = []
            for line in lines:
                n = line.shape[0] // dp
                small.append(lax.dynamic_slice_in_dim(line, lax.axis_index("dp") * n, n))
        return (
            env["outputs"],
            env["inputs"],
            g_query,
            small[0],
            g_key,
            g_value,
            small[2],
            g_output,
            small[5],
            small[3],
            small[4],
            g_inner,
            small[9],
            g_outer,
            small[8],
            small[6],
            small[7],
        )

    return body


def solution(mesh):
    rows = P("dp", "seq", None)
    matrix, vector = P("dp", None), P("dp")
    in_specs = (rows, rows, P("dp", "seq"), *[P()] * 15)
    out_specs = (
        rows,
        rows,
        matrix,
        vector,
        matrix,
        matrix,
        vector,
        matrix,
        vector,
        vector,
        vector,
        matrix,
        vector,
        matrix,
        vector,
        vector,
        vector,
    )
    body = make_body(dict(mesh.shape))
    return jax.shard_map(
        body, mesh=mesh, in_specs=in_specs, out_specs=out_specs, check_vma=False
    )
```

```python
import jax
import jax.numpy as jnp
from jax import lax
from jax.experimental import pallas as pl
from jax.experimental.pallas import tpu as pltpu
from jax.sharding import PartitionSpec as P

HD = 64
PAIR = 2 * HD
TILE = 256
EPSILON = 1e-05
F32, BF16 = jnp.float32, jnp.bfloat16
CORE, SEQ, DP, SLOTS = 0, 1, 2, 3
TABLE = 16
SCALE = 3e9
ORDER = (
    "ho", "hm", "go", "co", "gi", "fb", "ao", "o", "am", "o", "gr", "i", "r", "ib", "i", "o", "r",
    "i", "o", "ci", "r", "fo", "i", "r", "fi", "fr",
)
OUTER, INNER, REST = ((0, 1, 2), (1, 0, 2)), ((2, 0, 1), (1, 2, 0)), ((0, 1, 2), (1, 0, 2))


def nn(a, b):
    return lax.dot_general(a, b, (((1,), (0,)), ((), ())), preferred_element_type=F32)


def nt(a, b):
    return lax.dot_general(a, b, (((1,), (1,)), ((), ())), preferred_element_type=F32)


def tn(a, b):
    return lax.dot_general(a, b, (((0,), (0,)), ((), ())), preferred_element_type=F32)


def like(shape, dtype=BF16):
    return jax.ShapeDtypeStruct(shape, dtype)


def call(kernel, name, info, ins, outs, us, mb=14, after=(), hbm=0, scratch=()):
    n, skip = len(ins), len(after)

    def run(info_ref, *refs):
        kernel(info_ref, *refs[:n], *refs[n + skip :])

    return pl.pallas_call(
        run,
        in_specs=[pl.BlockSpec(memory_space=pltpu.SMEM)]
        + [pl.BlockSpec(memory_space=pltpu.VMEM)] * (n - hbm)
        + [pl.BlockSpec(memory_space=pltpu.HBM)] * hbm
        + [pl.BlockSpec(memory_space=pl.ANY)] * skip,
        out_shape=outs,
        scratch_shapes=list(scratch),
        compiler_params=pltpu.CompilerParams(vmem_limit_bytes=mb * 1024 * 1024),
        cost_estimate=pl.CostEstimate(
            flops=int(us * SCALE), bytes_accessed=1, transcendentals=0
        ),
        name=name,
    )(info, *ins, *after)


def fetch(sources, targets, sems):
    copies = [pltpu.make_async_copy(a, b, sems.at[i]) for i, (a, b) in enumerate(zip(sources, targets))]
    for c in copies:
        c.start()
    return copies


def halves(value):
    lane = lax.broadcasted_iota(jnp.int32, value.shape, 1)
    zero = jnp.zeros_like(value)
    return jnp.where(lane < HD, value, zero), jnp.where(lane < HD, zero, value)


def standardize(v):
    mean = jnp.mean(v, axis=-1, keepdims=True)
    c = v - mean
    r = lax.rsqrt(jnp.mean(c * c, axis=-1, keepdims=True) + EPSILON)
    return c * r, r


def norm_back(e, n, r):
    return r * (e - jnp.mean(e, axis=-1, keepdims=True) - n * jnp.mean(e * n, axis=-1, keepdims=True))


def columns(width):
    return [slice(j, j + TILE) for j in range(0, width, TILE)]


def tiles_loop(width, each, body):
    def step(i, carry):
        for j in range(each):
            body(pl.ds(pl.multiple_of((i * each + j) * TILE, TILE), TILE))
        return carry

    lax.fori_loop(0, width // (TILE * each), step, 0)


def total(value):
    return jnp.sum(value, axis=0, keepdims=True)


def attention_kernel(
    info_ref, x0, x1, x2, x3, bq_ref, bv_ref, bo_ref, gain_ref, shift_ref, wq_hbm, wk_hbm, wv_hbm, wo_hbm,
    x_ref, q_ref, k_ref, v_ref, p_ref, ctx_ref, n_ref, r_ref, low_ref,
    wq_ref, wk_ref, wv_ref, wo_ref, sems,
):
    rows, width = x_ref.shape
    block = x0.shape[0]
    copies = fetch((wq_hbm, wk_hbm, wv_hbm, wo_hbm), (wq_ref, wk_ref, wv_ref, wo_ref), sems)
    for i, part in enumerate((x0, x1, x2, x3)):
        x_ref[i * block : (i + 1) * block, :] = part[...]
    x = x_ref[...]
    for c in copies[:3]:
        c.wait()

    def tile(at):
        q = (nn(x, wq_ref[:, at]) + bq_ref[:, at].astype(F32)).astype(BF16)
        q_ref[:, at] = q * jnp.asarray(HD ** -0.5, BF16)
        k_ref[:, at] = nn(x, wk_ref[:, at]).astype(BF16)
        v_ref[:, at] = (nn(x, wv_ref[:, at]) + bv_ref[:, at].astype(F32)).astype(BF16)

    tiles_loop(width, 1, tile)
    for p in range(width // PAIR):
        at = slice(p * PAIR, (p + 1) * PAIR)
        q, k, v = q_ref[:, at], k_ref[:, at], v_ref[:, at]
        vt = v.astype(F32).T.astype(BF16)
        out = []
        for i, kh in enumerate(halves(k)):
            s = nt(kh, q)
            e = jnp.exp(s - jnp.max(s, axis=0, keepdims=True))
            w = (e * (1.0 / total(e))).astype(BF16)
            p_ref[2 * p + i] = w
            out.append(nn(vt[i * HD : (i + 1) * HD], w))
        ctx_ref[:, at] = jnp.concatenate(out, axis=0).T.astype(BF16)
    copies[3].wait()
    v1 = jnp.concatenate([nn(ctx_ref[...], wo_ref[:, at]) for at in columns(width)], axis=1)
    v1 = x_ref[...].astype(F32) + (v1 + bo_ref[...].astype(F32))
    n, r = standardize(v1)
    n_ref[...] = n
    r_ref[...] = r
    low_ref[...] = (n * gain_ref[...].astype(F32) + shift_ref[...].astype(F32)).astype(BF16)


def hidden_kernel(info_ref, low_ref, w_ref, b_ref, act_ref, slope_ref):
    def tile(at):
        h = nn(low_ref[...], w_ref[:, at]) + b_ref[:, at].astype(F32)
        z = h * 0.7071067811865476
        phi = 0.5 + 0.5 * lax.erf(z)
        bell = jnp.exp2(z * z * -1.4426950408889634)
        act_ref[:, at] = (h * phi).astype(BF16)
        slope_ref[:, at] = (phi + z * bell * 0.5641895835477563).astype(BF16)

    tiles_loop(w_ref.shape[1], 3, tile)


def split_store(core, value, mine_ref, other_ref):
    half = value.shape[1] // 2
    mine_ref[...] = jnp.where(core == 0, value[:, :half], value[:, half:])
    other_ref[...] = jnp.where(core == 0, value[:, half:], value[:, :half])


def branch_kernel(
    info_ref, act_ref, w_ref, b_ref, n_ref, gain1_ref, shift1_ref, gain_ref, shift_ref, c0, c1, c2, c3,
    o0, o1, o2, o3, mid_ref, low_ref, mine_ref, other_ref, sums_ref,
):
    width = mid_ref.shape[1]
    normed = n_ref[...] * gain1_ref[...].astype(F32) + shift1_ref[...].astype(F32)
    branch = jnp.concatenate([nn(act_ref[...], w_ref[:, at]) for at in columns(width)], axis=1)
    n, r = standardize(normed + (branch + b_ref[...].astype(F32)))
    gain = gain_ref[...].astype(F32)
    out = (n * gain + shift_ref[...].astype(F32)).astype(BF16)
    for i, ref in enumerate((o0, o1, o2, o3)):
        ref[...] = out[i * ref.shape[0] : (i + 1) * ref.shape[0]]
    go = jnp.concatenate([c[...] for c in (c0, c1, c2, c3)]).astype(F32)
    mid = norm_back(go * gain, n, r)
    mid_ref[...] = mid
    low = mid.astype(BF16)
    low_ref[...] = low
    split_store(info_ref[CORE], low, mine_ref, other_ref)
    sums_ref[0:1] = total(go * n)
    sums_ref[1:2] = total(go)
    sums_ref[2:3] = total(low.astype(F32))


def hidden_back_kernel(flip):
    def kernel(info_ref, low_ref, w_ref, slope_ref, out_ref, sums_ref):
        half = out_ref.shape[1]
        core = info_ref[CORE]
        first = ((1 - core) if flip else core) * half
        for to in columns(half):
            at = pl.ds(pl.multiple_of(first + to.start, TILE), TILE)
            g = (nt(low_ref[...], w_ref[at, :]) * slope_ref[:, at].astype(F32)).astype(BF16)
            out_ref[:, to] = g
            sums_ref[:, to] = total(g.astype(F32))

    return kernel


def first_back_kernel(
    info_ref, gm_ref, go_ref, w_ref, mid_ref, n_ref, r_ref, gain_ref, wo_ref,
    sum_ref, gctx_ref, mine_ref, other_ref, sums_ref,
):
    width, half = mid_ref.shape[1], gm_ref.shape[1]
    core = info_ref[CORE]
    mine = pl.ds(pl.multiple_of(core * half, half), half)
    other = pl.ds(pl.multiple_of((1 - core) * half, half), half)
    gn = jnp.concatenate(
        [nt(gm_ref[...], w_ref[at, mine]) + nt(go_ref[...], w_ref[at, other]) for at in columns(width)], axis=1
    )
    gn = gn + mid_ref[...]
    n = n_ref[...]
    gs = norm_back(gn * gain_ref[...].astype(F32), n, r_ref[...])
    sum_ref[...] = gs
    low = gs.astype(BF16)
    split_store(core, low, mine_ref, other_ref)
    sums_ref[0:1] = total(gn * n)
    sums_ref[1:2] = total(gn)
    sums_ref[2:3] = total(low.astype(F32))
    for at in columns(width):
        gctx_ref[:, at] = nt(low, wo_ref[at, :]).astype(BF16)


def attention_back_kernel(flip):
    def kernel(info_ref, q_ref, k_ref, v_ref, p_ref, g_ref, out_ref, sums_ref):
        rows, width = q_ref.shape
        per = width // PAIR // 2
        core = info_ref[CORE]
        first = ((1 - core) if flip else core) * per

        def pair(p, carry):
            at = pl.ds(pl.multiple_of((first + p) * PAIR, PAIR), PAIR)
            to = pl.ds(pl.multiple_of(p * PAIR, PAIR), PAIR)
            q, k, v, g = q_ref[:, at], k_ref[:, at], v_ref[:, at], g_ref[:, at]
            kt = k.astype(F32).T.astype(BF16)
            gk = jnp.zeros((rows, PAIR), F32)
            gv = jnp.zeros((rows, PAIR), F32)
            gq = []
            for i, (qh, vh, gh) in enumerate(zip(halves(q), halves(v), halves(g))):
                w = p_ref[2 * (first + p) + i]
                w32 = w.astype(F32)
                prod = w32 * nt(vh, g)
                gs = (prod - w32 * total(prod)).astype(BF16)
                gk = gk + nn(gs, qh)
                gv = gv + nn(w, gh)
                gq.append(nn(kt[i * HD : (i + 1) * HD], gs))
            gq = jnp.concatenate(gq, axis=0).T * HD ** -0.5
            for i, value in enumerate((gq, gk, gv)):
                value = value.astype(BF16)
                out_ref[i, :, to] = value
                sums_ref[i : i + 1, to] = total(value.astype(F32))
            return carry

        lax.fori_loop(0, per, pair, 0)

    return kernel


def input_back_kernel(info_ref, gm_ref, go_ref, sum_ref, wq_hbm, wk_hbm, wv_hbm, o0, o1, o2, o3, wq_ref, wk_ref, wv_ref, sems):
    half = gm_ref.shape[2]
    copies = fetch((wq_hbm, wk_hbm, wv_hbm), (wq_ref, wk_ref, wv_ref), sems)
    core = info_ref[CORE]
    mine = pl.ds(pl.multiple_of(core * half, half), half)
    other = pl.ds(pl.multiple_of((1 - core) * half, half), half)
    tiles = columns(sum_ref.shape[1])
    values = [sum_ref[:, at] for at in tiles]
    for i, w in enumerate((wq_ref, wk_ref, wv_ref)):
        copies[i].wait()
        for j, at in enumerate(tiles):
            values[j] = values[j] + nt(gm_ref[i], w[at, mine]) + nt(go_ref[i], w[at, other])
    for value, at in zip(values, tiles):
        value = value.astype(BF16)
        for i, ref in enumerate((o0, o1, o2, o3)):
            ref[:, at] = value[i * ref.shape[0] : (i + 1) * ref.shape[0]]


def place(info_ref, base, rows, buf_ref, keep_ref, send_ref):
    slots = buf_ref.shape[0] // rows
    for ref, first in ((keep_ref, base), (send_ref, base + slots // 2)):

        def copy(slot, carry):
            at = pl.ds(pl.multiple_of(info_ref[first + slot] * rows, 16), rows)
            ref[pl.ds(pl.multiple_of(slot * rows, 16), rows), :] = buf_ref[at, :]
            return carry

        lax.fori_loop(0, slots // 2, copy, 0)


def outer_kernel(base, rows):
    def kernel(info_ref, la, lb, ra, rb, keep_ref, send_ref, buf_ref):
        def tile(at):
            buf_ref[at, :] = (tn(la[:, at], ra[...]) + tn(lb[:, at], rb[...])).astype(BF16)

        tiles_loop(la.shape[1], 3, tile)
        place(info_ref, base, rows, buf_ref, keep_ref, send_ref)

    return kernel


def inner_kernel(base, rows):
    def kernel(info_ref, la, lb, ra, rb, keep_ref, send_ref, buf_ref):
        def tile(at):
            buf_ref[:, at] = (tn(la[...], ra[:, at]) + tn(lb[...], rb[:, at])).astype(BF16)

        tiles_loop(ra.shape[1], 3, tile)
        place(info_ref, base, rows, buf_ref, keep_ref, send_ref)

    return kernel


def fill_table(info_ref, table_ref, s0m, s0o, s1, s2, sim, sio):
    half = s0m.shape[1]
    core = info_ref[CORE]
    own = pl.ds(pl.multiple_of(core * half, half), half)
    others = pl.ds(pl.multiple_of((1 - core) * half, half), half)
    table_ref[...] = jnp.zeros_like(table_ref)
    table_ref[0:3, own] = s0m[...]
    table_ref[0:3, others] = s0o[...]
    table_ref[3:6] = s1[...]
    table_ref[6:9] = s2[...]
    per = sim.shape[1] // half
    for part, which in ((sim, core), (sio, 1 - core)):
        for i in range(per):
            flat = which * per + i
            at = pl.ds(pl.multiple_of(lax.rem(flat, 2) * half, half), half)
            table_ref[pl.ds(9 + lax.div(flat, 2), 1), at] = part[:, i * half : (i + 1) * half]


def rest_kernel(base, rows):
    def kernel(
        info_ref, xa, xb, ca, cb, ga, gb, oa, ob, s0m, s0o, s1, s2, sim, sio, keep_ref, send_ref, table_ref, buf_ref
    ):
        half = s0m.shape[1]
        slots = xa.shape[1] // rows
        for i in range(4):
            la, lb, ra, rb = (xa, xb, ga.at[i], gb.at[i]) if i < 3 else (ca, cb, oa, ob)
            buf_ref[i] = (tn(la[...], ra[...]) + tn(lb[...], rb[...])).astype(BF16)
            for slot in range(slots):
                chunk = buf_ref[i, pl.ds(pl.multiple_of(info_ref[base + slot] * rows, 16), rows), :]
                ref, to = (keep_ref, slot) if slot < slots // 2 else (send_ref, slot - slots // 2)
                ref[(4 * to + i) * rows : (4 * to + i + 1) * rows, :] = chunk
        fill_table(info_ref, table_ref, s0m, s0o, s1, s2, sim, sio)
        at = keep_ref.shape[0]
        for i in range(2):
            send_ref[at + i * TABLE : at + (i + 1) * TABLE] = table_ref[:, i * half : (i + 1) * half].astype(BF16)

    return kernel


def stage_kernel(low, high, out_dtype, tables):
    def kernel(info_ref, *refs):
        ins, out_ref = refs[:-1], refs[-1]
        if tables:
            sent_ref, ins = ins[-1], ins[:-1]
        value = ins[0][low:high].astype(F32)
        for ref in ins[1:]:
            value = value + ref[low:high].astype(F32)
        out_ref[0 : high - low] = value.astype(out_dtype)
        if tables:
            rows = sent_ref.shape[0]
            value = sent_ref[rows - 2 * TABLE :].astype(F32) + ins[-1][rows - 2 * TABLE :].astype(F32)
            out_ref[high - low :] = value.astype(out_dtype)

    return kernel


def deal_kernel(info_ref, in_hbm, *refs):
    outs, sems = refs[:-1], refs[-1]
    for c in fetch([in_hbm.at[info_ref[SEQ] ^ k] for k in range(len(outs))], outs, sems):
        c.wait()


def collect_kernel(info_ref, *refs):
    for k, part in enumerate(refs[:-1]):
        refs[-1][info_ref[SEQ] ^ k] = part[...]


def finish_kernel(part, tables):
    def kernel(info_ref, *refs):
        quarters, outs = refs[:4], refs[4:]
        core, ybit = info_ref[CORE], info_ref[SEQ] // 2
        half = quarters[0].shape[1]
        if tables:
            outs, small_ref, wide_ref = outs[:-2], outs[-2], outs[-1]
        for i, ref in enumerate(quarters):
            row = pl.multiple_of((ybit ^ (i & 1)) * part, 8)
            column = pl.multiple_of((core ^ (i >> 1)) * half, 128)
            for j, out_ref in enumerate(outs):
                out_ref[pl.ds(row, part), pl.ds(column, half)] = ref[j * part : (j + 1) * part].astype(F32)
        if tables:
            at = len(outs) * part
            table = [
                quarters[0][at + i * TABLE : at + (i + 1) * TABLE].astype(F32)
                + quarters[2][at + i * TABLE : at + (i + 1) * TABLE].astype(F32)
                for i in range(2)
            ]
            d = info_ref[DP]
            lanes = 2 * half
            step = 2 * part
            rolled = pltpu.roll(jnp.concatenate(table, axis=1), lax.rem(lanes - d * step, lanes), 1)
            small_ref[...] = rolled[:, : small_ref.shape[1]]
            per = wide_ref.shape[1]
            count = lanes // per
            for row in range(TABLE - 9):
                for k in range(count):
                    line = jnp.concatenate([t[9 + row : 10 + row] for t in table], axis=1)

                    @pl.when(d == row * count + k)
                    def _():
                        wide_ref[...] = line[:, k * per : (k + 1) * per]

    return kernel


def swap(value, axis, size, bit):
    return lax.ppermute(value, axis, [(i, i ^ bit) for i in range(size)])


def make_body(sizes):
    size, dp = sizes["seq"], sizes["dp"]
    nbits = dp.bit_length()
    chunks = 2 * dp
    rest_bits = list(range(3, nbits))
    orders = {
        name: [[*bits, *rest_bits] for bits in order]
        for name, order in (("outer", OUTER), ("inner", INNER), ("rest", REST))
    }
    bases = {name: SLOTS + i * chunks for i, name in enumerate(orders)}

    def my_bit(axis, bit):
        return (lax.axis_index(axis) & bit) // bit

    def pair(value):
        return swap(value, "seq", size, 1)

    def exchange(value, bits):
        moves = []
        for d in range(dp):
            for s in range(size):
                bit = bits[s % 2]
                to = (d, s ^ 2) if bit == 0 else (d ^ (1 << (bit - 1)), s)
                moves.append((d * size + s, to[0] * size + to[1]))
        return lax.ppermute(value, ("dp", "seq"), moves)

    def chunk_table(me, core, order):
        slot = jnp.arange(chunks, dtype=jnp.int32)
        rel = [sum(((slot >> (nbits - 1 - s)) & 1) << bit for s, bit in enumerate(bits)) for bits in order]
        return jnp.where(core == 0, rel[0], rel[1]) ^ me

    class Halving:
        def __init__(self, info, keep, send, name, part, tables=False):
            self.info, self.keep, self.send, self.name, self.part = info, keep, send, name, part
            self.tables, self.got, self.left, self.stage = tables, [], chunks // 2, 0
            self.move()

        def move(self):
            first, second = orders[self.name]
            self.got.append(exchange(self.send, (first[self.stage], second[self.stage])))

        def step(self, *after):
            part, n = self.part, self.left
            last = self.stage == nbits - 1
            low, high = (0, part) if last else (n // 2 * part, n * part)
            ins = [self.keep, *self.got] + ([self.send] if self.tables else [])
            shape = like((high - low + (2 * TABLE if self.tables else 0), self.keep.shape[1]))
            self.send = call(
                stage_kernel(low, high, BF16, self.tables),
                f"{self.name}{self.stage}", self.info, ins, shape, 1, after=after,
            )
            self.left, self.stage = n // 2, self.stage + 1
            if not last:
                self.move()
            return self.send

    def spread(value, bit):
        other = swap(value, "seq", size, bit)
        first = my_bit("seq", bit) == 0
        return jnp.where(first, value, other), jnp.where(first, other, value)

    def plain_halving(value, order, me, core):
        kept = [jnp.take(value, chunk_table(me, core, order), axis=0)]
        n = chunks
        for s in range(nbits):
            n //= 2
            send = sum(v[n : 2 * n].astype(F32) for v in kept).astype(BF16)
            kept.append(exchange(send, (order[0][s], order[1][s])))
        return sum(v[0].astype(F32) for v in kept).astype(BF16)

    def body(
        inputs,
        cotangent,
        masked,
        w_query,
        b_query,
        w_key,
        w_value,
        b_value,
        w_output,
        b_output,
        attn_gain,
        attn_shift,
        w_inner,
        b_inner,
        w_outer,
        b_outer,
        ffn_gain,
        ffn_shift,
    ):
        shape = inputs.shape
        count, block, width = shape
        rows, wide, half = count * block, w_inner.shape[1], width // 2
        assert count == size == 4
        seq = lax.axis_index("seq")
        core, ybit = my_bit("seq", 1), my_bit("seq", 2)
        me = lax.axis_index("dp") * 2 + ybit
        info = jnp.concatenate(
            [jnp.stack([core, seq, lax.axis_index("dp")])] + [chunk_table(me, core, order) for order in orders.values()]
        ).astype(jnp.int32)
        row = lambda v: v.reshape(1, -1)
        full = like((rows, width))

        part_o, part_i = wide // dp // 2, width // dp // 2
        fast = nbits == 4 and part_i % 16 == 0 and (2 * part_o) % 128 == 0 and width % (2 * part_o) == 0
        blocks = [like((block, width))] * size

        def gather(value, name):
            parts = call(
                deal_kernel, name, info, [value], blocks, 1, hbm=1,
                scratch=[pltpu.SemaphoreType.DMA((size,))],
            )
            return [swap(v, "seq", size, k) if k else v for k, v in enumerate(parts)]

        def scatter(parts):
            return [parts[0]] + [swap(parts[k], "seq", size, k) for k in range(1, size)]

        def collect(parts, name, *after):
            return call(collect_kernel, name, info, parts, like(shape), 1, after=after)

        x_parts = gather(inputs, "deal_inputs")
        cot_parts = gather(cotangent * masked[:, :, None].astype(BF16), "deal_cotangent")
        square = pltpu.VMEM((width, width), BF16)
        x, q, k, v, p, ctx, n1, r1, low1 = call(
            attention_kernel, "attention", info,
            [*x_parts, row(b_query), row(b_value), row(b_output), row(attn_gain), row(attn_shift),
             w_query, w_key, w_value, w_output],
            (full, full, full, full, like((width // HD, rows, rows)), full, like((rows, width), F32),
             like((rows, 1), F32), full),
            13, 20, hbm=4, scratch=[square] * 4 + [pltpu.SemaphoreType.DMA((4,))],
        )
        x_other, ctx_other, low_other = pair(x), pair(ctx), pair(low1)
        act, slope = call(
            hidden_kernel, "hidden", info, [low1, w_inner, row(b_inner)],
            (like((rows, wide)), like((rows, wide))), 9, after=cot_parts,
        )
        act_other = pair(act)
        *out, mid, gb, gb_mine, gb_send, sums2 = call(
            branch_kernel, "branch", info,
            [act, w_outer, row(b_outer), n1, row(attn_gain), row(attn_shift), row(ffn_gain), row(ffn_shift),
             *cot_parts],
            (*blocks, like((rows, width), F32), full, like((rows, half)), like((rows, half)), like((3, width), F32)),
            4, 16,
        )
        gb_other = pair(gb_send)
        out = scatter(out)
        env, groups, token = {}, {}, []

        def buffers(part, columns, extra=0):
            return like((dp * part, columns)), like((dp * part + extra, columns))

        def product(a, b):
            return (tn(a[0], b[0]) + tn(a[1], b[1])).astype(BF16)

        def quarters(own):
            other = swap(own, "seq", size, 2)
            return [own, other, pair(own), pair(other)]

        def hidden_back(name, flip):
            shapes = (like((rows, wide // 2)), like((1, wide // 2), F32))
            env["gh_" + name], env["sumi_" + name] = call(
                hidden_back_kernel(flip), "hidden_back_" + name, info, [gb, w_outer, slope], shapes, 3,
                after=[*token, act_other] if flip else [*token, gb_other],
            )
            if flip:
                env["gh_pair"] = pair(env["gh_other"])
            return env["sumi_" + name]

        def grad_outer():
            keep, send = call(
                outer_kernel(bases["outer"], part_o), "grad_outer", info, [act, act_other, gb_mine, gb_other],
                buffers(part_o, half), 5, after=token, scratch=[pltpu.VMEM((wide, half), BF16)],
            )
            groups["o"] = Halving(info, keep, send, "outer", part_o)
            return send

        def grad_inner():
            keep, send = call(
                inner_kernel(bases["inner"], part_i), "grad_inner", info,
                [low1, low_other, env["gh_mine"], env["gh_pair"]], buffers(part_i, wide // 2), 4, after=token,
                scratch=[pltpu.VMEM((width, wide // 2), BF16)],
            )
            groups["i"] = Halving(info, keep, send, "inner", part_i)
            return send

        def first_back():
            env["gsum"], env["gctx"], env["ga"], ga_send, env["sums1"] = call(
                first_back_kernel, "first_back", info,
                [env["gh_mine"], env["gh_other"], w_inner, mid, n1, r1, row(attn_gain), w_output],
                (like((rows, width), F32), full, like((rows, half)), like((rows, half)), like((3, width), F32)),
                6, after=token,
            )
            env["ga_pair"] = pair(ga_send)
            return env["sums1"]

        def attention_back(name, flip):
            env["g3_" + name], env["sums0_" + name] = call(
                attention_back_kernel(flip), "attention_back_" + name, info, [q, k, v, p, env["gctx"]],
                (like((3, rows, half)), like((3, half), F32)), 1, after=token,
            )
            if flip:
                env["g3_pair"] = pair(env["g3_other"])
            return env["sums0_" + name]

        def grad_rest():
            sums = [env["sums0_mine"], env["sums0_other"], env["sums1"], sums2, env["sumi_mine"], env["sumi_other"]]
            keep, send, table = call(
                rest_kernel(bases["rest"], part_i), "grad_rest", info,
                [x, x_other, ctx, ctx_other, env["g3_mine"], env["g3_pair"], env["ga"], env["ga_pair"], *sums],
                (*buffers(4 * part_i, half, 2 * TABLE), like((TABLE, width), F32)), 1, after=token,
                scratch=[pltpu.VMEM((4, width, half), BF16)],
            )
            groups["r"] = Halving(info, keep, send, "rest", 4 * part_i, True)
            return table

        def input_back():
            parts = call(
                input_back_kernel, "input_back", info,
                [env["g3_mine"], env["g3_other"], env["gsum"], w_query, w_key, w_value], blocks, 2, after=token,
                hbm=3, mb=52, scratch=[square] * 3 + [pltpu.SemaphoreType.DMA((3,))],
            )
            env["back"] = scatter(parts)
            return parts[0]

        def step(name):
            own = groups[name].step(*token)
            if groups[name].stage == nbits:
                env["q" + name] = quarters(own)
            return own

        def finish_group(name, part, columns, title):
            env["g" + name] = call(
                finish_kernel(part, False), title, info, env["q" + name], like((2 * part, columns), F32), 1, after=token
            )
            return env["g" + name]

        def finish_rest():
            matrix, thin = like((2 * part_i, width), F32), like((TABLE, 128), F32)
            env["gr"] = call(
                finish_kernel(part_i, True), "finish_rest", info, env["qr"],
                (matrix, matrix, matrix, matrix, thin, like((1, 2 * part_o), F32)), 1, after=token,
            )
            return env["gr"][4]

        def collect(name, parts):
            env[name] = call(collect_kernel, "collect_" + name, info, parts, like(shape), 1, after=token)
            return env[name]

        tasks = {
            "ho": lambda: hidden_back("other", True),
            "hm": lambda: hidden_back("mine", False),
            "go": grad_outer,
            "gi": grad_inner,
            "fb": first_back,
            "ao": lambda: attention_back("other", True),
            "am": lambda: attention_back("mine", False),
            "gr": grad_rest,
            "ib": input_back,
            "o": lambda: step("o"),
            "i": lambda: step("i"),
            "r": lambda: step("r"),
            "fo": lambda: finish_group("o", part_o, width, "finish_outer"),
            "fi": lambda: finish_group("i", part_i, wide, "finish_inner"),
            "fr": finish_rest,
            "co": lambda: collect("outputs", out),
            "ci": lambda: collect("inputs", env["back"]),
        }
        for name in ORDER:
            if fast or name in ("ho", "hm", "fb", "ao", "am", "ib", "co", "ci"):
                token = [tasks[name]()]

        def finish(value, group, part, columns):
            value = jnp.stack(spread(value.reshape(group, part, columns // 2), 2), axis=1)
            value = value.reshape(group, 2 * part, columns // 2)
            return jnp.concatenate(spread(value, 1), axis=-1).astype(F32)

        if fast:
            g_outer, g_inner = env["go"], env["gi"]
            g_query, g_key, g_value, g_output, small, wide_row = env["gr"]
            small = [small[i, : 2 * part_i] for i in range(9)] + [wide_row[0]]
        else:
            me_core = (me, core)

            def cut(value, part):
                return value.reshape(chunks, part, value.shape[1])

            own_o = plain_halving(
                cut(product((act, act_other), (gb_mine, gb_other)), part_o), orders["outer"], *me_core
            )
            own_i = plain_halving(
                cut(product((low1, low_other), (env["gh_mine"], env["gh_pair"])), part_i), orders["inner"], *me_core
            )
            four = [product((x, x_other), (env["g3_mine"][i], env["g3_pair"][i])) for i in range(3)]
            four.append(product((ctx, ctx_other), (env["ga"], env["ga_pair"])))
            four = jnp.stack([cut(f, part_i) for f in four], axis=1)
            own_r = plain_halving(four, orders["rest"], *me_core)

            def both(mine, other):
                return jnp.where(
                    core == 0,
                    jnp.concatenate([mine, other], axis=1),
                    jnp.concatenate([other, mine], axis=1),
                )

            table = jnp.concatenate(
                [
                    both(env["sums0_mine"], env["sums0_other"]),
                    env["sums1"],
                    sums2,
                    both(env["sumi_mine"], env["sumi_other"]).reshape(-1, width),
                ]
            )
            table = lax.psum(table, ("dp", "seq"))
            (g_outer,) = finish(own_o, 1, part_o, width)
            (g_inner,) = finish(own_i, 1, part_i, wide)
            g_query, g_key, g_value, g_output = finish(own_r, 4, part_i, width)
            lines = [table[i] for i in range(9)] + [table[9:].reshape(-1)]
            small = []
            for line in lines:
                n = line.shape[0] // dp
                small.append(lax.dynamic_slice_in_dim(line, lax.axis_index("dp") * n, n))
        return (
            env["outputs"],
            env["inputs"],
            g_query,
            small[0],
            g_key,
            g_value,
            small[2],
            g_output,
            small[5],
            small[3],
            small[4],
            g_inner,
            small[9],
            g_outer,
            small[8],
            small[6],
            small[7],
        )

    return body


def solution(mesh):
    rows = P("dp", "seq", None)
    matrix, vector = P("dp", None), P("dp")
    in_specs = (rows, rows, P("dp", "seq"), *[P()] * 15)
    out_specs = (
        rows,
        rows,
        matrix,
        vector,
        matrix,
        matrix,
        vector,
        matrix,
        vector,
        vector,
        vector,
        matrix,
        vector,
        matrix,
        vector,
        vector,
        vector,
    )
    body = make_body(dict(mesh.shape))
    return jax.shard_map(
        body, mesh=mesh, in_specs=in_specs, out_specs=out_specs, check_vma=False
    )
```
